32 devices in a mesh: dp: 8 (over z, y), mp: 4 (over x, core).
Axes of the slice: x: 2, y: 2, z: 4, core: 2. Of those that a mesh axis runs over, the one named last changes fastest.
Arguments:
- tokens: bfloat16 [18432, 768], P(('dp', 'mp')), may hold values from -6 to 6
- norm_gain: float32 [2, 768], replicated, may hold values from 0.1 to 1.9
- norm_shift: float32 [2, 768], replicated, may hold values from -1.75 to 1.75
- qkv_weight: bfloat16 [3, 768, 768], P(None, None, 'mp'), may hold values from -0.21875 to 0.21875
- qkv_bias: float32 [2, 768], P(None, 'mp'), may hold values from -3 to 3
- proj_weight: bfloat16 [768, 768], P('mp'), may hold values from -1.75 to 1.75
- proj_bias: float32 [2, 768], replicated, may hold values from -1.75 to 1.75
- up_weight: bfloat16 [768, 3072], P(None, 'mp'), may hold values from -0.21875 to 0.21875
- up_bias: float32 [3072], P('mp'), may hold values from -3 to 3
- down_weight: bfloat16 [3072, 768], P('mp'), may hold values from -0.109375 to 0.109375
- patch_grids: int32 [64, 2], P('dp'), may hold values from 8 to 35, as said below
- keep_masks: int32 [64, 2], P('dp'), may hold values 0 or 1
- out_cotangent: bfloat16 [18432, 768], P(('dp', 'mp')), may hold values from -6 to 6
Outputs:
- block_out: bfloat16 [18432, 768], P(('dp', 'mp'))
- tokens_grad: float32 [18432, 768], P(('dp', 'mp'))
- norm_gain_grad: float32 [2, 768], replicated
- norm_shift_grad: float32 [2, 768], replicated
- qkv_weight_grad: float32 [3, 768, 768], P(None, None, 'mp')
- qkv_bias_grad: float32 [2, 768], P(None, 'mp')
- proj_weight_grad: float32 [768, 768], P('mp')
- proj_bias_grad: float32 [2, 768], replicated
- up_weight_grad: float32 [768, 3072], P(None, 'mp')
- up_bias_grad: float32 [3072], P('mp')
- down_weight_grad: float32 [3072, 768], P('mp')
The draws below stay inside these ranges and needn't reach their ends.
Inputs may be any that keep to these rules, and one draw needn't show every extreme that they name: `patch_grids`: row i is image i's grid of patch rows and columns; their product is at most 280, and some image in every draw has exactly 280 patches.
All inputs are finite; a program needn't handle non-finite values. No bound on the sum of `keep_masks` on one device may be relied on, other than what follows from the above.
Results may differ from the reference program's by a relative error of at most 0.012.
The reference program's roundings to bfloat16 on the way count: a program that leaves them out, or rounds other values in their place, can miss the bound.
Values may be sent and summed in bfloat16 or wider, within the bound.
A program may use at most 128 MiB of HBM per device.

```python
import jax
import jax.numpy as jnp
from jax import lax

D = 768
HEADS = 12
HEAD_DIM = 64
FF = 3072
SLOT = 288
IMG_DEV = 8
IMAGES = 64
TOKENS = 18432


def draw_patch_grids(key, part):
    key = jax.random.fold_in(key, 7)
    most = SLOT - 8
    low_side = max(2, most // 35)
    high_side = max(low_side + 1, most // 14)
    least = most * 24 // 35
    first_key, second_key, third_key = jax.random.split(key, 3)
    grid_rows = jax.random.randint(first_key, (IMAGES,), low_side, high_side + 1)
    lowest_cols = (least + grid_rows - 1) // grid_rows
    highest_cols = most // grid_rows
    spread_bits = jax.random.randint(second_key, (IMAGES,), 0, 1 << 20)
    grid_cols = lowest_cols + spread_bits % (highest_cols - lowest_cols + 1)
    chosen = jax.random.permutation(third_key, IMAGES)
    grid_rows = grid_rows.at[chosen[0]].set(high_side).at[chosen[1]].set(low_side)
    grid_cols = grid_cols.at[chosen[0]].set(most // high_side).at[chosen[1]].set(most // low_side)
    return jnp.stack([grid_rows, grid_cols], axis=1).astype(jnp.int32)


def with_ends(values, stream_key, low, top_value):
    index_at = [jax.random.randint(jax.random.fold_in(stream_key, axis), (), 0, length) for axis, length in enumerate(values.shape)]
    longest = values.shape.index(max(values.shape))
    neighbour = index_at[:longest] + [(index_at[longest] + 1) % values.shape[longest]] + index_at[longest + 1:]
    return values.at[tuple(index_at)].set(low).at[tuple(neighbour)].set(top_value)


def levels(stream_key, dims, cuts, low, largest):
    level = 1.0
    for dim, blocks in cuts:
        draws = jax.random.uniform(jax.random.fold_in(jax.random.fold_in(stream_key, 6), dim), (blocks,), jnp.float32, low / len(cuts), largest / len(cuts))
        level = level * jnp.repeat(jnp.exp(draws), dims[dim] // blocks).reshape((-1,) + (1,) * (len(dims) - 1 - dim))
    return level


def noise(rng, shape, scale, reach, shards=(), kind=jnp.bfloat16):
    values = jax.random.normal(rng, shape, jnp.float32) * scale
    if len(shards) > 0:
        values = levels(rng, shape, shards, -0.22, 0.18) * values
    return jnp.clip(values, min=-reach, max=reach).astype(kind)


def setup_inputs(seed: int = 0) -> dict:
    arg_keys = jax.random.split(jax.random.key(seed), 14)
    tokens = noise(arg_keys[0], (TOKENS, D), 1.0, 6.0, ((0, 32),))
    norm_gain = jnp.clip(1.0 + 0.18 * jax.random.normal(arg_keys[1], (2, D), jnp.float32), 0.1, 1.9)
    norm_shift = noise(arg_keys[2], (2, D), 0.3, 1.75, (), jnp.float32)
    qkv_weight = noise(arg_keys[3], (3, D, D), D ** -0.5, 0.21875, ((2, 4),))
    qkv_bias = noise(arg_keys[4], (2, D), 0.5, 3.0, ((1, 4),), jnp.float32)
    proj_weight = noise(arg_keys[5], (D, D), (D // 64) ** -0.5, 1.75, ((0, 4),))
    proj_bias = noise(arg_keys[6], (2, D), 0.3, 1.75, (), jnp.float32)
    up_weight = noise(arg_keys[7], (D, FF), D ** -0.5, 0.21875, ((1, 4),))
    up_bias = noise(arg_keys[8], (FF,), 0.5, 3.0, ((0, 4),), jnp.float32)
    down_weight = noise(arg_keys[9], (FF, D), FF ** -0.5, 0.109375, ((0, 4),))
    patch_grids = draw_patch_grids(jax.random.fold_in(arg_keys[13], 71), 0)
    keep_masks = with_ends((jax.random.randint(arg_keys[11], (IMAGES, 2), 0, 10) < 9).astype(jnp.int32), jax.random.fold_in(arg_keys[11], 1), 0, 1)
    out_cotangent = noise(arg_keys[12], (TOKENS, D), 1.0, 6.0, ((0, 32),))
    return dict(tokens=tokens, norm_gain=norm_gain, norm_shift=norm_shift, qkv_weight=qkv_weight, qkv_bias=qkv_bias, proj_weight=proj_weight, proj_bias=proj_bias, up_weight=up_weight, up_bias=up_bias, down_weight=down_weight, patch_grids=patch_grids, keep_masks=keep_masks, out_cotangent=out_cotangent)


EPSILON = 1e-06
KEEP_RATE = 0.9
HIGHEST = lax.Precision.HIGHEST

@jax.custom_vjp
def low(v):
    return lax.optimization_barrier(v.astype(jnp.bfloat16)).astype(jnp.float32)

@jax.custom_vjp
def low_back(v):
    return v

def low_keep(v):
    return (low(v), None)

def low_pass(kept, grad):
    return (grad,)

def back_keep(v):
    return (v, None)

def back_low(kept, grad):
    return (low(grad),)
low.defvjp(low_keep, low_pass)
low_back.defvjp(back_keep, back_low)

def rounded_both(value):
    return low(low_back(value))

def product(left, right):
    return jnp.dot(left, right, precision=HIGHEST, preferred_element_type=jnp.float32)

def layer_norm(stream, gain, shift):
    centred = stream - lax.optimization_barrier(jnp.mean(stream, axis=-1, keepdims=True))
    spread = lax.optimization_barrier(jnp.mean(centred * centred, axis=-1, keepdims=True))
    return centred * lax.rsqrt(spread + EPSILON) * gain + shift

def attend(block):
    queries, key_rows, value_rows, key_ok = block
    scores = jnp.einsum('bqhd,bkhd->bhqk', queries, key_rows, precision=HIGHEST, preferred_element_type=jnp.float32) * HEAD_DIM ** (-0.5)
    scores = low_back(scores)
    scores = jnp.where(key_ok[:, None, None, :], scores, -1000000000.0)
    top_score = lax.optimization_barrier(jnp.max(scores, axis=-1, keepdims=True))
    raised = jnp.exp(scores - top_score)
    weights = low(raised / lax.optimization_barrier(jnp.sum(raised, axis=-1, keepdims=True)))
    return jnp.einsum('bhqk,bkhd->bqhd', weights, value_rows, precision=HIGHEST, preferred_element_type=jnp.float32)

def reference(tokens, norm_gain, norm_shift, qkv_weight, qkv_bias, proj_weight, proj_bias, up_weight, up_bias, down_weight, patch_grids, keep_masks, out_cotangent):
    lengths = patch_grids[:, 0] * patch_grids[:, 1] + 2
    position = jnp.arange(SLOT, dtype=jnp.int32)
    key_ok = position[None, :] < lengths[:, None]
    valid_rows = key_ok.astype(jnp.float32).reshape(TOKENS, 1)
    keep_float = keep_masks.astype(jnp.float32)
    attn_rate = valid_rows * jnp.repeat(keep_float[:, 0], SLOT)[:, None] / KEEP_RATE
    mlp_rate = valid_rows * jnp.repeat(keep_float[:, 1], SLOT)[:, None] / KEEP_RATE
    block_ok = key_ok.reshape(IMAGES // IMG_DEV, IMG_DEV, SLOT)
    block_shape = (IMAGES // IMG_DEV, IMG_DEV, SLOT, HEADS, HEAD_DIM)

    def forward(stream, gain_rows, shift_rows, qkv_matrix, qkv_offset, proj_matrix, proj_offset, up_matrix, up_offset, down_matrix):
        normed = low(layer_norm(stream, gain_rows[0], shift_rows[0]))
        queries = rounded_both(product(normed, qkv_matrix[0]) + qkv_offset[0])
        key_rows = rounded_both(product(normed, qkv_matrix[1]))
        value_rows = rounded_both(product(normed, qkv_matrix[2]) + qkv_offset[1])
        mixed_rows = lax.map(jax.checkpoint(attend), (queries.reshape(block_shape), key_rows.reshape(block_shape), value_rows.reshape(block_shape), block_ok))
        mixed_rows = rounded_both(mixed_rows.reshape(TOKENS, D))
        attended = low_back(product(mixed_rows, proj_matrix))
        middle = stream + attn_rate * (attended + proj_offset[0])
        normed_two = low(layer_norm(middle, gain_rows[1], shift_rows[1]))
        hidden = low_back(product(normed_two, up_matrix) + up_offset)
        activated = low(jax.nn.gelu(hidden, approximate=False))
        returned = low_back(product(activated, down_matrix))
        return middle + mlp_rate * (returned + proj_offset[1])
    inputs_float = tuple((item.astype(jnp.float32) for item in (tokens, norm_gain, norm_shift, qkv_weight, qkv_bias, proj_weight, proj_bias, up_weight, up_bias, down_weight)))
    result, pullback = jax.vjp(forward, *inputs_float)
    gradients = pullback(out_cotangent.astype(jnp.float32))
    return (result.astype(jnp.bfloat16), gradients[0], gradients[1], gradients[2], gradients[3], gradients[4], gradients[5], gradients[6], gradients[7], gradients[8], gradients[9])
```

```python
import functools

import jax
import jax.numpy as jnp
from jax import lax
from jax.experimental import pallas as pl
from jax.experimental.pallas import tpu as pltpu
from jax.sharding import PartitionSpec as P

HEAD_DIM = 64
EPSILON = 1e-06
KEEP_RATE = 0.9
MESH = pl.DeviceIdType.MESH
BF = jnp.bfloat16
F32 = jnp.float32
TILE = 96
JOBS = 3
SUBS = 4


def dot(left, right, left_dim, right_dim):
    return lax.dot_general(
        left, right, (((left_dim,), (right_dim,)), ((), ())), preferred_element_type=F32
    )


def normalise(rows):
    centred = rows - jnp.mean(rows, axis=-1, keepdims=True)
    spread = jnp.mean(centred * centred, axis=-1, keepdims=True)
    scale = lax.rsqrt(spread + EPSILON)
    return centred * scale, scale


def column_sum(rows):
    return jnp.sum(rows, axis=0, keepdims=True)


def layer_kernel(
    sizes,
    tok,
    cot,
    gain,
    shift,
    pbias,
    grids,
    masks,
    bias_in,
    wqkv_in,
    wproj_in,
    wup_in,
    wdn_in,
    grads_out,
    tokens_grad,
    block_out,
    small_out,
    wqkv,
    wproj,
    wup,
    wdn,
    bias_all,
    entry,
    entry_two,
    ret_grad,
    heads,
    mixed,
    mixed_grad,
    mixer_grad,
    act,
    slope,
    work,
    middle,
    give,
    sum_core,
    got_x,
    got_y,
    got_z,
    small,
    small_got,
    local_sem,
    ag_send,
    ag_recv,
    bias_send,
    bias_recv,
    core_send,
    core_recv,
    x_send,
    x_recv,
    y_send,
    y_recv,
    z_send,
    z_recv,
    zag_send,
    zag_recv,
    yag_send,
    yag_recv,
    own_sem,
    small_send,
    small_recv,
):
    nz, images, slot, width, cols = sizes
    rows = images * slot
    pair = 2 * cols
    half = cols // 2
    packs = pair // 128
    per_unit = nz // 4
    units = JOBS * SUBS // per_unit

    d = lax.axis_index("dp")
    m = lax.axis_index("mp")
    y = lax.rem(d, 2)
    z = d // 2
    x = m // 2
    c = lax.rem(m, 2)
    core_dev = (d, x * 2 + 1 - c)
    x_dev = (d, (1 - x) * 2 + c)
    diag_dev = (d, (1 - x) * 2 + 1 - c)
    y_dev = (z * 2 + 1 - y, m)

    def z_dev(other):
        return (other * 2 + y, m)

    def remote(src, dst, send, recv, device):
        return pltpu.make_async_remote_copy(
            src_ref=src,
            dst_ref=dst,
            send_sem=send,
            recv_sem=recv,
            device_id=device,
            device_id_type=MESH,
        )

    barrier = pltpu.get_barrier_semaphore()
    greeted = [core_dev, x_dev, diag_dev, y_dev]
    greeted += [z_dev(lax.rem(z + k, nz)) for k in range(1, nz)]
    for device in greeted:
        pl.semaphore_signal(barrier, inc=1, device_id=device, device_id_type=MESH)
    pl.semaphore_wait(barrier, len(greeted))

    own_block = m
    peer_block = x * 2 + 1 - c
    far_block = (1 - x) * 2 + c
    far_peer = (1 - x) * 2 + 1 - c
    own_x = (x * 2, x * 2 + 1)

    pieces = [("q", 0), ("k", 0), ("v", 0), ("p", 0), ("u", 0), ("u", 1), ("d", 0), ("d", 1)]
    index_of = {piece: i for i, piece in enumerate(pieces)}
    big = width // 4

    def view(piece, block, part):
        kind, number = piece
        if kind in "qkvp":
            start, size = (0, cols) if part is None else (part * half, half)
            start = pl.multiple_of(block * cols + start, 16)
            if kind == "p":
                return wproj.at[pl.ds(start, size), :]
            return wqkv.at["qkv".index(kind), pl.ds(start, size), :]
        start, size = (0, 2 * big) if part is None else (part * big, big)
        start = pl.multiple_of(number * 2 * big + start, 16)
        return (wup if kind == "u" else wdn).at[block, pl.ds(start, size), :]

    def view_in(piece, part):
        kind, number = piece
        if kind in "qkvp":
            start, size = (0, cols) if part is None else (part * half, half)
            if part is not None:
                start = pl.multiple_of(start, 16)
            if kind == "p":
                return wproj_in.at[pl.ds(start, size), :]
            return wqkv_in.at["qkv".index(kind), pl.ds(start, size), :]
        start, size = (0, 2 * big) if part is None else (part * big, big)
        start = pl.multiple_of(number * 2 * big + start, 16)
        return (wup_in if kind == "u" else wdn_in).at[pl.ds(start, size), :]

    def ag_local(p):
        i = index_of[p]
        return pltpu.make_async_copy(view_in(p, None), view(p, own_block, None), local_sem.at[i])

    def ag_copy(route, p):
        i = index_of[p]
        send, recv = ag_send.at[route, i], ag_recv.at[route, i]
        if route == 0:
            return remote(view_in(p, None), view(p, own_block, None), send, recv, core_dev)
        if route == 1:
            return remote(view_in(p, y), view(p, own_block, y), send, recv, x_dev)
        part = 1 - y if route == 4 else y
        source = view(p, far_block, part)
        return remote(source, source, send, recv, y_dev if route == 2 else core_dev)

    bias_out = [
        remote(bias_in, bias_all.at[m], bias_send.at[i], bias_recv.at[i], device)
        for i, device in enumerate((core_dev, x_dev, diag_dev))
    ]
    bias_own = pltpu.make_async_copy(bias_in, bias_all.at[m], local_sem.at[len(pieces)])
    for copy in bias_out:
        copy.start()
    bias_own.start()
    for p in pieces:
        ag_copy(1, p).start()
        ag_copy(0, p).start()
        ag_local(p).start()

    def near_ready(*names):
        for p in names:
            ag_local(p).wait()
            ag_copy(0, p).wait_recv()

    def from_x(*names):
        for p in names:
            ag_copy(1, p).wait_recv()
            ag_copy(2, p).start()
            ag_copy(3, p).start()

    def from_y(*names):
        for p in names:
            ag_copy(2, p).wait_recv()
            ag_copy(4, p).start()

    def far_ready(*names):
        for p in names:
            ag_copy(3, p).wait_recv()
            ag_copy(4, p).wait_recv()

    def sub_rows(sub):
        return sub // SUBS, pl.ds((sub % SUBS) * cols, cols)

    def core_copy(job, xb, slot_, sub):
        if sub is None:
            src, dst = give.at[job, xb], sum_core.at[job, xb]
        else:
            part = pl.ds((sub % SUBS) * cols, cols)
            src, dst = give.at[job, xb, part, :], sum_core.at[job, xb, part, :]
        return remote(src, dst, core_send.at[slot_], core_recv.at[slot_], core_dev)

    def x_copy(sub):
        job, part = sub_rows(sub)
        return remote(
            sum_core.at[job, 1 - x, part, :], got_x.at[sub], x_send.at[sub], x_recv.at[sub], x_dev
        )

    def y_part(sub, which):
        job, _ = sub_rows(sub)
        start = pl.multiple_of((sub % SUBS) * cols + which * half, 16)
        return job, pl.ds(start, half)

    def y_copy(sub):
        job, part = y_part(sub, 1 - y)
        return remote(
            sum_core.at[job, x, part, :], got_y.at[sub], y_send.at[sub], y_recv.at[sub], y_dev
        )

    tall, wide = half // 2, width // 2

    def z_part(owner):
        part = lax.rem(owner, 4)
        row = pl.multiple_of((part // 2) * tall, 16)
        col = pl.multiple_of(lax.rem(part, 2) * wide, 128)
        return owner // 4, row, col

    def z_copy(unit, step):
        owner = lax.rem(z + step, nz)
        inner, row, col = z_part(owner)
        src = got_y.at[unit * per_unit + inner, pl.ds(row, tall), pl.ds(col, wide)]
        sem = unit * (nz - 1) + step - 1
        return remote(
            src, got_z.at[unit, step - 1], z_send.at[sem], z_recv.at[sem], z_dev(owner)
        )

    def final_part(unit):
        inner, row, col = z_part(z)
        row = pl.multiple_of(y * half + row, 16)
        return grads_out.at[unit * per_unit + inner, pl.ds(row, tall), pl.ds(col, wide)]

    def zag_copy(unit, step):
        sem = unit * (nz - 1) + step - 1
        return remote(
            got_z.at[unit, nz - 1],
            final_part(unit),
            zag_send.at[sem],
            zag_recv.at[sem],
            z_dev(lax.rem(z + step, nz)),
        )

    def own_copy(unit):
        return pltpu.make_async_copy(got_z.at[unit, nz - 1], final_part(unit), own_sem.at[unit])

    def yag_copy(unit):
        part = grads_out.at[
            pl.ds(unit * per_unit, per_unit), pl.ds(pl.multiple_of(y * half, 16), half), :
        ]
        return remote(part, part, yag_send.at[unit], yag_recv.at[unit], y_dev)

    def x_stage(sub):
        x_copy(sub).wait_recv()
        job, part = sub_rows(sub)
        total = sum_core[job, x, part, :].astype(F32) + got_x[sub].astype(F32)
        sum_core[job, x, part, :] = total.astype(BF)
        y_copy(sub).start()

    def y_stage(sub):
        y_copy(sub).wait_recv()
        job, part = y_part(sub, y)
        total = sum_core[job, x, part, :].astype(F32) + got_y[sub].astype(F32)
        got_y[sub] = total.astype(BF)
        if sub % per_unit == per_unit - 1:
            for step in range(1, nz):
                z_copy(sub // per_unit, step).start()

    def z_stage(sub):
        if sub % per_unit != per_unit - 1:
            return
        unit = sub // per_unit
        inner, row, col = z_part(z)
        total = got_y[unit * per_unit + inner, pl.ds(row, tall), pl.ds(col, wide)].astype(F32)
        for step in range(1, nz):
            z_copy(unit, step).wait_recv()
            total = total + got_z[unit, step - 1].astype(F32)
        got_z[unit, nz - 1] = total.astype(BF)
        own_copy(unit).start()
        for step in range(1, nz):
            zag_copy(unit, step).start()

    def zag_stage(sub):
        if sub % per_unit != per_unit - 1:
            return
        unit = sub // per_unit
        own_copy(unit).wait()
        for step in range(1, nz):
            zag_copy(unit, step).wait_recv()
        yag_copy(unit).start()

    stages = (x_stage, y_stage, z_stage, zag_stage)
    ticks = [0]

    def tick():
        now = ticks[0]
        ticks[0] += 1
        for lag, stage in enumerate(stages):
            if 0 <= now - lag < JOBS * SUBS:
                stage(now - lag)

    def live_rate(which, image, row):
        index = m * images + image
        length = grids[index, 0] * grids[index, 1] + 2
        keep = masks[index, which].astype(F32) / KEEP_RATE
        position = lax.broadcasted_iota(jnp.int32, (TILE, 1), 0) + row
        return jnp.where(position < length, keep, 0.0)

    def over_rows(body):
        for image in range(images):

            def step(i, carry):
                row = i * TILE
                body(image, row, pl.ds(pl.multiple_of(image * slot + row, 16), TILE))
                return carry

            lax.fori_loop(0, slot // TILE, step, 0)

    small[...] = jnp.zeros_like(small)

    def first_norm(image, row, at):
        normed, _ = normalise(tok[at, :].astype(F32))
        entry[at, :] = (normed * gain[0:1, :] + shift[0:1, :]).astype(BF)
        grad = live_rate(1, image, row) * cot[at, :].astype(F32)
        ret_grad[at, :] = grad.astype(BF)
        small[7:8, :] += column_sum(grad)

    over_rows(first_norm)

    lane = lax.broadcasted_iota(jnp.int32, (slot, 128), 1)
    low_lanes = lane < HEAD_DIM
    position = lax.broadcasted_iota(jnp.int32, (slot, slot), 1)
    score_scale = HEAD_DIM ** (-0.5)

    def pick(head, values):
        mask = low_lanes if head == 0 else jnp.logical_not(low_lanes)
        return jnp.where(mask, values, jnp.zeros_like(values))

    def key_length(image):
        index = m * images + image
        return grids[index, 0] * grids[index, 1] + 2

    def softmax(queries, keys, length):
        scores = dot(queries, keys, 1, 1) * score_scale
        scores = jnp.where(position < length, scores, -1000000000.0)
        raised = jnp.exp(scores - jnp.max(scores, axis=-1, keepdims=True))
        return raised * (1.0 / jnp.sum(raised, axis=-1, keepdims=True))

    def project(xb):
        at = pl.ds(pl.multiple_of(xb * pair, 16), pair)
        for j in range(3):
            value = dot(entry[...], wqkv[j, at, :], 1, 1)
            if j != 1:
                row = 1 if j == 0 else 2
                value = value + (
                    bias_all[xb * 2, row : row + 1, 0:pair]
                    + bias_all[xb * 2 + 1, row : row + 1, 0:pair]
                )
            value = value.astype(BF)
            for pack in range(packs):
                heads[j, xb * packs + pack] = value[:, pack * 128 : (pack + 1) * 128]

    def attend(xb):
        def step(i, carry):
            image = i // packs
            pack = xb * packs + lax.rem(i, packs)
            at = pl.ds(pl.multiple_of(image * slot, 16), slot)
            queries, keys, values = (heads[j, pack, at, :] for j in range(3))
            length = key_length(image)
            total = jnp.zeros((slot, 128), F32)
            for head in range(2):
                probs = softmax(queries, pick(head, keys), length).astype(BF)
                total = total + dot(probs, pick(head, values), 1, 0)
            mixed[pack, at, :] = total.astype(BF)
            return carry

        lax.fori_loop(0, images * packs, step, 0)

    for copy in bias_out:
        copy.wait_recv()
    bias_own.wait()
    near_ready(("q", 0), ("k", 0), ("v", 0))
    project(x)
    from_x(("q", 0), ("k", 0), ("v", 0))
    attend(x)
    from_x(("p", 0))
    from_y(("q", 0), ("k", 0), ("v", 0))
    far_ready(("q", 0), ("k", 0), ("v", 0))
    project(1 - x)
    from_x(("u", 0))
    from_y(("p", 0))
    attend(1 - x)

    near_ready(("p", 0))
    far_ready(("p", 0))
    all_mixed = jnp.concatenate([mixed[pack] for pack in range(2 * packs)], axis=1)
    work[...] = dot(all_mixed, wproj[...], 1, 0)

    def second_norm(image, row, at):
        value = tok[at, :].astype(F32) + live_rate(0, image, row) * (work[at, :] + pbias[0:1, :])
        middle[at, :] = value
        normed, _ = normalise(value)
        entry_two[at, :] = (normed * gain[1:2, :] + shift[1:2, :]).astype(BF)

    over_rows(second_norm)
    from_x(("u", 1))
    from_y(("u", 0), ("u", 1))

    def emit_wide(job, xb, mine, value):
        slot_ = job * 2 + (0 if mine[1] else 1)
        if not mine[0]:
            give[job, xb] = value.astype(BF)
            core_copy(job, xb, slot_, None).start()
        else:
            core_copy(job, xb, slot_, None).wait_recv()
            sum_core[job, xb] = (value + sum_core[job, xb].astype(F32)).astype(BF)
            if mine[1]:
                for s in range(SUBS):
                    x_copy(job * SUBS + s).start()

    def gelu_loop(block):
        def step(i, carry):
            at = pl.ds(pl.multiple_of(i * TILE, 16), TILE)
            hidden = work[at, :] + bias_all[block, 0:1, :]
            share = 0.5 * (1.0 + lax.erf(hidden * 0.7071067811865476))
            density = jnp.exp(-0.5 * hidden * hidden) * 0.3989422804014327
            act[block, at, :] = (hidden * share).astype(BF)
            slope[block, at, :] = (share + hidden * density).astype(BF)
            return carry

        lax.fori_loop(0, rows // TILE, step, 0)

    def feed_first(block, xb, mine):
        work[...] = dot(entry_two[...], wup[block], 1, 0)
        gelu_loop(block)
        emit_wide(0, xb, mine, dot(act[block], ret_grad[...], 0, 0))

    def feed_back(block, xb, mine, first):
        work[...] = dot(ret_grad[...], wdn[block], 1, 1)

        def step(i, carry):
            at = pl.ds(pl.multiple_of(i * TILE, 16), TILE)
            grad = (work[at, :] * slope[block, at, :].astype(F32)).astype(BF)
            slope[block, at, :] = grad
            small[pl.ds(8 + block, 1), :] += column_sum(grad.astype(F32))
            return carry

        lax.fori_loop(0, rows // TILE, step, 0)
        emit_wide(1, xb, mine, dot(entry_two[...], slope[block], 0, 0))
        value = dot(slope[block], wup[block], 1, 1)
        if first:
            tokens_grad[...] = value
        else:
            tokens_grad[...] += value

    order = (
        (far_peer, 1 - x, (False, True)),
        (far_block, 1 - x, (True, True)),
        (peer_block, x, (False, False)),
        (own_block, x, (True, False)),
    )
    near_ready(("u", 0), ("u", 1))
    far_ready(("u", 0), ("u", 1))
    feed_first(*order[0])
    from_x(("d", 0))
    feed_first(*order[1])
    from_x(("d", 1))
    from_y(("d", 0))
    feed_first(*order[2])
    from_y(("d", 1))
    feed_first(*order[3])
    near_ready(("d", 0), ("d", 1))
    far_ready(("d", 0), ("d", 1))
    feed_back(*order[0], True)
    feed_back(*order[1], False)
    tick()
    feed_back(*order[2], False)
    tick()
    feed_back(*order[3], False)
    tick()

    def norm_back(values, grad, r):
        normed, scale = normalise(values)
        small[r : r + 1, :] += column_sum(grad * normed)
        small[2 + r : 3 + r, :] += column_sum(grad)
        scaled = grad * gain[r : r + 1, :]
        mean_one = jnp.mean(scaled, axis=-1, keepdims=True)
        mean_two = jnp.mean(scaled * normed, axis=-1, keepdims=True)
        return scale * (scaled - mean_one - normed * mean_two)

    def second_back(image, row, at):
        grad = cot[at, :].astype(F32) + norm_back(middle[at, :], tokens_grad[at, :], 1)
        tokens_grad[at, :] = grad
        scaled = live_rate(0, image, row) * grad
        mixer_grad[at, :] = scaled.astype(BF)
        small[6:7, :] += column_sum(scaled)

    over_rows(second_back)

    def emit_narrow(s, xb, far, value):
        sub = 2 * SUBS + s
        slot_ = 4 + s * 2 + (0 if far else 1)
        part = pl.ds(s * cols, cols)
        work[0:pair, :] = value
        theirs = pl.multiple_of((1 - c) * cols, 16)
        ours = pl.multiple_of(c * cols, 16)
        give[2, xb, part, :] = work[pl.ds(theirs, cols), :].astype(BF)
        core_copy(2, xb, slot_, sub).start()
        core_copy(2, xb, slot_, sub).wait_recv()
        total = work[pl.ds(ours, cols), :] + sum_core[2, xb, part, :].astype(F32)
        sum_core[2, xb, part, :] = total.astype(BF)
        if far:
            x_copy(sub).start()

    def side(ref, xb):
        return jnp.concatenate([ref[xb * packs + pack] for pack in range(packs)], axis=1)

    def attend_back(xb):
        def step(i, carry):
            image = i // packs
            pack = xb * packs + lax.rem(i, packs)
            at = pl.ds(pl.multiple_of(image * slot, 16), slot)
            queries, keys, values = (heads[j, pack, at, :] for j in range(3))
            grads = mixed_grad[pack, at, :]
            length = key_length(image)
            query_grad = jnp.zeros((slot, 128), F32)
            key_grad = jnp.zeros((slot, 128), F32)
            value_grad = jnp.zeros((slot, 128), F32)
            for head in range(2):
                head_keys = pick(head, keys)
                probs = softmax(queries, head_keys, length)
                probs_grad = dot(grads, pick(head, values), 1, 1)
                inner = jnp.sum(probs * probs_grad, axis=-1, keepdims=True)
                score_grad = (probs * (probs_grad - inner)).astype(BF)
                query_grad = query_grad + dot(score_grad, head_keys, 1, 0)
                key_grad = key_grad + dot(score_grad, pick(head, queries), 0, 0)
                value_grad = value_grad + dot(probs.astype(BF), pick(head, grads), 0, 0)
            heads[0, pack, at, :] = (query_grad * score_scale).astype(BF)
            heads[1, pack, at, :] = (key_grad * score_scale).astype(BF)
            heads[2, pack, at, :] = value_grad.astype(BF)
            return carry

        lax.fori_loop(0, images * packs, step, 0)

    def qkv_back(xb, far):
        lanes = pl.ds(pl.multiple_of(xb * pair, 128), pair)
        for j in range(3):
            grad = side(heads.at[j], xb)
            emit_narrow(1 + j, xb, far, dot(grad, entry[...], 0, 0))
            if j != 1:
                row = 4 if j == 0 else 5
                small[row : row + 1, lanes] = column_sum(grad.astype(F32))

    value = dot(mixer_grad[...], wproj[...], 1, 1).astype(BF)
    for pack in range(2 * packs):
        mixed_grad[pack] = value[:, pack * 128 : (pack + 1) * 128]
    for xb, far in ((1 - x, True), (x, False)):
        emit_narrow(0, xb, far, dot(side(mixed, xb), mixer_grad[...], 0, 0))
    tick()
    attend_back(1 - x)
    tick()
    qkv_back(1 - x, True)
    tick()
    attend_back(x)
    tick()
    qkv_back(x, False)

    value = None
    for j in range(3):
        grad = jnp.concatenate([heads[j, pack] for pack in range(2 * packs)], axis=1)
        part = dot(grad, wqkv[j], 1, 0)
        work[...] = part if j == 0 else work[...] + part

    def first_back(image, row, at):
        tokens_grad[at, :] += norm_back(tok[at, :].astype(F32), work[at, :], 0)

    over_rows(first_back)
    tick()

    def small_copy(stage, device):
        return remote(
            small.at[stage] if False else small_got.at[0, stage],
            small_got.at[1, stage],
            small_send.at[stage],
            small_recv.at[stage],
            device,
        )

    small_got[0, 0] = small[...]
    small_copy(0, core_dev).start()
    for i, (block, _, _) in enumerate(order):
        part = dot(act[block], wdn[block], 1, 0)
        work[...] = part if i == 0 else work[...] + part
        if i == 1:
            small_copy(0, core_dev).wait_recv()
            small_got[0, 1] = small_got[0, 0] + small_got[1, 0]
            small_copy(1, x_dev).start()

    def finish(image, row, at):
        value = middle[at, :] + live_rate(1, image, row) * (work[at, :] + pbias[1:2, :])
        block_out[at, :] = value.astype(BF)

    over_rows(finish)
    small_copy(1, x_dev).wait_recv()
    small_got[0, 2] = small_got[0, 1] + small_got[1, 1]
    small_copy(2, y_dev).start()
    tick()
    small_copy(2, y_dev).wait_recv()
    mine = 3 + z
    small_got[0, mine] = small_got[0, 2] + small_got[1, 2]

    def small_z(step):
        sem = 2 + step
        return remote(
            small_got.at[0, mine],
            small_got.at[0, mine],
            small_send.at[sem],
            small_recv.at[sem],
            z_dev(lax.rem(z + step, nz)),
        )

    for step in range(1, nz):
        small_z(step).start()
    while ticks[0] < JOBS * SUBS + len(stages) - 1:
        tick()
    for step in range(1, nz):
        small_z(step).wait_recv()
    total = small_got[0, 3]
    for other in range(1, nz):
        total = total + small_got[0, 3 + other]
    small_out[...] = total

    for unit in range(units):
        yag_copy(unit).wait_recv()
    for copy in bias_out:
        copy.wait_send()
    for p in pieces:
        for route in range(5):
            ag_copy(route, p).wait_send()
    for job in range(2):
        core_copy(job, 1 - x, job * 2, None).wait_send()
        core_copy(job, x, job * 2 + 1, None).wait_send()
    for s in range(SUBS):
        for k, xb in enumerate((1 - x, x)):
            core_copy(2, xb, 4 + s * 2 + k, 2 * SUBS + s).wait_send()
    for sub in range(JOBS * SUBS):
        x_copy(sub).wait_send()
        y_copy(sub).wait_send()
    for unit in range(units):
        for step in range(1, nz):
            z_copy(unit, step).wait_send()
            zag_copy(unit, step).wait_send()
        yag_copy(unit).wait_send()
    small_copy(0, core_dev).wait_send()
    small_copy(1, x_dev).wait_send()
    small_copy(2, y_dev).wait_send()
    for step in range(1, nz):
        small_z(step).wait_send()


def local(
    tokens,
    norm_gain,
    norm_shift,
    qkv_weight,
    qkv_bias,
    proj_weight,
    proj_bias,
    up_weight,
    up_bias,
    down_weight,
    patch_grids,
    keep_masks,
    out_cotangent,
):
    rows, width = tokens.shape
    mp = lax.axis_size("mp")
    nz = lax.axis_size("dp") // 2
    images = patch_grids.shape[0] // mp
    slot = rows // images
    cols = qkv_weight.shape[2]
    pair = 2 * cols
    packs = pair // 128
    units = JOBS * SUBS // (nz // 4)
    m = lax.axis_index("mp")
    offset = lax.rem(m, 2) * cols
    qkv_rows = jnp.transpose(qkv_weight, (0, 2, 1))
    bias_rows = lax.dynamic_update_slice(
        jnp.zeros((8, width), F32), qkv_bias, (jnp.int32(1), offset)
    )
    bias_rows = lax.dynamic_update_slice(bias_rows, up_bias[None, :], (0, 0))
    vmem = pl.BlockSpec(memory_space=pltpu.VMEM)
    smem = pl.BlockSpec(memory_space=pltpu.SMEM)
    hbm = pl.BlockSpec(memory_space=pl.ANY)
    dma = pltpu.SemaphoreType.DMA
    scratch = [
        pltpu.VMEM((3, width, width), BF),
        pltpu.VMEM((width, width), BF),
        pltpu.VMEM((4, width, width), BF),
        pltpu.VMEM((4, width, width), BF),
        pltpu.VMEM((4, 8, width), F32),
        pltpu.VMEM((rows, width), BF),
        pltpu.VMEM((rows, width), BF),
        pltpu.VMEM((rows, width), BF),
        pltpu.VMEM((3, 2 * packs, rows, 128), BF),
        pltpu.VMEM((2 * packs, rows, 128), BF),
        pltpu.VMEM((2 * packs, rows, 128), BF),
        pltpu.VMEM((rows, width), BF),
        pltpu.VMEM((4, rows, width), BF),
        pltpu.VMEM((4, rows, width), BF),
        pltpu.VMEM((rows, width), F32),
        pltpu.VMEM((rows, width), F32),
        pltpu.VMEM((JOBS, 2, width, width), BF),
        pltpu.VMEM((JOBS, 2, width, width), BF),
        pltpu.VMEM((JOBS * SUBS, cols, width), BF),
        pltpu.VMEM((JOBS * SUBS, cols // 2, width), BF),
        pltpu.VMEM((units, nz, cols // 4, width // 2), BF),
        pltpu.VMEM((16, width), F32),
        pltpu.VMEM((2, 3 + nz, 16, width), F32),
        dma((9,)),
        dma((5, 8)),
        dma((5, 8)),
        dma((3,)),
        dma((3,)),
        dma((12,)),
        dma((12,)),
        dma((JOBS * SUBS,)),
        dma((JOBS * SUBS,)),
        dma((JOBS * SUBS,)),
        dma((JOBS * SUBS,)),
        dma((units * (nz - 1),)),
        dma((units * (nz - 1),)),
        dma((units * (nz - 1),)),
        dma((units * (nz - 1),)),
        dma((units,)),
        dma((units,)),
        dma((units,)),
        dma((2 + nz,)),
        dma((2 + nz,)),
    ]
    grads, tokens_grad, block_out, small = pl.pallas_call(
        functools.partial(layer_kernel, (nz, images, slot, width, cols)),
        out_shape=(
            jax.ShapeDtypeStruct((JOBS * SUBS, cols, width), BF),
            jax.ShapeDtypeStruct((rows, width), F32),
            jax.ShapeDtypeStruct((rows, width), BF),
            jax.ShapeDtypeStruct((16, width), F32),
        ),
        in_specs=[vmem] * 5 + [smem] * 2 + [hbm] * 5,
        out_specs=(hbm, vmem, vmem, vmem),
        scratch_shapes=scratch,
        compiler_params=pltpu.CompilerParams(
            collective_id=0, has_side_effects=True, vmem_limit_bytes=64 * 2**20 - 2**17
        ),
    )(
        tokens,
        out_cotangent,
        norm_gain,
        norm_shift,
        proj_bias,
        patch_grids,
        keep_masks,
        bias_rows,
        qkv_rows,
        proj_weight,
        up_weight,
        down_weight,
    )
    grads = grads.astype(F32)
    down_grad = grads[0:SUBS].reshape(down_weight.shape)
    up_grad = grads[SUBS : 2 * SUBS].reshape(up_weight.shape)
    proj_grad = grads[2 * SUBS]
    qkv_grad = jnp.transpose(grads[2 * SUBS + 1 :], (0, 2, 1))
    qkv_bias_grad = lax.dynamic_slice(small, (jnp.int32(4), m * cols), (2, cols))
    up_bias_grad = lax.dynamic_slice(small, (8 + m, jnp.int32(0)), (1, width))[0]
    return (
        block_out,
        tokens_grad,
        small[0:2],
        small[2:4],
        qkv_grad,
        qkv_bias_grad,
        proj_grad,
        small[6:8],
        up_grad,
        up_bias_grad,
        down_grad,
    )


def solution(mesh):
    return jax.shard_map(
        local,
        mesh=mesh,
        in_specs=(
            P(("dp", "mp"), None),
            P(),
            P(),
            P(None, None, "mp"),
            P(None, "mp"),
            P("mp", None),
            P(),
            P(None, "mp"),
            P("mp"),
            P("mp", None),
            P("dp", None),
            P("dp", None),
            P(("dp", "mp"), None),
        ),
        out_specs=(
            P(("dp", "mp"), None),
            P(("dp", "mp"), None),
            P(),
            P(),
            P(None, None, "mp"),
            P(None, "mp"),
            P("mp", None),
            P(),
            P(None, "mp"),
            P("mp"),
            P("mp", None),
        ),
        check_vma=False,
    )
```

```python
import functools

import jax
import jax.numpy as jnp
from jax import lax
from jax.experimental import pallas as pl
from jax.experimental.pallas import tpu as pltpu
from jax.sharding import PartitionSpec as P

HEAD_DIM = 64
EPSILON = 1e-06
KEEP_RATE = 0.9
MESH = pl.DeviceIdType.MESH
BF = jnp.bfloat16
F32 = jnp.float32
TILE = 96
JOBS = 3
SUBS = 4


def dot(left, right, left_dim, right_dim):
    return lax.dot_general(
        left, right, (((left_dim,), (right_dim,)), ((), ())), preferred_element_type=F32
    )


def normalise(rows):
    centred = rows - jnp.mean(rows, axis=-1, keepdims=True)
    spread = jnp.mean(centred * centred, axis=-1, keepdims=True)
    scale = lax.rsqrt(spread + EPSILON)
    return centred * scale, scale


def column_sum(rows):
    return jnp.sum(rows, axis=0, keepdims=True)


def layer_kernel(
    sizes,
    tok_in,
    cot_in,
    gain,
    shift,
    pbias,
    grids,
    masks,
    up_bias,
    qkv_bias,
    wqkv_in,
    wproj_in,
    wup_in,
    wdn_in,
    grads_out,
    tokens_grad,
    block_out,
    small_out,
    wqkv,
    wproj,
    wup,
    wdn,
    tok,
    cot,
    up_all,
    qkv_all,
    up_own,
    qkv_row,
    keep,
    entry,
    entry_two,
    ret_grad,
    heads,
    mixed,
    mixed_grad,
    mixer_grad,
    act,
    slope,
    work,
    middle,
    give,
    sum_core,
    got_x,
    got_y,
    got_z,
    small,
    small_got,
    small_from,
    local_sem,
    ag_send,
    ag_recv,
    bias_send,
    bias_recv,
    core_send,
    core_recv,
    x_send,
    x_recv,
    y_send,
    y_recv,
    z_send,
    z_recv,
    zag_send,
    zag_recv,
    yag_send,
    yag_recv,
    own_sem,
    small_send,
    small_recv,
):
    nz, images, slot, width, cols = sizes
    rows = images * slot
    pair = 2 * cols
    half = cols // 2
    packs = pair // 128
    per_unit = nz // 4
    units = JOBS * SUBS // per_unit

    d = lax.axis_index("dp")
    m = lax.axis_index("mp")
    y = lax.rem(d, 2)
    z = d // 2
    x = m // 2
    c = lax.rem(m, 2)
    core_dev = (d, x * 2 + 1 - c)
    x_dev = (d, (1 - x) * 2 + c)
    diag_dev = (d, (1 - x) * 2 + 1 - c)
    y_dev = (z * 2 + 1 - y, m)

    def z_dev(other):
        return (other * 2 + y, m)

    def remote(src, dst, send, recv, device):
        return pltpu.make_async_remote_copy(
            src_ref=src,
            dst_ref=dst,
            send_sem=send,
            recv_sem=recv,
            device_id=device,
            device_id_type=MESH,
        )

    tok_copy = pltpu.make_async_copy(tok_in, tok, local_sem.at[8])
    cot_copy = pltpu.make_async_copy(cot_in, cot, local_sem.at[9])
    tok_copy.start()
    cot_copy.start()
    barrier = pltpu.get_barrier_semaphore()
    greeted = [core_dev, x_dev, diag_dev, y_dev]
    greeted += [z_dev(lax.rem(z + k, nz)) for k in range(1, nz)]
    for device in greeted:
        pl.semaphore_signal(barrier, inc=1, device_id=device, device_id_type=MESH)
    pl.semaphore_wait(barrier, len(greeted))

    own_block = m
    peer_block = x * 2 + 1 - c
    far_block = (1 - x) * 2 + c
    far_peer = (1 - x) * 2 + 1 - c
    own_x = (x * 2, x * 2 + 1)

    pieces = [("q", 0), ("k", 0), ("v", 0), ("p", 0), ("u", 0), ("u", 1), ("d", 0), ("d", 1)]
    index_of = {piece: i for i, piece in enumerate(pieces)}
    big = width // 4

    def view(piece, block, part):
        kind, number = piece
        if kind in "qkvp":
            start, size = (0, cols) if part is None else (part * half, half)
            start = pl.multiple_of(block * cols + start, 16)
            if kind == "p":
                return wproj.at[pl.ds(start, size), :]
            return wqkv.at["qkv".index(kind), pl.ds(start, size), :]
        start, size = (0, 2 * big) if part is None else (part * big, big)
        start = pl.multiple_of(number * 2 * big + start, 16)
        return (wup if kind == "u" else wdn).at[block, pl.ds(start, size), :]

    def view_in(piece, part):
        kind, number = piece
        if kind in "qkvp":
            start, size = (0, cols) if part is None else (part * half, half)
            if part is not None:
                start = pl.multiple_of(start, 16)
            if kind == "p":
                return wproj_in.at[pl.ds(start, size), :]
            return wqkv_in.at["qkv".index(kind), pl.ds(start, size), :]
        start, size = (0, 2 * big) if part is None else (part * big, big)
        start = pl.multiple_of(number * 2 * big + start, 16)
        return (wup_in if kind == "u" else wdn_in).at[pl.ds(start, size), :]

    def ag_local(p):
        i = index_of[p]
        return pltpu.make_async_copy(view_in(p, None), view(p, own_block, None), local_sem.at[i])

    def ag_copy(route, p):
        i = index_of[p]
        send, recv = ag_send.at[route, i], ag_recv.at[route, i]
        if route == 0:
            return remote(view_in(p, None), view(p, own_block, None), send, recv, core_dev)
        if route == 1:
            return remote(view_in(p, y), view(p, own_block, y), send, recv, x_dev)
        part = 1 - y if route == 4 else y
        source = view(p, far_block, part)
        return remote(source, source, send, recv, y_dev if route == 2 else core_dev)

    def bias_copy(i):
        source, dest = (up_own, up_all) if i % 2 == 0 else (qkv_bias, qkv_all)
        device = (core_dev, x_dev, diag_dev)[i // 2]
        return remote(source, dest.at[m], bias_send.at[i], bias_recv.at[i], device)

    def bias_own(i):
        source, dest = (up_own, up_all) if i % 2 == 0 else (qkv_bias, qkv_all)
        return pltpu.make_async_copy(source, dest.at[m], local_sem.at[10 + i])

    up_own[...] = up_bias[...].reshape(1, width)
    for i in range(6):
        bias_copy(i).start()
    for i in range(2):
        bias_own(i).start()
    for p in pieces:
        ag_copy(1, p).start()
        ag_copy(0, p).start()
        ag_local(p).start()

    def near_ready(*names):
        for p in names:
            ag_local(p).wait()
            ag_copy(0, p).wait_recv()

    def from_x(*names):
        for p in names:
            ag_copy(1, p).wait_recv()
            ag_copy(2, p).start()
            ag_copy(3, p).start()

    def from_y(*names):
        for p in names:
            ag_copy(2, p).wait_recv()
            ag_copy(4, p).start()

    def far_ready(*names):
        for p in names:
            ag_copy(3, p).wait_recv()
            ag_copy(4, p).wait_recv()

    def sub_rows(sub):
        return sub // SUBS, pl.ds((sub % SUBS) * cols, cols)

    def core_copy(job, xb, slot_, sub):
        if sub is None:
            src, dst = give.at[job % 2, xb], sum_core.at[job, xb]
        else:
            part = pl.ds((sub % SUBS) * cols, cols)
            src, dst = give.at[job % 2, xb, part, :], sum_core.at[job, xb, part, :]
        return remote(src, dst, core_send.at[slot_], core_recv.at[slot_], core_dev)

    def x_copy(sub):
        job, part = sub_rows(sub)
        return remote(
            sum_core.at[job, 1 - x, part, :], got_x.at[sub], x_send.at[sub], x_recv.at[sub], x_dev
        )

    def y_part(sub, which):
        job, _ = sub_rows(sub)
        start = pl.multiple_of((sub % SUBS) * cols + which * half, 16)
        return job, pl.ds(start, half)

    def y_copy(sub):
        job, part = y_part(sub, 1 - y)
        return remote(
            sum_core.at[job, x, part, :], got_y.at[sub], y_send.at[sub], y_recv.at[sub], y_dev
        )

    tall, wide = half // 2, width // 2

    def z_part(owner):
        part = lax.rem(owner, 4)
        row = pl.multiple_of((part // 2) * tall, 16)
        col = pl.multiple_of(lax.rem(part, 2) * wide, 128)
        return owner // 4, row, col

    def z_copy(unit, step):
        owner = lax.rem(z + step, nz)
        inner, row, col = z_part(owner)
        src = got_y.at[unit * per_unit + inner, pl.ds(row, tall), pl.ds(col, wide)]
        sem = unit * (nz - 1) + step - 1
        return remote(
            src, got_z.at[unit, step - 1], z_send.at[sem], z_recv.at[sem], z_dev(owner)
        )

    def final_part(unit):
        inner, row, col = z_part(z)
        row = pl.multiple_of(y * half + row, 16)
        return grads_out.at[unit * per_unit + inner, pl.ds(row, tall), pl.ds(col, wide)]

    def zag_copy(unit, step):
        sem = unit * (nz - 1) + step - 1
        return remote(
            got_z.at[unit, nz - 1],
            final_part(unit),
            zag_send.at[sem],
            zag_recv.at[sem],
            z_dev(lax.rem(z + step, nz)),
        )

    def own_copy(unit):
        return pltpu.make_async_copy(got_z.at[unit, nz - 1], final_part(unit), own_sem.at[unit])

    def yag_copy(unit):
        part = grads_out.at[
            pl.ds(unit * per_unit, per_unit), pl.ds(pl.multiple_of(y * half, 16), half), :
        ]
        return remote(part, part, yag_send.at[unit], yag_recv.at[unit], y_dev)

    def x_stage(sub):
        x_copy(sub).wait_recv()
        job, part = sub_rows(sub)
        total = sum_core[job, x, part, :].astype(F32) + got_x[sub].astype(F32)
        sum_core[job, x, part, :] = total.astype(BF)
        y_copy(sub).start()

    def y_stage(sub):
        y_copy(sub).wait_recv()
        job, part = y_part(sub, y)
        total = sum_core[job, x, part, :].astype(F32) + got_y[sub].astype(F32)
        got_y[sub] = total.astype(BF)
        if sub % per_unit == per_unit - 1:
            for step in range(1, nz):
                z_copy(sub // per_unit, step).start()

    def z_stage(sub):
        if sub % per_unit != per_unit - 1:
            return
        unit = sub // per_unit
        inner, row, col = z_part(z)
        total = got_y[unit * per_unit + inner, pl.ds(row, tall), pl.ds(col, wide)].astype(F32)
        for step in range(1, nz):
            z_copy(unit, step).wait_recv()
            total = total + got_z[unit, step - 1].astype(F32)
        got_z[unit, nz - 1] = total.astype(BF)
        own_copy(unit).start()
        for step in range(1, nz):
            zag_copy(unit, step).start()

    def zag_stage(sub):
        if sub % per_unit != per_unit - 1:
            return
        unit = sub // per_unit
        own_copy(unit).wait()
        for step in range(1, nz):
            zag_copy(unit, step).wait_recv()
        yag_copy(unit).start()

    stages = (x_stage, y_stage, z_stage, zag_stage)
    ticks = [0]

    def tick():
        now = ticks[0]
        ticks[0] += 1
        for lag, stage in enumerate(stages):
            if 0 <= now - lag < JOBS * SUBS:
                stage(now - lag)

    def live_rate(which, image, row):
        index = m * images + image
        length = grids[0, index] * grids[1, index] + 2
        kept = masks[which, index].astype(F32) / KEEP_RATE
        position = lax.broadcasted_iota(jnp.int32, (TILE, 1), 0) + row
        return jnp.where(position < length, kept, 0.0)

    def over_rows(body):
        for image in range(images):

            def step(i, carry):
                row = i * TILE
                body(image, row, pl.ds(pl.multiple_of(image * slot + row, 16), TILE))
                return carry

            lax.fori_loop(0, slot // TILE, step, 0, unroll=True)

    small[...] = jnp.zeros_like(small)

    def first_norm(image, row, at):
        normed, _ = normalise(tok[at, :].astype(F32))
        entry[at, :] = (normed * gain[0:1, :] + shift[0:1, :]).astype(BF)

    def return_rows(image, row, at):
        grad = live_rate(1, image, row) * cot[at, :].astype(F32)
        ret_grad[at, :] = grad.astype(BF)
        small[7:8, :] += column_sum(grad)

    tok_copy.wait()
    over_rows(first_norm)

    lane = lax.broadcasted_iota(jnp.int32, (slot, 128), 1)
    low_lanes = lane < HEAD_DIM
    position = lax.broadcasted_iota(jnp.int32, (slot, slot), 1)
    score_scale = HEAD_DIM ** (-0.5)

    def pick(head, values):
        mask = low_lanes if head == 0 else jnp.logical_not(low_lanes)
        return jnp.where(mask, values, jnp.zeros_like(values))

    def key_length(image):
        index = m * images + image
        return grids[0, index] * grids[1, index] + 2

    def softmax(queries, keys, length):
        scores = dot(queries, keys, 1, 1) * score_scale
        scores = jnp.where(position < length, scores, -1000000000.0)
        raised = jnp.exp(scores - jnp.max(scores, axis=-1, keepdims=True))
        return raised * (1.0 / jnp.sum(raised, axis=-1, keepdims=True))

    def project(xb):
        at = pl.ds(pl.multiple_of(xb * pair, 16), pair)
        qkv_row[:, 0:cols] = qkv_all[xb * 2]
        qkv_row[:, cols:pair] = qkv_all[xb * 2 + 1]
        for j in range(3):
            value = dot(entry[...], wqkv[j, at, :], 1, 1)
            if j != 1:
                row = j // 2
                value = value + qkv_row[row : row + 1, :]
            value = value.astype(BF)
            for pack in range(packs):
                heads[j, xb * packs + pack] = value[:, pack * 128 : (pack + 1) * 128]

    def attend(xb, image):
        def step(i, carry):
            pack = xb * packs + i
            at = pl.ds(pl.multiple_of(image * slot, 16), slot)
            queries, keys, values = (heads[j, pack, at, :] for j in range(3))
            length = key_length(image)
            total = jnp.zeros((slot, 128), F32)
            for head in range(2):
                probs = softmax(queries, pick(head, keys), length).astype(BF)
                total = total + dot(probs, pick(head, values), 1, 0)
            mixed[pack, at, :] = total.astype(BF)
            return carry

        lax.fori_loop(0, packs, step, 0)

    for i in range(2):
        bias_own(i).wait()
    for i in range(6):
        bias_copy(i).wait_recv()
    cot_copy.wait()
    near_ready(("q", 0), ("k", 0), ("v", 0))
    project(x)
    from_x(("q", 0))
    for image in range(images):
        attend(x, image)
        from_x((("k", 0), ("v", 0))[image % 2])
    from_y(("q", 0))
    over_rows(return_rows)
    from_x(("p", 0))
    from_y(("k", 0), ("v", 0))
    far_ready(("q", 0), ("k", 0), ("v", 0))
    project(1 - x)
    from_y(("p", 0))
    for image in range(images):
        attend(1 - x, image)
        from_x(("u", image % 2))

    near_ready(("p", 0))
    far_ready(("p", 0))
    all_mixed = jnp.concatenate([mixed[pack] for pack in range(2 * packs)], axis=1)
    work[...] = dot(all_mixed, wproj[...], 1, 0)

    def second_norm(image, row, at):
        value = tok[at, :].astype(F32) + live_rate(0, image, row) * (work[at, :] + pbias[0:1, :])
        middle[at, :] = value
        normed, _ = normalise(value)
        entry_two[at, :] = (normed * gain[1:2, :] + shift[1:2, :]).astype(BF)

    over_rows(second_norm)

    def emit_wide(job, xb, mine, value):
        slot_ = job * 2 + (0 if mine[1] else 1)
        if not mine[0]:
            give[job % 2, xb] = value.astype(BF)
            core_copy(job, xb, slot_, None).start()
        else:
            core_copy(job, xb, slot_, None).wait_recv()
            sum_core[job, xb] = (value + sum_core[job, xb].astype(F32)).astype(BF)
            if mine[1]:
                for s in range(SUBS):
                    x_copy(job * SUBS + s).start()

    def gelu_loop(block):
        def step(i, carry):
            at = pl.ds(pl.multiple_of(i * TILE, 16), TILE)
            hidden = work[at, :] + up_all[block]
            share = 0.5 * (1.0 + lax.erf(hidden * 0.7071067811865476))
            density = jnp.exp(-0.5 * hidden * hidden) * 0.3989422804014327
            act[block, at, :] = (hidden * share).astype(BF)
            slope[block, at, :] = (share + hidden * density).astype(BF)
            return carry

        lax.fori_loop(0, rows // TILE, step, 0)

    def feed_first(block, xb, mine):
        work[...] = dot(entry_two[...], wup[block], 1, 0)
        gelu_loop(block)
        emit_wide(0, xb, mine, dot(act[block], ret_grad[...], 0, 0))

    def feed_back(block, xb, mine, first):
        work[...] = dot(ret_grad[...], wdn[block], 1, 1)

        def step(i, carry):
            at = pl.ds(pl.multiple_of(i * TILE, 16), TILE)
            grad = (work[at, :] * slope[block, at, :].astype(F32)).astype(BF)
            slope[block, at, :] = grad
            small[pl.ds(8 + block, 1), :] += column_sum(grad.astype(F32))
            return carry

        lax.fori_loop(0, rows // TILE, step, 0)
        emit_wide(1, xb, mine, dot(entry_two[...], slope[block], 0, 0))
        value = dot(slope[block], wup[block], 1, 1)
        if first:
            tokens_grad[...] = value
        else:
            tokens_grad[...] += value

    order = (
        (far_peer, 1 - x, (False, True)),
        (far_block, 1 - x, (True, True)),
        (peer_block, x, (False, False)),
        (own_block, x, (True, False)),
    )
    near_ready(("u", 0), ("u", 1))
    feed_first(*order[2])
    from_y(("u", 0))
    from_x(("d", 0))
    feed_first(*order[3])
    from_y(("u", 1))
    from_x(("d", 1))
    far_ready(("u", 0), ("u", 1))
    feed_first(*order[0])
    from_y(("d", 0))
    feed_first(*order[1])
    from_y(("d", 1))
    near_ready(("d", 0), ("d", 1))
    far_ready(("d", 0), ("d", 1))
    feed_back(*order[0], True)
    feed_back(*order[1], False)
    tick()
    feed_back(*order[2], False)
    tick()
    feed_back(*order[3], False)
    tick()

    def norm_back(values, grad, r):
        normed, scale = normalise(values)
        small[r : r + 1, :] += column_sum(grad * normed)
        small[2 + r : 3 + r, :] += column_sum(grad)
        scaled = grad * gain[r : r + 1, :]
        mean_one = jnp.mean(scaled, axis=-1, keepdims=True)
        mean_two = jnp.mean(scaled * normed, axis=-1, keepdims=True)
        return scale * (scaled - mean_one - normed * mean_two)

    def second_back(image, row, at):
        grad = cot[at, :].astype(F32) + norm_back(middle[at, :], tokens_grad[at, :], 1)
        tokens_grad[at, :] = grad
        scaled = live_rate(0, image, row) * grad
        mixer_grad[at, :] = scaled.astype(BF)
        small[6:7, :] += column_sum(scaled)

    over_rows(second_back)

    core_copy(0, 1 - x, 0, None).wait_send()
    core_copy(0, x, 1, None).wait_send()
    waiting = []

    def emit_narrow(s, xb, far, value):
        part = pl.ds(s * cols, cols)
        place = len(waiting) % 2
        keep[place] = value
        theirs = pl.multiple_of((1 - c) * cols, 16)
        give[0, xb, part, :] = keep[place, pl.ds(theirs, cols), :].astype(BF)
        core_copy(2, xb, 4 + s * 2 + (0 if far else 1), 2 * SUBS + s).start()
        waiting.append((s, xb, far, place))

    def settle(left):
        while len(waiting) - settled[0] > left:
            s, xb, far, place = waiting[settled[0]]
            settled[0] += 1
            sub = 2 * SUBS + s
            part = pl.ds(s * cols, cols)
            ours = pl.multiple_of(c * cols, 16)
            core_copy(2, xb, 4 + s * 2 + (0 if far else 1), sub).wait_recv()
            total = keep[place, pl.ds(ours, cols), :] + sum_core[2, xb, part, :].astype(F32)
            sum_core[2, xb, part, :] = total.astype(BF)
            if far:
                x_copy(sub).start()

    settled = [0]

    def side(ref, xb):
        return jnp.concatenate([ref[xb * packs + pack] for pack in range(packs)], axis=1)

    def attend_back(xb, image):
        def step(i, carry):
            pack = xb * packs + i
            at = pl.ds(pl.multiple_of(image * slot, 16), slot)
            queries, keys, values = (heads[j, pack, at, :] for j in range(3))
            grads = mixed_grad[pack, at, :]
            length = key_length(image)
            query_grad = jnp.zeros((slot, 128), F32)
            key_grad = jnp.zeros((slot, 128), F32)
            value_grad = jnp.zeros((slot, 128), F32)
            for head in range(2):
                head_keys = pick(head, keys)
                probs = softmax(queries, head_keys, length)
                probs_grad = dot(grads, pick(head, values), 1, 1)
                inner = jnp.sum(probs * probs_grad, axis=-1, keepdims=True)
                score_grad = (probs * (probs_grad - inner)).astype(BF)
                query_grad = query_grad + dot(score_grad, head_keys, 1, 0)
                key_grad = key_grad + dot(score_grad, pick(head, queries), 0, 0)
                value_grad = value_grad + dot(probs.astype(BF), pick(head, grads), 0, 0)
            heads[0, pack, at, :] = (query_grad * score_scale).astype(BF)
            heads[1, pack, at, :] = (key_grad * score_scale).astype(BF)
            heads[2, pack, at, :] = value_grad.astype(BF)
            return carry

        lax.fori_loop(0, packs, step, 0)

    def qkv_back(xb, far):
        lanes = pl.ds(pl.multiple_of(xb * pair, 128), pair)
        for j in range(3):
            grad = side(heads.at[j], xb)
            emit_narrow(1 + j, xb, far, dot(grad, entry[...], 0, 0))
            settle(1)
            if j != 1:
                row = 4 if j == 0 else 5
                small[row : row + 1, lanes] = column_sum(grad.astype(F32))

    value = dot(mixer_grad[...], wproj[...], 1, 1).astype(BF)
    for pack in range(2 * packs):
        mixed_grad[pack] = value[:, pack * 128 : (pack + 1) * 128]
    for xb, far in ((1 - x, True), (x, False)):
        emit_narrow(0, xb, far, dot(side(mixed, xb), mixer_grad[...], 0, 0))
    settle(1)
    tick()
    for image in range(images):
        attend_back(1 - x, image)
        settle(0)
        tick()
    qkv_back(1 - x, True)
    settle(0)
    tick()
    for image in range(images):
        attend_back(x, image)
        tick()
    qkv_back(x, False)
    settle(0)
    tick()

    for j in range(3):
        grad = jnp.concatenate([heads[j, pack] for pack in range(2 * packs)], axis=1)
        part = dot(grad, wqkv[j], 1, 0)
        work[...] = part if j == 0 else work[...] + part

    def first_back(image, row, at):
        tokens_grad[at, :] += norm_back(tok[at, :].astype(F32), work[at, :], 0)

    tick()
    over_rows(first_back)

    def small_copy(stage, device):
        return remote(
            small_got.at[stage],
            small_from.at[stage],
            small_send.at[stage],
            small_recv.at[stage],
            device,
        )

    small_got[0] = small[...]
    small_copy(0, core_dev).start()
    tick()
    for i, (block, _, _) in enumerate(order):
        part = dot(act[block], wdn[block], 1, 0)
        work[...] = part if i == 0 else work[...] + part
        if i == 1:
            small_copy(0, core_dev).wait_recv()
            small_got[1] = small_got[0] + small_from[0]
            small_copy(1, x_dev).start()
            tick()

    def finish(image, row, at):
        value = middle[at, :] + live_rate(1, image, row) * (work[at, :] + pbias[1:2, :])
        block_out[at, :] = value.astype(BF)

    tick()
    over_rows(finish)
    small_copy(1, x_dev).wait_recv()
    small_got[2] = small_got[1] + small_from[1]
    small_copy(2, y_dev).start()
    tick()
    small_copy(2, y_dev).wait_recv()
    mine = 3 + z
    small_got[mine] = small_got[2] + small_from[2]

    def small_z(step):
        sem = 2 + step
        return remote(
            small_got.at[mine],
            small_got.at[mine],
            small_send.at[sem],
            small_recv.at[sem],
            z_dev(lax.rem(z + step, nz)),
        )

    for step in range(1, nz):
        small_z(step).start()
    while ticks[0] < JOBS * SUBS + len(stages) - 1:
        tick()
    for step in range(1, nz):
        small_z(step).wait_recv()
    total = small_got[3]
    for other in range(1, nz):
        total = total + small_got[3 + other]
    small[...] = total
    small_out[0:8, :] = small[0:8, :]
    qkv_row[...] = small[4:6, pl.ds(pl.multiple_of(x * pair, 128), pair)]
    small_out[8:10, 0:cols] = jnp.where(c == 0, qkv_row[:, 0:cols], qkv_row[:, cols:pair])
    small_out[10:11, :] = small[pl.ds(8 + m, 1), :]

    for unit in range(units):
        yag_copy(unit).wait_recv()
    for i in range(6):
        bias_copy(i).wait_send()
    for p in pieces:
        for route in range(5):
            ag_copy(route, p).wait_send()
    core_copy(1, 1 - x, 2, None).wait_send()
    core_copy(1, x, 3, None).wait_send()
    for s in range(SUBS):
        for k, xb in enumerate((1 - x, x)):
            core_copy(2, xb, 4 + s * 2 + k, 2 * SUBS + s).wait_send()
    for sub in range(JOBS * SUBS):
        x_copy(sub).wait_send()
        y_copy(sub).wait_send()
    for unit in range(units):
        for step in range(1, nz):
            z_copy(unit, step).wait_send()
            zag_copy(unit, step).wait_send()
        yag_copy(unit).wait_send()
    small_copy(0, core_dev).wait_send()
    small_copy(1, x_dev).wait_send()
    small_copy(2, y_dev).wait_send()
    for step in range(1, nz):
        small_z(step).wait_send()


def finish_kernel(
    grads,
    tokens_part,
    block_part,
    small,
    block_out,
    tokens_grad,
    gain_grad,
    shift_grad,
    qkv_grad,
    qkv_bias_grad,
    proj_grad,
    proj_bias_grad,
    up_grad,
    up_bias_grad,
    down_grad,
):
    block_out[...] = block_part[...]
    tokens_grad[...] = tokens_part[...]
    down_grad[...] = grads[0:SUBS].astype(F32)
    up_grad[...] = grads[SUBS : 2 * SUBS].astype(F32)
    proj_grad[...] = grads[2 * SUBS].astype(F32)
    qkv_grad[...] = grads[2 * SUBS + 1 :].astype(F32)

    @pl.when(pl.program_id(0) == 0)
    def _():
        gain_grad[...] = small[0:2, :]
        shift_grad[...] = small[2:4, :]
        proj_bias_grad[...] = small[6:8, :]
        qkv_bias_grad[...] = small[8:10, 0 : qkv_bias_grad.shape[1]]
        up_bias_grad[...] = small[10:11, :].reshape(up_bias_grad.shape)


def local(
    tokens,
    norm_gain,
    norm_shift,
    qkv_weight,
    qkv_bias,
    proj_weight,
    proj_bias,
    up_weight,
    up_bias,
    down_weight,
    patch_grids,
    keep_masks,
    out_cotangent,
):
    rows, width = tokens.shape
    mp = lax.axis_size("mp")
    nz = lax.axis_size("dp") // 2
    images = patch_grids.shape[0] // mp
    slot = rows // images
    cols = qkv_weight.shape[2]
    pair = 2 * cols
    packs = pair // 128
    units = JOBS * SUBS // (nz // 4)
    qkv_rows = jnp.transpose(qkv_weight, (0, 2, 1))
    vmem = pl.BlockSpec(memory_space=pltpu.VMEM)
    smem = pl.BlockSpec(memory_space=pltpu.SMEM)
    hbm = pl.BlockSpec(memory_space=pl.ANY)
    dma = pltpu.SemaphoreType.DMA
    scratch = [
        pltpu.VMEM((3, width, width), BF),
        pltpu.VMEM((width, width), BF),
        pltpu.VMEM((4, width, width), BF),
        pltpu.VMEM((4, width, width), BF),
        pltpu.VMEM((rows, width), BF),
        pltpu.VMEM((rows, width), BF),
        pltpu.VMEM((4, 1, width), F32),
        pltpu.VMEM((4, 2, cols), F32),
        pltpu.VMEM((1, width), F32),
        pltpu.VMEM((2, pair), F32),
        pltpu.VMEM((2, pair, width), F32),
        pltpu.VMEM((rows, width), BF),
        pltpu.VMEM((rows, width), BF),
        pltpu.VMEM((rows, width), BF),
        pltpu.VMEM((3, 2 * packs, rows, 128), BF),
        pltpu.VMEM((2 * packs, rows, 128), BF),
        pltpu.VMEM((2 * packs, rows, 128), BF),
        pltpu.VMEM((rows, width), BF),
        pltpu.VMEM((4, rows, width), BF),
        pltpu.VMEM((4, rows, width), BF),
        pltpu.VMEM((rows, width), F32),
        pltpu.VMEM((rows, width), F32),
        pltpu.VMEM((2, 2, width, width), BF),
        pltpu.VMEM((JOBS, 2, width, width), BF),
        pltpu.VMEM((JOBS * SUBS, cols, width), BF),
        pltpu.VMEM((JOBS * SUBS, cols // 2, width), BF),
        pltpu.VMEM((units, nz, cols // 4, width // 2), BF),
        pltpu.VMEM((16, width), F32),
        pltpu.VMEM((3 + nz, 16, width), F32),
        pltpu.VMEM((3, 16, width), F32),
        dma((12,)),
        dma((5, 8)),
        dma((5, 8)),
        dma((6,)),
        dma((6,)),
        dma((12,)),
        dma((12,)),
        dma((JOBS * SUBS,)),
        dma((JOBS * SUBS,)),
        dma((JOBS * SUBS,)),
        dma((JOBS * SUBS,)),
        dma((units * (nz - 1),)),
        dma((units * (nz - 1),)),
        dma((units * (nz - 1),)),
        dma((units * (nz - 1),)),
        dma((units,)),
        dma((units,)),
        dma((units,)),
        dma((2 + nz,)),
        dma((2 + nz,)),
    ]
    grads, tokens_grad, block_out, small = pl.pallas_call(
        functools.partial(layer_kernel, (nz, images, slot, width, cols)),
        out_shape=(
            jax.ShapeDtypeStruct((JOBS * SUBS, cols, width), BF),
            jax.ShapeDtypeStruct((rows, width), F32),
            jax.ShapeDtypeStruct((rows, width), BF),
            jax.ShapeDtypeStruct((16, width), F32),
        ),
        in_specs=[hbm] * 2 + [vmem] * 3 + [smem] * 2 + [vmem] * 2 + [hbm] * 4,
        out_specs=(hbm, vmem, vmem, vmem),
        scratch_shapes=scratch,
        compiler_params=pltpu.CompilerParams(
            collective_id=0, has_side_effects=True, vmem_limit_bytes=64 * 2**20 - 2**17
        ),
    )(
        tokens,
        out_cotangent,
        norm_gain,
        norm_shift,
        proj_bias,
        patch_grids.T,
        keep_masks.T,
        up_bias,
        qkv_bias,
        qkv_rows,
        proj_weight,
        up_weight,
        down_weight,
    )
    steps = width // 128
    block = functools.partial(pl.BlockSpec, memory_space=pltpu.VMEM)
    out = pl.pallas_call(
        finish_kernel,
        grid=(steps,),
        out_shape=(
            jax.ShapeDtypeStruct((rows, width), BF),
            jax.ShapeDtypeStruct((rows, width), F32),
            jax.ShapeDtypeStruct((2, width), F32),
            jax.ShapeDtypeStruct((2, width), F32),
            jax.ShapeDtypeStruct((3, cols, width), F32),
            jax.ShapeDtypeStruct((2, cols), F32),
            jax.ShapeDtypeStruct((cols, width), F32),
            jax.ShapeDtypeStruct((2, width), F32),
            jax.ShapeDtypeStruct((SUBS, cols, width), F32),
            jax.ShapeDtypeStruct((width,), F32),
            jax.ShapeDtypeStruct((SUBS, cols, width), F32),
        ),
        in_specs=[
            block((JOBS * SUBS, cols // steps, width), lambda i: (0, i, 0)),
            block((rows // steps, width), lambda i: (i, 0)),
            block((rows // steps, width), lambda i: (i, 0)),
            block((16, width), lambda i: (0, 0)),
        ],
        out_specs=(
            block((rows // steps, width), lambda i: (i, 0)),
            block((rows // steps, width), lambda i: (i, 0)),
            block((2, width), lambda i: (0, 0)),
            block((2, width), lambda i: (0, 0)),
            block((3, cols // steps, width), lambda i: (0, i, 0)),
            block((2, cols), lambda i: (0, 0)),
            block((cols // steps, width), lambda i: (i, 0)),
            block((2, width), lambda i: (0, 0)),
            block((SUBS, cols // steps, width), lambda i: (0, i, 0)),
            block((width,), lambda i: (0,)),
            block((SUBS, cols // steps, width), lambda i: (0, i, 0)),
        ),
        compiler_params=pltpu.CompilerParams(vmem_limit_bytes=60 * 2**20),
    )(grads, tokens_grad, block_out, small)
    out = list(out)
    out[4] = jnp.transpose(out[4], (0, 2, 1))
    out[8] = out[8].reshape(up_weight.shape)
    out[10] = out[10].reshape(down_weight.shape)
    return tuple(out)


def solution(mesh):
    return jax.shard_map(
        local,
        mesh=mesh,
        in_specs=(
            P(("dp", "mp"), None),
            P(),
            P(),
            P(None, None, "mp"),
            P(None, "mp"),
            P("mp", None),
            P(),
            P(None, "mp"),
            P("mp"),
            P("mp", None),
            P("dp", None),
            P("dp", None),
            P(("dp", "mp"), None),
        ),
        out_specs=(
            P(("dp", "mp"), None),
            P(("dp", "mp"), None),
            P(),
            P(),
            P(None, None, "mp"),
            P(None, "mp"),
            P("mp", None),
            P(),
            P(None, "mp"),
            P("mp"),
            P("mp", None),
        ),
        check_vma=False,
    )
```

```python
import functools
import heapq

import jax
import jax.numpy as jnp
from jax import lax
from jax.experimental import pallas as pl
from jax.experimental.pallas import tpu as pltpu
from jax.sharding import PartitionSpec as P

HEAD_DIM = 64
EPSILON = 1e-06
KEEP_RATE = 0.9
MESH = pl.DeviceIdType.MESH
BF = jnp.bfloat16
F32 = jnp.float32
TILE = 96
JOBS = 3
SUBS = 4
LINK_ROW = 0.033
HOP = 2.5
HANDLE = 0.4


def dot(left, right, left_dim, right_dim):
    return lax.dot_general(
        left, right, (((left_dim,), (right_dim,)), ((), ())), preferred_element_type=F32
    )


def normalise(rows):
    centred = rows - jnp.mean(rows, axis=-1, keepdims=True)
    spread = jnp.mean(centred * centred, axis=-1, keepdims=True)
    scale = lax.rsqrt(spread + EPSILON)
    return centred * scale, scale


def sub_list(width, cols):
    parts = [(k * cols, cols) for k in range(JOBS * SUBS)]
    third = cols // 3
    first = [(k * third, third) for k in range(3)]
    last = [(parts[-1][0] + k * third, third) for k in range(3)]
    return first + parts[1:-1] + last


class Agenda:
    def __init__(self):
        self.now = 0.0
        self.free = {}
        self.queue = []
        self.number = 0

    def send(self, link, rows):
        begin = max(self.now, self.free.get(link, 0.0))
        self.free[link] = begin + rows * LINK_ROW
        return self.free[link] + HOP

    def post(self, ready, action):
        self.number += 1
        heapq.heappush(self.queue, (ready, self.number, action))

    def handle(self):
        ready, _, action = heapq.heappop(self.queue)
        self.now = max(self.now, ready) + HANDLE
        action()

    def spend(self, time):
        self.now += time
        while self.queue and self.queue[0][0] <= self.now:
            self.handle()

    def until(self, reached):
        while not reached():
            self.handle()


def column_sum(rows):
    return jnp.sum(rows, axis=0, keepdims=True)


def layer_kernel(
    sizes,
    tok_in,
    cot_in,
    gain,
    shift,
    pbias,
    grids,
    masks,
    up_bias,
    qkv_bias,
    wqkv_in,
    wproj_in,
    wup_in,
    wdn_in,
    grads_out,
    tokens_grad,
    block_out,
    small_out,
    wqkv,
    wproj,
    wup,
    wdn,
    tok,
    cot,
    up_all,
    qkv_all,
    up_own,
    qkv_row,
    keep,
    entry,
    entry_two,
    ret_grad,
    heads,
    mixed,
    mixed_grad,
    act,
    slope,
    work,
    middle,
    give,
    sum_core,
    got_x,
    got_y,
    got_z,
    got_group,
    small,
    small_got,
    small_from,
    local_sem,
    ag_send,
    ag_recv,
    bias_send,
    bias_recv,
    core_send,
    core_recv,
    x_send,
    x_recv,
    y_send,
    y_recv,
    z_send,
    z_recv,
    group_send,
    group_recv,
    zag_send,
    zag_recv,
    yag_send,
    yag_recv,
    own_sem,
    small_send,
    small_recv,
):
    nz, images, slot, width, cols = sizes
    rows = images * slot
    pair = 2 * cols
    half = cols // 2
    packs = pair // 128
    groups = nz // 4
    subs = sub_list(width, cols)

    d = lax.axis_index("dp")
    m = lax.axis_index("mp")
    y = lax.rem(d, 2)
    z = d // 2
    x = m // 2
    c = lax.rem(m, 2)
    core_dev = (d, x * 2 + 1 - c)
    x_dev = (d, (1 - x) * 2 + c)
    diag_dev = (d, (1 - x) * 2 + 1 - c)
    y_dev = (z * 2 + 1 - y, m)
    group, quad = z // 4, lax.rem(z, 4)

    def z_dev(other):
        return (other * 2 + y, m)

    def quad_dev(step):
        return z_dev(group * 4 + lax.rem(quad + step, 4))

    def group_dev(step):
        return z_dev(lax.rem(group + step, groups) * 4 + quad)

    def remote(src, dst, send, recv, device):
        return pltpu.make_async_remote_copy(
            src_ref=src,
            dst_ref=dst,
            send_sem=send,
            recv_sem=recv,
            device_id=device,
            device_id_type=MESH,
        )

    tok_copy = pltpu.make_async_copy(tok_in, tok, local_sem.at[8])
    cot_copy = pltpu.make_async_copy(cot_in, cot, local_sem.at[9])
    tok_copy.start()
    cot_copy.start()
    barrier = pltpu.get_barrier_semaphore()
    greeted = [core_dev, x_dev, diag_dev, y_dev]
    greeted += [quad_dev(k) for k in range(1, 4)]
    greeted += [group_dev(k) for k in range(1, groups)]
    for device in greeted:
        pl.semaphore_signal(barrier, inc=1, device_id=device, device_id_type=MESH)
    pl.semaphore_wait(barrier, len(greeted))

    own_block = m
    peer_block = x * 2 + 1 - c
    far_block = (1 - x) * 2 + c
    far_peer = (1 - x) * 2 + 1 - c

    pieces = ("qk", "v", "p", "u0", "u1", "d")
    near_z = z + 1 - 2 * lax.rem(z, 2)
    side_z = lax.rem(z, 2)
    quarters = (y * 2 + side_z, (1 - y) * 2 + side_z, y * 2 + 1 - side_z, 3 - y * 2 - side_z)
    wide = width // 2

    def rows_of(piece, part):
        size = {"u0": width // 2, "u1": width // 2, "d": width}.get(piece, cols)
        if part is None:
            return 0, size
        return quarters[part] * (size // 4), size // 4

    def view(piece, block, part, lanes=None):
        start, size = rows_of(piece, part)
        lanes = pl.ds(0, width) if lanes is None else pl.ds(lanes * wide, wide)
        if piece in ("qk", "v", "p"):
            at = pl.ds(pl.multiple_of(block * cols + start, 16), size)
            if piece == "p":
                return wproj.at[at, lanes]
            return wqkv.at[pl.ds(0, 2) if piece == "qk" else pl.ds(2, 1), at, lanes]
        first = width // 2 if piece == "u1" else 0
        at = pl.ds(pl.multiple_of(first + start, 16), size)
        return (wdn if piece == "d" else wup).at[block, at, lanes]

    def view_in(piece, part):
        start, size = rows_of(piece, part)
        first = width // 2 if piece == "u1" else 0
        at = pl.ds(first + start if part is None else pl.multiple_of(first + start, 16), size)
        if piece in ("qk", "v"):
            return wqkv_in.at[pl.ds(0, 2) if piece == "qk" else pl.ds(2, 1), at, :]
        return {"p": wproj_in, "d": wdn_in}.get(piece, wup_in).at[at, :]

    def ag_local(p):
        i = pieces.index(p)
        return pltpu.make_async_copy(view_in(p, None), view(p, own_block, None), local_sem.at[i])

    def ag_copy(route, p):
        i = pieces.index(p)
        send, recv = ag_send.at[route, i], ag_recv.at[route, i]
        if route == 0:
            return remote(view_in(p, None), view(p, own_block, None), send, recv, core_dev)
        if route == 1:
            return remote(view_in(p, 0), view(p, own_block, 0), send, recv, x_dev)
        if route == 2:
            part, lanes, device = 0, None, y_dev
        elif route == 3:
            part, lanes, device = 0, None, z_dev(near_z)
        elif route == 4:
            part, lanes, device = 2, 0, y_dev
        elif route == 5:
            part, lanes, device = 1, 1, z_dev(near_z)
        else:
            part, lanes, device = route - 6, None, core_dev
        source = view(p, far_block, part, lanes)
        return remote(source, source, send, recv, device)

    def quarter_rows(p):
        return rows_of(p, None)[1] // 4 * (2 if p == "qk" else 1)

    def from_x(p):
        ag_copy(1, p).wait_recv()
        for route in (2, 3, 6):
            ag_copy(route, p).start()
        ready = max(agenda.send("y", quarter_rows(p)), agenda.send("z", quarter_rows(p)))
        agenda.post(ready, functools.partial(from_yz, p))

    def from_yz(p):
        ag_copy(2, p).wait_recv()
        ag_copy(5, p).start()
        ag_copy(7, p).start()
        ag_copy(3, p).wait_recv()
        ag_copy(4, p).start()
        ag_copy(8, p).start()
        rows_ = quarter_rows(p) // 2
        ready = max(agenda.send("y", rows_), agenda.send("z", rows_))
        agenda.post(ready, functools.partial(from_both, p))

    def from_both(p):
        ag_copy(4, p).wait_recv()
        ag_copy(5, p).wait_recv()
        ag_copy(9, p).start()
        gathered.add(p)

    def bias_copy(i):
        source, dest = (up_own, up_all) if i % 2 == 0 else (qkv_bias, qkv_all)
        device = (x_dev, diag_dev, core_dev)[i // 2]
        return remote(source, dest.at[m], bias_send.at[i], bias_recv.at[i], device)

    def bias_own(i):
        source, dest = (up_own, up_all) if i % 2 == 0 else (qkv_bias, qkv_all)
        return pltpu.make_async_copy(source, dest.at[m], local_sem.at[10 + i])

    up_own[...] = up_bias[...].reshape(1, width)
    for i in range(4):
        bias_copy(i).start()
    agenda = Agenda()
    gathered = set()
    for p in pieces:
        ag_copy(1, p).start()
        agenda.post(agenda.send("x", quarter_rows(p)), functools.partial(from_x, p))
    for p in pieces[:2]:
        ag_copy(0, p).start()
        ag_local(p).start()
    for i in range(2):
        bias_copy(4 + i).start()
        bias_own(i).start()

    def near_ready(*names):
        for p in names:
            ag_local(p).wait()
            ag_copy(0, p).wait_recv()

    def far_ready(*names):
        for p in names:
            agenda.until(lambda: p in gathered)
            for route in (6, 7, 8, 9):
                ag_copy(route, p).wait_recv()

    core_started = []

    def core_copy(job, xb, slot_, first, size):
        at = pl.ds(first, size)
        return remote(
            give.at[job % 2, xb, at, :],
            sum_core.at[job, xb, at, :],
            core_send.at[slot_],
            core_recv.at[slot_],
            core_dev,
        )

    def core_start(*copy):
        core_started.append(copy)
        core_copy(*copy).start()

    def x_copy(sub):
        first, size = subs[sub]
        source = sum_core.at[first // width, 1 - x, pl.ds(first % width, size), :]
        return remote(
            source, got_x.at[pl.ds(first, size), :], x_send.at[sub], x_recv.at[sub], x_dev
        )

    def y_part(sub, which):
        first, size = subs[sub]
        start = pl.multiple_of(first % width + which * (size // 2), 16)
        return first // width, pl.ds(start, size // 2)

    def y_got(sub):
        first, size = subs[sub]
        return pl.ds(first // 2, size // 2)

    def y_copy(sub):
        job, at = y_part(sub, 1 - y)
        return remote(
            sum_core.at[job, x, at, :],
            got_y.at[y_got(sub), :],
            y_send.at[sub],
            y_recv.at[sub],
            y_dev,
        )

    def z_part(sub, owner):
        tall = subs[sub][1] // 4
        row = pl.multiple_of((owner // 2) * tall, 16)
        lanes = pl.ds(pl.multiple_of(lax.rem(owner, 2) * wide, 128), wide)
        return row, lanes, tall

    def z_got(sub, owner):
        row, lanes, tall = z_part(sub, owner)
        return got_y.at[pl.ds(pl.multiple_of(subs[sub][0] // 2 + row, 16), tall), lanes]

    def z_slot(sub, place):
        first, size = subs[sub]
        return got_z.at[place, pl.ds(first // 4, size // 4), :]

    def z_copy(sub, step):
        sem = sub * 3 + step - 1
        return remote(
            z_got(sub, lax.rem(quad + step, 4)),
            z_slot(sub, step - 1),
            z_send.at[sem],
            z_recv.at[sem],
            quad_dev(step),
        )

    def group_slot(sub, place):
        first, size = subs[sub]
        return got_group.at[place, pl.ds(first // 4, size // 4), :]

    def group_copy(sub, step):
        sem = sub * (groups - 1) + step - 1
        part = group_slot(sub, group)
        return remote(part, part, group_send.at[sem], group_recv.at[sem], group_dev(step))

    def final_part(sub):
        first, size = subs[sub]
        row, lanes, tall = z_part(sub, quad)
        row = pl.multiple_of(first + row + y * (size // 2), 16)
        return grads_out.at[pl.ds(row, tall), lanes]

    def zag_copy(sub, step):
        sem = sub * 3 + step - 1
        return remote(
            z_slot(sub, 3), final_part(sub), zag_send.at[sem], zag_recv.at[sem], quad_dev(step)
        )

    def own_copy(sub):
        return pltpu.make_async_copy(z_slot(sub, 3), final_part(sub), own_sem.at[sub])

    def yag_copy(sub):
        first, size = subs[sub]
        start = pl.multiple_of(first + y * (size // 2), 16)
        part = grads_out.at[pl.ds(start, size // 2), :]
        return remote(part, part, yag_send.at[sub], yag_recv.at[sub], y_dev)

    own_rows = []
    early = []

    def start_x(first, size):
        for sub, (row, length) in enumerate(subs):
            if first <= row < first + size:
                x_copy(sub).start()
                agenda.post(agenda.send("x", length), functools.partial(x_stage, sub))

    def own_ready(first, size):
        own_rows.append((first, first + size))
        for sub in list(early):
            if has_own(sub):
                early.remove(sub)
                agenda.post(agenda.now, functools.partial(x_stage, sub))

    def has_own(sub):
        first, size = subs[sub]
        return any(low <= first and first + size <= high for low, high in own_rows)

    def x_stage(sub):
        if not has_own(sub):
            early.append(sub)
            return
        x_copy(sub).wait_recv()
        first, size = subs[sub]
        job, at = first // width, pl.ds(first % width, size)
        total = sum_core[job, x, at, :].astype(F32) + got_x[pl.ds(first, size), :].astype(F32)
        sum_core[job, x, at, :] = total.astype(BF)
        y_copy(sub).start()
        agenda.post(agenda.send("y", size // 2), functools.partial(y_stage, sub))

    def y_stage(sub):
        y_copy(sub).wait_recv()
        job, at = y_part(sub, y)
        got = y_got(sub)
        total = sum_core[job, x, at, :].astype(F32) + got_y[got, :].astype(F32)
        got_y[got, :] = total.astype(BF)
        for step in range(1, 4):
            z_copy(sub, step).start()
        agenda.post(agenda.send("z", subs[sub][1] // 2), functools.partial(z_stage, sub))

    def z_stage(sub):
        total = z_got(sub, quad)[...].astype(F32)
        for step in range(1, 4):
            z_copy(sub, step).wait_recv()
            total = total + z_slot(sub, step - 1)[...].astype(F32)
        if groups == 1:
            publish(sub, total)
            return
        group_slot(sub, group)[...] = total.astype(BF)
        for step in range(1, groups):
            group_copy(sub, step).start()
        agenda.post(agenda.send("z", subs[sub][1] // 2), functools.partial(group_stage, sub))

    def group_stage(sub):
        for step in range(1, groups):
            group_copy(sub, step).wait_recv()
        total = group_slot(sub, 0)[...].astype(F32)
        for other in range(1, groups):
            total = total + group_slot(sub, other)[...].astype(F32)
        publish(sub, total)

    def publish(sub, total):
        z_slot(sub, 3)[...] = total.astype(BF)
        own_copy(sub).start()
        for step in range(1, 4):
            zag_copy(sub, step).start()
        agenda.post(agenda.send("z", subs[sub][1] // 2), functools.partial(zag_stage, sub))

    def zag_stage(sub):
        own_copy(sub).wait()
        for step in range(1, 4):
            zag_copy(sub, step).wait_recv()
        yag_copy(sub).start()
        agenda.send("y", subs[sub][1] // 2)

    def live_rate(which, image, row):
        index = m * images + image
        length = grids[0, index] * grids[1, index] + 2
        kept = masks[which, index].astype(F32) / KEEP_RATE
        position = lax.broadcasted_iota(jnp.int32, (TILE, 1), 0) + row
        return jnp.where(position < length, kept, 0.0)

    def over_rows(body):
        for image in range(images):

            def step(i, carry):
                row = i * TILE
                body(image, row, pl.ds(pl.multiple_of(image * slot + row, 16), TILE))
                return carry

            lax.fori_loop(0, slot // TILE, step, 0, unroll=True)

    small[...] = jnp.zeros_like(small)

    def first_norm(image, row, at):
        normed, _ = normalise(tok[at, :].astype(F32))
        entry[at, :] = (normed * gain[0:1, :] + shift[0:1, :]).astype(BF)

    def return_rows(image, row, at):
        grad = live_rate(1, image, row) * cot[at, :].astype(F32)
        ret_grad[at, :] = grad.astype(BF)
        small[7:8, :] += column_sum(grad)

    tok_copy.wait()
    over_rows(first_norm)

    lane = lax.broadcasted_iota(jnp.int32, (slot, 128), 1)
    low_lanes = lane < HEAD_DIM
    position = lax.broadcasted_iota(jnp.int32, (slot, slot), 1)
    score_scale = HEAD_DIM ** (-0.5)

    def pick(head, values):
        mask = low_lanes if head == 0 else jnp.logical_not(low_lanes)
        return jnp.where(mask, values, jnp.zeros_like(values))

    def key_length(image):
        index = m * images + image
        return grids[0, index] * grids[1, index] + 2

    def softmax(queries, keys, length):
        scores = dot(queries, keys, 1, 1) * score_scale
        scores = jnp.where(position < length, scores, -1000000000.0)
        raised = jnp.exp(scores - jnp.max(scores, axis=-1, keepdims=True))
        return raised * (1.0 / jnp.sum(raised, axis=-1, keepdims=True))

    def project(xb):
        at = pl.ds(pl.multiple_of(xb * pair, 16), pair)
        qkv_row[:, 0:cols] = qkv_all[xb * 2]
        qkv_row[:, cols:pair] = qkv_all[xb * 2 + 1]
        for j in range(3):
            value = dot(entry[...], wqkv[j, at, :], 1, 1)
            if j != 1:
                row = j // 2
                value = value + qkv_row[row : row + 1, :]
            value = value.astype(BF)
            for pack in range(packs):
                heads[j, xb * packs + pack] = value[:, pack * 128 : (pack + 1) * 128]

    def attend(xb, image):
        def step(i, carry):
            pack = xb * packs + i
            at = pl.ds(pl.multiple_of(image * slot, 16), slot)
            queries, keys, values = (heads[j, pack, at, :] for j in range(3))
            length = key_length(image)
            total = jnp.zeros((slot, 128), F32)
            for head in range(2):
                probs = softmax(queries, pick(head, keys), length).astype(BF)
                total = total + dot(probs, pick(head, values), 1, 0)
            mixed[pack, at, :] = total.astype(BF)
            return carry

        lax.fori_loop(0, packs, step, 0)

    agenda.spend(1.5)
    for p in pieces[2:]:
        ag_copy(0, p).start()
        ag_local(p).start()
    bias_own(1).wait()
    bias_copy(5).wait_recv()
    near_ready("qk", "v")
    project(x)
    agenda.spend(2.5)
    for image in range(images):
        attend(x, image)
        agenda.spend(2.5)
        if image == 0:
            cot_copy.wait()
            over_rows(return_rows)
            agenda.spend(1.0)
    bias_own(0).wait()
    for i in range(5):
        bias_copy(i).wait_recv()
    far_ready("qk", "v")
    project(1 - x)
    agenda.spend(2.5)
    for image in range(images):
        attend(1 - x, image)
        agenda.spend(2.5)

    near_ready("p")
    far_ready("p")
    all_mixed = jnp.concatenate([mixed[pack] for pack in range(2 * packs)], axis=1)
    work[...] = dot(all_mixed, wproj[...], 1, 0)

    def second_norm(image, row, at):
        value = tok[at, :].astype(F32) + live_rate(0, image, row) * (work[at, :] + pbias[0:1, :])
        middle[at, :] = value
        normed, _ = normalise(value)
        entry_two[at, :] = (normed * gain[1:2, :] + shift[1:2, :]).astype(BF)

    over_rows(second_norm)
    agenda.spend(2.7)

    def emit(job, xb, slot_, mine, first, size, value):
        kept, far = mine
        at = pl.ds(first, size)
        if not kept:
            give[job % 2, xb, at, :] = value.astype(BF)
            core_start(job, xb, slot_, first, size)
            return
        core_copy(job, xb, slot_, first, size).wait_recv()
        total = value + sum_core[job, xb, at, :].astype(F32)
        sum_core[job, xb, at, :] = total.astype(BF)
        if far:
            start_x(job * width + first, size)
        else:
            own_ready(job * width + first, size)

    def feed_first(block, xb, mine, part):
        first, size = part * wide, wide
        lanes = slice(first, first + size)
        hidden = dot(entry_two[...], wup[block, :, lanes], 1, 0) + up_all[block, :, lanes]
        share = 0.5 * (1.0 + lax.erf(hidden * 0.7071067811865476))
        density = jnp.exp(-0.5 * hidden * hidden) * 0.3989422804014327
        active = (hidden * share).astype(BF)
        act[block, :, lanes] = active
        slope[block, :, lanes] = (share + hidden * density).astype(BF)
        slot_ = (0 if mine[1] else 2) + part
        emit(0, xb, slot_, mine, first, size, dot(active, ret_grad[...], 0, 0))
        agenda.spend(1.9)

    def feed_back(block, xb, mine, first):
        grad = dot(ret_grad[...], wdn[block], 1, 1) * slope[block].astype(F32)
        grad = grad.astype(BF)
        slope[block] = grad
        small[pl.ds(8 + block, 1), :] = column_sum(grad.astype(F32))
        slot_ = 4 if mine[1] else 5
        emit(1, xb, slot_, mine, 0, width, dot(entry_two[...], slope[block], 0, 0))
        value = dot(slope[block], wup[block], 1, 1)
        if first:
            tokens_grad[...] = value
        else:
            tokens_grad[...] += value
        agenda.spend(4.0)

    order = (
        (far_peer, 1 - x, (False, True)),
        (far_block, 1 - x, (True, True)),
        (peer_block, x, (False, False)),
        (own_block, x, (True, False)),
    )
    near_ready("u0", "u1")
    far_ready("u0", "u1")
    for part in range(2):
        for item in order:
            feed_first(*item, part)
    near_ready("d")
    far_ready("d")
    for i, item in enumerate(order):
        feed_back(*item, i == 0)

    def norm_back(values, grad, r):
        normed, scale = normalise(values)
        small[r : r + 1, :] += column_sum(grad * normed)
        small[2 + r : 3 + r, :] += column_sum(grad)
        scaled = grad * gain[r : r + 1, :]
        mean_one = jnp.mean(scaled, axis=-1, keepdims=True)
        mean_two = jnp.mean(scaled * normed, axis=-1, keepdims=True)
        return scale * (scaled - mean_one - normed * mean_two)

    def second_back(image, row, at):
        grad = cot[at, :].astype(F32) + norm_back(middle[at, :], tokens_grad[at, :], 1)
        tokens_grad[at, :] = grad
        scaled = live_rate(0, image, row) * grad
        mixer_grad[at, :] = scaled.astype(BF)
        small[6:7, :] += column_sum(scaled)

    mixer_grad = entry_two
    over_rows(second_back)
    agenda.spend(2.2)

    for copy in core_started[:4]:
        core_copy(*copy).wait_send()
    waiting = []

    def emit_narrow(s, xb, far, value):
        part = pl.ds(s * cols, cols)
        place = len(waiting) % 2
        low, high = value[0:cols], value[cols:pair]
        give[0, xb, part, :] = jnp.where(c == 0, high, low).astype(BF)
        keep[place] = jnp.where(c == 0, low, high)
        core_start(2, xb, 6 + s * 2 + (0 if far else 1), s * cols, cols)
        waiting.append((s, xb, far, place))

    def settle(left):
        while len(waiting) - settled[0] > left:
            s, xb, far, place = waiting[settled[0]]
            settled[0] += 1
            part = pl.ds(s * cols, cols)
            core_copy(2, xb, 6 + s * 2 + (0 if far else 1), s * cols, cols).wait_recv()
            total = keep[place] + sum_core[2, xb, part, :].astype(F32)
            sum_core[2, xb, part, :] = total.astype(BF)
            if far:
                start_x(2 * width + s * cols, cols)
            else:
                own_ready(2 * width + s * cols, cols)

    settled = [0]

    def side(ref, xb):
        return jnp.concatenate([ref[xb * packs + pack] for pack in range(packs)], axis=1)

    def attend_back(xb, image):
        def step(i, carry):
            pack = xb * packs + i
            at = pl.ds(pl.multiple_of(image * slot, 16), slot)
            queries, keys, values = (heads[j, pack, at, :] for j in range(3))
            grads = mixed_grad[pack, at, :]
            length = key_length(image)
            query_grad = jnp.zeros((slot, 128), F32)
            key_grad = jnp.zeros((slot, 128), F32)
            value_grad = jnp.zeros((slot, 128), F32)
            for head in range(2):
                head_keys = pick(head, keys)
                probs = softmax(queries, head_keys, length)
                probs_grad = dot(grads, pick(head, values), 1, 1)
                inner = jnp.sum(probs * probs_grad, axis=-1, keepdims=True)
                score_grad = (probs * (probs_grad - inner)).astype(BF)
                query_grad = query_grad + dot(score_grad, head_keys, 1, 0)
                key_grad = key_grad + dot(score_grad, pick(head, queries), 0, 0)
                value_grad = value_grad + dot(probs.astype(BF), pick(head, grads), 0, 0)
            heads[0, pack, at, :] = (query_grad * score_scale).astype(BF)
            heads[1, pack, at, :] = (key_grad * score_scale).astype(BF)
            heads[2, pack, at, :] = value_grad.astype(BF)
            return carry

        lax.fori_loop(0, packs, step, 0)

    def qkv_back(xb, far):
        lanes = pl.ds(pl.multiple_of(xb * pair, 128), pair)
        for j in range(3):
            grad = side(heads.at[j], xb)
            emit_narrow(1 + j, xb, far, dot(grad, entry[...], 0, 0))
            settle(1)
            if j != 1:
                row = 4 if j == 0 else 5
                small[row : row + 1, lanes] = column_sum(grad.astype(F32))
            agenda.spend(1.2)

    value = dot(mixer_grad[...], wproj[...], 1, 1).astype(BF)
    for pack in range(2 * packs):
        mixed_grad[pack] = value[:, pack * 128 : (pack + 1) * 128]
    for xb, far in ((1 - x, True), (x, False)):
        emit_narrow(0, xb, far, dot(side(mixed, xb), mixer_grad[...], 0, 0))
    agenda.spend(3.5)
    settle(0)
    for image in range(images):
        attend_back(1 - x, image)
        agenda.spend(3.8)
    qkv_back(1 - x, True)
    settle(0)
    for image in range(images):
        attend_back(x, image)
        agenda.spend(3.8)
    qkv_back(x, False)
    settle(0)

    for j in range(3):
        grad = jnp.concatenate([heads[j, pack] for pack in range(2 * packs)], axis=1)
        part = dot(grad, wqkv[j], 1, 0)
        work[...] = part if j == 0 else work[...] + part
        agenda.spend(1.4)

    def first_back(image, row, at):
        tokens_grad[at, :] += norm_back(tok[at, :].astype(F32), work[at, :], 0)

    over_rows(first_back)
    agenda.spend(2.2)

    def small_copy(stage, device):
        return remote(
            small_got.at[stage],
            small_from.at[stage],
            small_send.at[stage],
            small_recv.at[stage],
            device,
        )

    small_devices = (core_dev, x_dev, y_dev)

    def small_quad(step):
        part = small_got.at[3 + quad]
        sem = 2 + step
        return remote(part, part, small_send.at[sem], small_recv.at[sem], quad_dev(step))

    def small_group(step):
        part = small_got.at[7 + group]
        sem = 5 + step
        return remote(part, part, small_send.at[sem], small_recv.at[sem], group_dev(step))

    def small_stage(stage):
        small_copy(stage, small_devices[stage]).wait_recv()
        total = small_got[stage] + small_from[stage]
        if stage < 2:
            small_got[stage + 1] = total
            small_copy(stage + 1, small_devices[stage + 1]).start()
            agenda.post(agenda.now + 6.0, functools.partial(small_stage, stage + 1))
        else:
            small_got[3 + quad] = total
            for step in range(1, 4):
                small_quad(step).start()
            agenda.post(agenda.now + 6.0, small_last)

    def small_last():
        for step in range(1, 4):
            small_quad(step).wait_recv()
        total = small_got[3]
        for other in range(1, 4):
            total = total + small_got[3 + other]
        if groups > 1:
            small_got[7 + group] = total
            for step in range(1, groups):
                small_group(step).start()
            for step in range(1, groups):
                small_group(step).wait_recv()
            total = small_got[7]
            for other in range(1, groups):
                total = total + small_got[7 + other]
        small[...] = total

    small_got[0] = small[...]
    small_copy(0, core_dev).start()
    agenda.post(agenda.now + HOP, functools.partial(small_stage, 0))
    for i, (block, _, _) in enumerate(order):
        part = dot(act[block], wdn[block], 1, 0)
        work[...] = part if i == 0 else work[...] + part
        agenda.spend(1.4)

    def finish(image, row, at):
        value = middle[at, :] + live_rate(1, image, row) * (work[at, :] + pbias[1:2, :])
        block_out[at, :] = value.astype(BF)

    over_rows(finish)
    agenda.spend(1.2)
    agenda.until(lambda: not agenda.queue)
    small_out[0:8, :] = small[0:8, :]
    qkv_row[...] = small[4:6, pl.ds(pl.multiple_of(x * pair, 128), pair)]
    small_out[8:10, 0:cols] = jnp.where(c == 0, qkv_row[:, 0:cols], qkv_row[:, cols:pair])
    small_out[10:11, :] = small[pl.ds(8 + m, 1), :]

    for sub in range(len(subs)):
        yag_copy(sub).wait_recv()
    for i in range(6):
        bias_copy(i).wait_send()
    for p in pieces:
        for route in range(10):
            ag_copy(route, p).wait_send()
    for copy in core_started[4:]:
        core_copy(*copy).wait_send()
    for sub in range(len(subs)):
        x_copy(sub).wait_send()
        y_copy(sub).wait_send()
        yag_copy(sub).wait_send()
        for step in range(1, 4):
            z_copy(sub, step).wait_send()
            zag_copy(sub, step).wait_send()
        for step in range(1, groups):
            group_copy(sub, step).wait_send()
    for stage, device in enumerate(small_devices):
        small_copy(stage, device).wait_send()
    for step in range(1, 4):
        small_quad(step).wait_send()
    for step in range(1, groups):
        small_group(step).wait_send()


def finish_kernel(
    grads,
    tokens_part,
    block_part,
    small,
    block_out,
    tokens_grad,
    gain_grad,
    shift_grad,
    qkv_grad,
    qkv_bias_grad,
    proj_grad,
    proj_bias_grad,
    up_grad,
    up_bias_grad,
    down_grad,
):
    block_out[...] = block_part[...]
    tokens_grad[...] = tokens_part[...]
    down_grad[...] = grads[0:SUBS].astype(F32)
    up_grad[...] = grads[SUBS : 2 * SUBS].astype(F32)
    proj_grad[...] = grads[2 * SUBS].astype(F32)
    qkv_grad[...] = grads[2 * SUBS + 1 :].astype(F32)

    @pl.when(pl.program_id(0) == 0)
    def _():
        gain_grad[...] = small[0:2, :]
        shift_grad[...] = small[2:4, :]
        proj_bias_grad[...] = small[6:8, :]
        qkv_bias_grad[...] = small[8:10, 0 : qkv_bias_grad.shape[1]]
        up_bias_grad[...] = small[10:11, :].reshape(up_bias_grad.shape)


def local(
    tokens,
    norm_gain,
    norm_shift,
    qkv_weight,
    qkv_bias,
    proj_weight,
    proj_bias,
    up_weight,
    up_bias,
    down_weight,
    patch_grids,
    keep_masks,
    out_cotangent,
):
    rows, width = tokens.shape
    mp = lax.axis_size("mp")
    nz = lax.axis_size("dp") // 2
    images = patch_grids.shape[0] // mp
    slot = rows // images
    cols = qkv_weight.shape[2]
    pair = 2 * cols
    packs = pair // 128
    subs = len(sub_list(width, cols))
    groups = nz // 4
    cross = max(1, subs * (groups - 1))
    qkv_rows = jnp.transpose(qkv_weight, (0, 2, 1))
    vmem = pl.BlockSpec(memory_space=pltpu.VMEM)
    smem = pl.BlockSpec(memory_space=pltpu.SMEM)
    hbm = pl.BlockSpec(memory_space=pl.ANY)
    dma = pltpu.SemaphoreType.DMA
    scratch = [
        pltpu.VMEM((3, width, width), BF),
        pltpu.VMEM((width, width), BF),
        pltpu.VMEM((4, width, width), BF),
        pltpu.VMEM((4, width, width), BF),
        pltpu.VMEM((rows, width), BF),
        pltpu.VMEM((rows, width), BF),
        pltpu.VMEM((4, 1, width), F32),
        pltpu.VMEM((4, 2, cols), F32),
        pltpu.VMEM((1, width), F32),
        pltpu.VMEM((2, pair), F32),
        pltpu.VMEM((2, cols, width), F32),
        pltpu.VMEM((rows, width), BF),
        pltpu.VMEM((rows, width), BF),
        pltpu.VMEM((rows, width), BF),
        pltpu.VMEM((3, 2 * packs, rows, 128), BF),
        pltpu.VMEM((2 * packs, rows, 128), BF),
        pltpu.VMEM((2 * packs, rows, 128), BF),
        pltpu.VMEM((4, rows, width), BF),
        pltpu.VMEM((4, rows, width), BF),
        pltpu.VMEM((rows, width), F32),
        pltpu.VMEM((rows, width), F32),
        pltpu.VMEM((2, 2, width, width), BF),
        pltpu.VMEM((JOBS, 2, width, width), BF),
        pltpu.VMEM((JOBS * width, width), BF),
        pltpu.VMEM((JOBS * width // 2, width), BF),
        pltpu.VMEM((4, JOBS * width // 4, width // 2), BF),
        pltpu.VMEM((groups, JOBS * width // 4 if groups > 1 else 16, width // 2), BF),
        pltpu.VMEM((16, width), F32),
        pltpu.VMEM((7 + groups, 16, width), F32),
        pltpu.VMEM((3, 16, width), F32),
        dma((12,)),
        dma((10, 6)),
        dma((10, 6)),
        dma((6,)),
        dma((6,)),
        dma((14,)),
        dma((14,)),
        dma((subs,)),
        dma((subs,)),
        dma((subs,)),
        dma((subs,)),
        dma((3 * subs,)),
        dma((3 * subs,)),
        dma((cross,)),
        dma((cross,)),
        dma((3 * subs,)),
        dma((3 * subs,)),
        dma((subs,)),
        dma((subs,)),
        dma((subs,)),
        dma((5 + groups,)),
        dma((5 + groups,)),
    ]
    grads, tokens_grad, block_out, small = pl.pallas_call(
        functools.partial(layer_kernel, (nz, images, slot, width, cols)),
        out_shape=(
            jax.ShapeDtypeStruct((JOBS * width, width), BF),
            jax.ShapeDtypeStruct((rows, width), F32),
            jax.ShapeDtypeStruct((rows, width), BF),
            jax.ShapeDtypeStruct((16, width), F32),
        ),
        in_specs=[hbm] * 2 + [vmem] * 3 + [smem] * 2 + [vmem] * 2 + [hbm] * 4,
        out_specs=(hbm, vmem, vmem, vmem),
        scratch_shapes=scratch,
        compiler_params=pltpu.CompilerParams(
            collective_id=0, has_side_effects=True, vmem_limit_bytes=64 * 2**20 - 2**17
        ),
    )(
        tokens,
        out_cotangent,
        norm_gain,
        norm_shift,
        proj_bias,
        patch_grids.T,
        keep_masks.T,
        up_bias,
        qkv_bias,
        qkv_rows,
        proj_weight,
        up_weight,
        down_weight,
    )
    steps = width // 128
    block = functools.partial(pl.BlockSpec, memory_space=pltpu.VMEM)
    out = pl.pallas_call(
        finish_kernel,
        grid=(steps,),
        out_shape=(
            jax.ShapeDtypeStruct((rows, width), BF),
            jax.ShapeDtypeStruct((rows, width), F32),
            jax.ShapeDtypeStruct((2, width), F32),
            jax.ShapeDtypeStruct((2, width), F32),
            jax.ShapeDtypeStruct((3, cols, width), F32),
            jax.ShapeDtypeStruct((2, cols), F32),
            jax.ShapeDtypeStruct((cols, width), F32),
            jax.ShapeDtypeStruct((2, width), F32),
            jax.ShapeDtypeStruct((SUBS, cols, width), F32),
            jax.ShapeDtypeStruct((width,), F32),
            jax.ShapeDtypeStruct((SUBS, cols, width), F32),
        ),
        in_specs=[
            block((JOBS * SUBS, cols // steps, width), lambda i: (0, i, 0)),
            block((rows // steps, width), lambda i: (i, 0)),
            block((rows // steps, width), lambda i: (i, 0)),
            block((16, width), lambda i: (0, 0)),
        ],
        out_specs=(
            block((rows // steps, width), lambda i: (i, 0)),
            block((rows // steps, width), lambda i: (i, 0)),
            block((2, width), lambda i: (0, 0)),
            block((2, width), lambda i: (0, 0)),
            block((3, cols // steps, width), lambda i: (0, i, 0)),
            block((2, cols), lambda i: (0, 0)),
            block((cols // steps, width), lambda i: (i, 0)),
            block((2, width), lambda i: (0, 0)),
            block((SUBS, cols // steps, width), lambda i: (0, i, 0)),
            block((width,), lambda i: (0,)),
            block((SUBS, cols // steps, width), lambda i: (0, i, 0)),
        ),
        compiler_params=pltpu.CompilerParams(vmem_limit_bytes=60 * 2**20),
    )(grads.reshape(JOBS * SUBS, cols, width), tokens_grad, block_out, small)
    out = list(out)
    out[4] = jnp.transpose(out[4], (0, 2, 1))
    out[8] = out[8].reshape(up_weight.shape)
    out[10] = out[10].reshape(down_weight.shape)
    return tuple(out)


def solution(mesh):
    return jax.shard_map(
        local,
        mesh=mesh,
        in_specs=(
            P(("dp", "mp"), None),
            P(),
            P(),
            P(None, None, "mp"),
            P(None, "mp"),
            P("mp", None),
            P(),
            P(None, "mp"),
            P("mp"),
            P("mp", None),
            P("dp", None),
            P("dp", None),
            P(("dp", "mp"), None),
        ),
        out_specs=(
            P(("dp", "mp"), None),
            P(("dp", "mp"), None),
            P(),
            P(),
            P(None, None, "mp"),
            P(None, "mp"),
            P("mp", None),
            P(),
            P(None, "mp"),
            P("mp"),
            P("mp", None),
        ),
        check_vma=False,
    )
```

```python
import functools
import heapq

import jax
import jax.numpy as jnp
from jax import lax
from jax.experimental import pallas as pl
from jax.experimental.pallas import tpu as pltpu
from jax.sharding import PartitionSpec as P

HEAD_DIM = 64
EPSILON = 1e-06
KEEP_RATE = 0.9
MESH = pl.DeviceIdType.MESH
BF = jnp.bfloat16
F32 = jnp.float32
TILE = 96
JOBS = 3
SUBS = 4
LINK_ROW = 0.033
HOP = 2.5
HANDLE = 0.4
LATE = 4
LATE_Z = 0


def dot(left, right, left_dim, right_dim):
    return lax.dot_general(
        left, right, (((left_dim,), (right_dim,)), ((), ())), preferred_element_type=F32
    )


def normalise(rows):
    centred = rows - jnp.mean(rows, axis=-1, keepdims=True)
    spread = jnp.mean(centred * centred, axis=-1, keepdims=True)
    scale = lax.rsqrt(spread + EPSILON)
    return centred * scale, scale


def sub_list(width, cols):
    parts = [(k * cols, cols) for k in range(JOBS * SUBS)]
    third = cols // 3
    first = [(k * third, third) for k in range(3)]
    last = [(parts[-1][0] + k * third, third) for k in range(3)]
    return first + parts[1:-1] + last


class Agenda:
    def __init__(self):
        self.now = 0.0
        self.free = {}
        self.queue = []
        self.number = 0

    def send(self, link, rows):
        begin = max(self.now, self.free.get(link, 0.0))
        self.free[link] = begin + rows * LINK_ROW
        return self.free[link] + HOP

    def post(self, ready, action):
        self.number += 1
        heapq.heappush(self.queue, (ready, self.number, action))

    def handle(self):
        ready, _, action = heapq.heappop(self.queue)
        self.now = max(self.now, ready) + HANDLE
        action()

    def spend(self, time):
        self.now += time
        while self.queue and self.queue[0][0] <= self.now:
            self.handle()

    def until(self, reached):
        while not reached():
            self.handle()


def column_sum(rows):
    return jnp.sum(rows, axis=0, keepdims=True)


def layer_kernel(
    sizes,
    tok_in,
    cot_in,
    gain,
    shift,
    pbias,
    grids,
    masks,
    up_bias,
    qkv_bias,
    wqkv_in,
    wproj_in,
    wup_in,
    wdn_in,
    grads_out,
    tokens_grad,
    block_out,
    small_out,
    wqkv,
    wproj,
    wup,
    wdn,
    tok,
    cot,
    up_all,
    qkv_all,
    up_own,
    qkv_row,
    keep,
    entry,
    entry_two,
    ret_grad,
    heads,
    mixed,
    mixed_grad,
    act,
    slope,
    work,
    middle,
    give,
    sum_core,
    got_x,
    got_y,
    got_z,
    got_group,
    small,
    small_got,
    small_part,
    local_sem,
    ag_send,
    ag_recv,
    bias_send,
    bias_recv,
    core_send,
    core_recv,
    x_send,
    x_recv,
    y_send,
    y_recv,
    z_send,
    z_recv,
    group_send,
    group_recv,
    zag_send,
    zag_recv,
    yag_send,
    yag_recv,
    own_sem,
    small_send,
    small_recv,
):
    nz, images, slot, width, cols = sizes
    rows = images * slot
    pair = 2 * cols
    half = cols // 2
    packs = pair // 128
    groups = nz // 4
    subs = sub_list(width, cols)

    d = lax.axis_index("dp")
    m = lax.axis_index("mp")
    y = lax.rem(d, 2)
    z = d // 2
    x = m // 2
    c = lax.rem(m, 2)
    core_dev = (d, x * 2 + 1 - c)
    x_dev = (d, (1 - x) * 2 + c)
    diag_dev = (d, (1 - x) * 2 + 1 - c)
    y_dev = (z * 2 + 1 - y, m)
    group, quad = z // 4, lax.rem(z, 4)

    def z_dev(other):
        return (other * 2 + y, m)

    def quad_dev(step):
        return z_dev(group * 4 + lax.rem(quad + step, 4))

    def group_dev(step):
        return z_dev(lax.rem(group + step, groups) * 4 + quad)

    def remote(src, dst, send, recv, device):
        return pltpu.make_async_remote_copy(
            src_ref=src,
            dst_ref=dst,
            send_sem=send,
            recv_sem=recv,
            device_id=device,
            device_id_type=MESH,
        )

    tok_copy = pltpu.make_async_copy(tok_in, tok, local_sem.at[8])
    cot_copy = pltpu.make_async_copy(cot_in, cot, local_sem.at[9])
    tok_copy.start()
    cot_copy.start()
    barrier = pltpu.get_barrier_semaphore()
    greeted = [core_dev, x_dev, diag_dev, y_dev]
    greeted += [quad_dev(k) for k in range(1, 4)]
    greeted += [group_dev(k) for k in range(1, groups)]
    for device in greeted:
        pl.semaphore_signal(barrier, inc=1, device_id=device, device_id_type=MESH)
    pl.semaphore_wait(barrier, len(greeted))

    own_block = m
    peer_block = x * 2 + 1 - c
    far_block = (1 - x) * 2 + c
    far_peer = (1 - x) * 2 + 1 - c

    pieces = ("qk", "v", "p", "u0", "u1", "d")
    near_z = z + 1 - 2 * lax.rem(z, 2)
    side_z = lax.rem(z, 2)
    quarters = (y * 2 + side_z, (1 - y) * 2 + side_z, y * 2 + 1 - side_z, 3 - y * 2 - side_z)
    wide = width // 2

    def rows_of(piece, part):
        size = {"u0": width // 2, "u1": width // 2, "d": width}.get(piece, cols)
        if part is None:
            return 0, size
        return quarters[part] * (size // 4), size // 4

    def view(piece, block, part, lanes=None):
        start, size = rows_of(piece, part)
        lanes = pl.ds(0, width) if lanes is None else pl.ds(lanes * wide, wide)
        if piece in ("qk", "v", "p"):
            at = pl.ds(pl.multiple_of(block * cols + start, 16), size)
            if piece == "p":
                return wproj.at[at, lanes]
            return wqkv.at[pl.ds(0, 2) if piece == "qk" else pl.ds(2, 1), at, lanes]
        first = width // 2 if piece == "u1" else 0
        at = pl.ds(pl.multiple_of(first + start, 16), size)
        return (wdn if piece == "d" else wup).at[block, at, lanes]

    def view_in(piece, part):
        start, size = rows_of(piece, part)
        first = width // 2 if piece == "u1" else 0
        at = pl.ds(first + start if part is None else pl.multiple_of(first + start, 16), size)
        if piece in ("qk", "v"):
            return wqkv_in.at[pl.ds(0, 2) if piece == "qk" else pl.ds(2, 1), at, :]
        return {"p": wproj_in, "d": wdn_in}.get(piece, wup_in).at[at, :]

    def ag_local(p):
        i = pieces.index(p)
        return pltpu.make_async_copy(view_in(p, None), view(p, own_block, None), local_sem.at[i])

    def ag_copy(route, p):
        i = pieces.index(p)
        send, recv = ag_send.at[route, i], ag_recv.at[route, i]
        if route == 0:
            return remote(view_in(p, None), view(p, own_block, None), send, recv, core_dev)
        if route == 1:
            return remote(view_in(p, 0), view(p, own_block, 0), send, recv, x_dev)
        if route == 2:
            part, lanes, device = 0, None, y_dev
        elif route == 3:
            part, lanes, device = 0, None, z_dev(near_z)
        elif route == 4:
            part, lanes, device = 2, 0, y_dev
        elif route == 5:
            part, lanes, device = 1, 1, z_dev(near_z)
        else:
            part, lanes, device = route - 6, None, core_dev
        source = view(p, far_block, part, lanes)
        return remote(source, source, send, recv, device)

    def quarter_rows(p):
        return rows_of(p, None)[1] // 4 * (2 if p == "qk" else 1)

    def admit(*names):
        for p in names:
            agenda.post(max(agenda.now, x_ready[p]), functools.partial(from_x, p))

    def from_x(p):
        ag_copy(1, p).wait_recv()
        for route in (2, 3, 6):
            ag_copy(route, p).start()
        ready = max(agenda.send("y", quarter_rows(p)), agenda.send("z", quarter_rows(p)))
        agenda.post(ready, functools.partial(from_yz, p))

    def from_yz(p):
        ag_copy(2, p).wait_recv()
        ag_copy(5, p).start()
        ag_copy(7, p).start()
        ag_copy(3, p).wait_recv()
        ag_copy(4, p).start()
        ag_copy(8, p).start()
        rows_ = quarter_rows(p) // 2
        ready = max(agenda.send("y", rows_), agenda.send("z", rows_))
        agenda.post(ready, functools.partial(from_both, p))
        if p == "v":
            admit("p", "u0", "u1")
        elif p == "u1":
            admit("d")

    def from_both(p):
        ag_copy(4, p).wait_recv()
        ag_copy(5, p).wait_recv()
        ag_copy(9, p).start()
        gathered.add(p)

    def bias_copy(i):
        source, dest = (up_own, up_all) if i % 2 == 0 else (qkv_bias, qkv_all)
        device = (x_dev, diag_dev, core_dev)[i // 2]
        return remote(source, dest.at[m], bias_send.at[i], bias_recv.at[i], device)

    def bias_own(i):
        source, dest = (up_own, up_all) if i % 2 == 0 else (qkv_bias, qkv_all)
        return pltpu.make_async_copy(source, dest.at[m], local_sem.at[10 + i])

    up_own[...] = up_bias[...].reshape(1, width)
    for i in range(4):
        bias_copy(i).start()
    agenda = Agenda()
    gathered = set()
    x_ready = {}
    for p in pieces:
        ag_copy(1, p).start()
        x_ready[p] = agenda.send("x", quarter_rows(p))
    admit("qk", "v")
    for p in pieces[:2]:
        ag_copy(0, p).start()
        ag_local(p).start()
    for i in range(2):
        bias_copy(4 + i).start()
        bias_own(i).start()

    def near_ready(*names):
        for p in names:
            ag_local(p).wait()
            ag_copy(0, p).wait_recv()

    def far_ready(*names):
        for p in names:
            agenda.until(lambda: p in gathered)
            for route in (6, 7, 8, 9):
                ag_copy(route, p).wait_recv()

    core_started = []

    def core_copy(job, xb, slot_, first, size):
        at = pl.ds(first, size)
        return remote(
            give.at[job % 2, xb, at, :],
            sum_core.at[job, xb, at, :],
            core_send.at[slot_],
            core_recv.at[slot_],
            core_dev,
        )

    def core_start(*copy):
        core_started.append(copy)
        core_copy(*copy).start()

    def x_copy(sub):
        first, size = subs[sub]
        source = sum_core.at[first // width, 1 - x, pl.ds(first % width, size), :]
        return remote(
            source, got_x.at[pl.ds(first, size), :], x_send.at[sub], x_recv.at[sub], x_dev
        )

    def y_part(sub, which):
        first, size = subs[sub]
        start = pl.multiple_of(first % width + which * (size // 2), 16)
        return first // width, pl.ds(start, size // 2)

    def y_got(sub):
        first, size = subs[sub]
        return pl.ds(first // 2, size // 2)

    def y_copy(sub):
        job, at = y_part(sub, 1 - y)
        return remote(
            sum_core.at[job, x, at, :],
            got_y.at[y_got(sub), :],
            y_send.at[sub],
            y_recv.at[sub],
            y_dev,
        )

    def z_part(sub, owner):
        tall = subs[sub][1] // 4
        row = pl.multiple_of((owner // 2) * tall, 16)
        lanes = pl.ds(pl.multiple_of(lax.rem(owner, 2) * wide, 128), wide)
        return row, lanes, tall

    def z_got(sub, owner):
        row, lanes, tall = z_part(sub, owner)
        return got_y.at[pl.ds(pl.multiple_of(subs[sub][0] // 2 + row, 16), tall), lanes]

    def z_slot(sub, place):
        first, size = subs[sub]
        return got_z.at[place, pl.ds(first // 4, size // 4), :]

    def z_copy(sub, step):
        sem = sub * 3 + step - 1
        return remote(
            z_got(sub, lax.rem(quad + step, 4)),
            z_slot(sub, step - 1),
            z_send.at[sem],
            z_recv.at[sem],
            quad_dev(step),
        )

    def group_slot(sub, place):
        first, size = subs[sub]
        return got_group.at[place, pl.ds(first // 4, size // 4), :]

    def group_copy(sub, step):
        sem = sub * (groups - 1) + step - 1
        part = group_slot(sub, group)
        return remote(part, part, group_send.at[sem], group_recv.at[sem], group_dev(step))

    def final_part(sub):
        first, size = subs[sub]
        row, lanes, tall = z_part(sub, quad)
        row = pl.multiple_of(first + row + y * (size // 2), 16)
        return grads_out.at[pl.ds(row, tall), lanes]

    def zag_copy(sub, step):
        sem = sub * 3 + step - 1
        return remote(
            z_slot(sub, 3), final_part(sub), zag_send.at[sem], zag_recv.at[sem], quad_dev(step)
        )

    def own_copy(sub):
        return pltpu.make_async_copy(z_slot(sub, 3), final_part(sub), own_sem.at[sub])

    def yag_copy(sub):
        first, size = subs[sub]
        start = pl.multiple_of(first + y * (size // 2), 16)
        part = grads_out.at[pl.ds(start, size // 2), :]
        return remote(part, part, yag_send.at[sub], yag_recv.at[sub], y_dev)

    own_rows = []
    early = []
    summed_y = []
    held = []
    summed_z = []
    held_z = []

    def start_x(first, size):
        for sub, (row, length) in enumerate(subs):
            if first <= row < first + size:
                x_copy(sub).start()
                agenda.post(agenda.send("x", length), functools.partial(x_stage, sub))

    def own_ready(first, size):
        own_rows.append((first, first + size))
        for sub in list(early):
            if has_own(sub):
                early.remove(sub)
                agenda.post(agenda.now, functools.partial(x_stage, sub))

    def has_own(sub):
        first, size = subs[sub]
        return any(low <= first and first + size <= high for low, high in own_rows)

    def x_stage(sub):
        if not has_own(sub):
            early.append(sub)
            return
        x_copy(sub).wait_recv()
        first, size = subs[sub]
        job, at = first // width, pl.ds(first % width, size)
        total = sum_core[job, x, at, :].astype(F32) + got_x[pl.ds(first, size), :].astype(F32)
        sum_core[job, x, at, :] = total.astype(BF)
        y_copy(sub).start()
        agenda.post(agenda.send("y", size // 2), functools.partial(y_stage, sub))
        summed_y.append(sub)
        if len(summed_y) == len(subs):
            hand_out()

    def y_stage(sub):
        y_copy(sub).wait_recv()
        job, at = y_part(sub, y)
        got = y_got(sub)
        total = sum_core[job, x, at, :].astype(F32) + got_y[got, :].astype(F32)
        got_y[got, :] = total.astype(BF)
        for step in range(1, 4):
            z_copy(sub, step).start()
        agenda.post(agenda.send("z", subs[sub][1] // 2), functools.partial(z_stage, sub))
        summed_z.append(sub)
        if len(summed_z) == len(subs):
            share()

    def z_stage(sub):
        total = z_got(sub, quad)[...].astype(F32)
        for step in range(1, 4):
            z_copy(sub, step).wait_recv()
            total = total + z_slot(sub, step - 1)[...].astype(F32)
        if groups == 1:
            publish(sub, total)
            return
        group_slot(sub, group)[...] = total.astype(BF)
        for step in range(1, groups):
            group_copy(sub, step).start()
        agenda.post(agenda.send("z", subs[sub][1] // 2), functools.partial(group_stage, sub))

    def group_stage(sub):
        for step in range(1, groups):
            group_copy(sub, step).wait_recv()
        total = group_slot(sub, 0)[...].astype(F32)
        for other in range(1, groups):
            total = total + group_slot(sub, other)[...].astype(F32)
        publish(sub, total)

    def publish(sub, total):
        z_slot(sub, 3)[...] = total.astype(BF)
        own_copy(sub).start()
        held_z.append(sub)
        share()

    def share():
        if len(subs) - LATE_Z <= len(summed_z) < len(subs):
            return
        for sub in held_z:
            for step in range(1, 4):
                zag_copy(sub, step).start()
            agenda.post(agenda.send("z", subs[sub][1] // 2), functools.partial(zag_stage, sub))
        held_z.clear()

    def zag_stage(sub):
        own_copy(sub).wait()
        for step in range(1, 4):
            zag_copy(sub, step).wait_recv()
        held.append(sub)
        hand_out()

    def hand_out():
        if len(subs) - LATE <= len(summed_y) < len(subs):
            return
        for sub in held:
            yag_copy(sub).start()
            agenda.send("y", subs[sub][1] // 2)
        held.clear()

    def live_rate(which, image, row):
        index = m * images + image
        length = grids[0, index] * grids[1, index] + 2
        kept = masks[which, index].astype(F32) / KEEP_RATE
        position = lax.broadcasted_iota(jnp.int32, (TILE, 1), 0) + row
        return jnp.where(position < length, kept, 0.0)

    def over_rows(body):
        for image in range(images):

            def step(i, carry):
                row = i * TILE
                body(image, row, pl.ds(pl.multiple_of(image * slot + row, 16), TILE))
                return carry

            lax.fori_loop(0, slot // TILE, step, 0, unroll=True)

    small[...] = jnp.zeros_like(small)

    def first_norm(image, row, at):
        normed, _ = normalise(tok[at, :].astype(F32))
        entry[at, :] = (normed * gain[0:1, :] + shift[0:1, :]).astype(BF)

    def return_rows(image, row, at):
        grad = live_rate(1, image, row) * cot[at, :].astype(F32)
        ret_grad[at, :] = grad.astype(BF)
        small[7:8, :] += column_sum(grad)

    tok_copy.wait()
    over_rows(first_norm)

    lane = lax.broadcasted_iota(jnp.int32, (slot, 128), 1)
    low_lanes = lane < HEAD_DIM
    position = lax.broadcasted_iota(jnp.int32, (slot, slot), 1)
    padded = (slot + 127) // 128 * 128
    padded_position = lax.broadcasted_iota(jnp.int32, (slot, padded), 1)
    score_scale = HEAD_DIM ** (-0.5)

    def pick(head, values):
        mask = low_lanes if head == 0 else jnp.logical_not(low_lanes)
        return jnp.where(mask, values, jnp.zeros_like(values))

    def stacked(values):
        blank = jnp.zeros((padded - slot, 128), BF)
        return jnp.concatenate([pick(0, values), blank, pick(1, values), blank], axis=0)

    def key_length(image):
        index = m * images + image
        return grids[0, index] * grids[1, index] + 2

    def softmax(scores, length):
        places = position if scores.shape[1] == slot else padded_position
        scores = jnp.where(places < length, scores * score_scale, -1000000000.0)
        raised = jnp.exp(scores - jnp.max(scores, axis=-1, keepdims=True))
        return raised * (1.0 / jnp.sum(raised, axis=-1, keepdims=True))

    def project(xb):
        at = pl.ds(pl.multiple_of(xb * pair, 16), pair)
        qkv_row[:, 0:cols] = qkv_all[xb * 2]
        qkv_row[:, cols:pair] = qkv_all[xb * 2 + 1]
        for j in range(3):
            value = dot(entry[...], wqkv[j, at, :], 1, 1)
            if j != 1:
                row = j // 2
                value = value + qkv_row[row : row + 1, :]
            value = value.astype(BF)
            for pack in range(packs):
                heads[j, xb * packs + pack] = value[:, pack * 128 : (pack + 1) * 128]
            agenda.spend(0.8)

    def attend(xb, image):
        for i in range(packs):
            pack = xb * packs + i
            at = pl.ds(pl.multiple_of(image * slot, 16), slot)
            queries, keys, values = (heads[j, pack, at, :] for j in range(3))
            length = key_length(image)
            scores = dot(queries, stacked(keys), 1, 1)
            probs = [softmax(scores[:, k * padded : (k + 1) * padded], length) for k in range(2)]
            probs = jnp.concatenate([part.astype(BF) for part in probs], axis=1)
            total = dot(probs, stacked(values), 1, 0)
            mixed[pack, at, :] = total.astype(BF)
            agenda.spend(0.7)

    agenda.spend(1.5)
    for p in pieces[2:]:
        ag_copy(0, p).start()
        ag_local(p).start()
    bias_own(1).wait()
    bias_copy(5).wait_recv()
    near_ready("qk", "v")
    agenda.spend(1.0)
    project(x)
    for image in range(images):
        attend(x, image)
    cot_copy.wait()
    over_rows(return_rows)
    agenda.spend(1.0)
    near_ready("d")
    grad_peer = give.at[1, x, pl.ds(0, rows), :]
    grad_peer[...] = dot(ret_grad[...], wdn[peer_block], 1, 1).astype(BF)
    agenda.spend(1.2)
    value = dot(ret_grad[...], wdn[own_block], 1, 1).astype(BF)
    for pack in range(2 * packs):
        mixed_grad[pack] = value[:, pack * 128 : (pack + 1) * 128]
    agenda.spend(1.2)
    bias_own(0).wait()
    for i in range(5):
        bias_copy(i).wait_recv()
    far_ready("qk", "v")
    project(1 - x)
    for image in range(images):
        attend(1 - x, image)

    near_ready("p")
    far_ready("p")
    all_mixed = jnp.concatenate([mixed[pack] for pack in range(2 * packs)], axis=1)
    work[...] = dot(all_mixed, wproj[...], 1, 0)

    def second_norm(image, row, at):
        value = tok[at, :].astype(F32) + live_rate(0, image, row) * (work[at, :] + pbias[0:1, :])
        middle[at, :] = value
        normed, _ = normalise(value)
        entry_two[at, :] = (normed * gain[1:2, :] + shift[1:2, :]).astype(BF)

    over_rows(second_norm)
    agenda.spend(2.7)

    def emit(job, xb, slot_, mine, first, size, value):
        kept, far = mine
        at = pl.ds(first, size)
        if not kept:
            give[job % 2, xb, at, :] = value.astype(BF)
            core_start(job, xb, slot_, first, size)
            return
        core_copy(job, xb, slot_, first, size).wait_recv()
        total = value + sum_core[job, xb, at, :].astype(F32)
        sum_core[job, xb, at, :] = total.astype(BF)
        if far:
            start_x(job * width + first, size)
        else:
            own_ready(job * width + first, size)

    def feed_first(block, xb, mine, part):
        first, size = part * wide, wide
        lanes = slice(first, first + size)
        hidden = dot(entry_two[...], wup[block, :, lanes], 1, 0) + up_all[block, :, lanes]
        share = 0.5 * (1.0 + lax.erf(hidden * 0.7071067811865476))
        density = jnp.exp(-0.5 * hidden * hidden) * 0.3989422804014327
        active = (hidden * share).astype(BF)
        act[block, :, lanes] = active
        slope[block, :, lanes] = (share + hidden * density).astype(BF)
        slot_ = (0 if mine[1] else 2) + part
        emit(0, xb, slot_, mine, first, size, dot(active, ret_grad[...], 0, 0))
        agenda.spend(1.9)

    def feed_back(block, xb, mine, first):
        if mine == (False, False):
            grad = grad_peer[...].astype(F32)
        elif mine == (True, False):
            grad = jnp.concatenate([mixed_grad[pack] for pack in range(2 * packs)], axis=1)
            grad = grad.astype(F32)
        else:
            grad = dot(ret_grad[...], wdn[block], 1, 1)
            agenda.spend(1.2)
        grad = (grad * slope[block].astype(F32)).astype(BF)
        slope[block] = grad
        small[pl.ds(8 + block, 1), :] = column_sum(grad.astype(F32))
        agenda.spend(0.4)
        slot_ = 4 if mine[1] else 5
        emit(1, xb, slot_, mine, 0, width, dot(entry_two[...], slope[block], 0, 0))
        agenda.spend(1.4)
        value = dot(slope[block], wup[block], 1, 1)
        if first:
            tokens_grad[...] = value
        else:
            tokens_grad[...] += value
        agenda.spend(1.2)

    order = (
        (far_peer, 1 - x, (False, True)),
        (far_block, 1 - x, (True, True)),
        (peer_block, x, (False, False)),
        (own_block, x, (True, False)),
    )
    near_ready("u0", "u1")
    far_ready("u0", "u1")
    for part in range(2):
        for item in order:
            feed_first(*item, part)
    far_ready("d")
    for i, item in enumerate(order):
        feed_back(*item, i == 0)

    def norm_back(values, grad, r):
        normed, scale = normalise(values)
        small[r : r + 1, :] += column_sum(grad * normed)
        small[2 + r : 3 + r, :] += column_sum(grad)
        scaled = grad * gain[r : r + 1, :]
        mean_one = jnp.mean(scaled, axis=-1, keepdims=True)
        mean_two = jnp.mean(scaled * normed, axis=-1, keepdims=True)
        return scale * (scaled - mean_one - normed * mean_two)

    def second_back(image, row, at):
        grad = cot[at, :].astype(F32) + norm_back(middle[at, :], tokens_grad[at, :], 1)
        tokens_grad[at, :] = grad
        scaled = live_rate(0, image, row) * grad
        mixer_grad[at, :] = scaled.astype(BF)
        small[6:7, :] += column_sum(scaled)

    mixer_grad = entry_two
    over_rows(second_back)
    agenda.spend(2.2)

    for copy in core_started[:4]:
        core_copy(*copy).wait_send()
    waiting = []

    def emit_narrow(s, xb, far, value):
        part = pl.ds(s * cols, cols)
        place = len(waiting) % 2
        low, high = value[0:cols], value[cols:pair]
        give[0, xb, part, :] = jnp.where(c == 0, high, low).astype(BF)
        keep[place] = jnp.where(c == 0, low, high)
        core_start(2, xb, 6 + s * 2 + (0 if far else 1), s * cols, cols)
        waiting.append((s, xb, far, place))

    def settle(left):
        while len(waiting) - settled[0] > left:
            s, xb, far, place = waiting[settled[0]]
            settled[0] += 1
            part = pl.ds(s * cols, cols)
            core_copy(2, xb, 6 + s * 2 + (0 if far else 1), s * cols, cols).wait_recv()
            total = keep[place] + sum_core[2, xb, part, :].astype(F32)
            sum_core[2, xb, part, :] = total.astype(BF)
            if far:
                start_x(2 * width + s * cols, cols)
            else:
                own_ready(2 * width + s * cols, cols)

    settled = [0]

    def side(ref, xb):
        return jnp.concatenate([ref[xb * packs + pack] for pack in range(packs)], axis=1)

    def attend_back(xb, image):
        for i in range(packs):
            pack = xb * packs + i
            at = pl.ds(pl.multiple_of(image * slot, 16), slot)
            queries, keys, values = (heads[j, pack, at, :] for j in range(3))
            grads = mixed_grad[pack, at, :]
            length = key_length(image)
            query_grad = jnp.zeros((slot, 128), F32)
            key_grad = jnp.zeros((slot, 128), F32)
            value_grad = jnp.zeros((slot, 128), F32)
            for head in range(2):
                head_keys = pick(head, keys)
                probs = softmax(dot(queries, head_keys, 1, 1), length)
                probs_grad = dot(grads, pick(head, values), 1, 1)
                inner = jnp.sum(probs * probs_grad, axis=-1, keepdims=True)
                score_grad = (probs * (probs_grad - inner)).astype(BF)
                query_grad = query_grad + dot(score_grad, head_keys, 1, 0)
                key_grad = key_grad + dot(score_grad, pick(head, queries), 0, 0)
                value_grad = value_grad + dot(probs.astype(BF), pick(head, grads), 0, 0)
            heads[0, pack, at, :] = (query_grad * score_scale).astype(BF)
            heads[1, pack, at, :] = (key_grad * score_scale).astype(BF)
            heads[2, pack, at, :] = value_grad.astype(BF)
            agenda.spend(1.2)

    def qkv_back(xb, far):
        lanes = pl.ds(pl.multiple_of(xb * pair, 128), pair)
        for j in range(3):
            grad = side(heads.at[j], xb)
            emit_narrow(1 + j, xb, far, dot(grad, entry[...], 0, 0))
            settle(1)
            if j != 1:
                row = 4 if j == 0 else 5
                small[row : row + 1, lanes] = column_sum(grad.astype(F32))
            agenda.spend(1.2)

    value = dot(mixer_grad[...], wproj[...], 1, 1).astype(BF)
    for pack in range(2 * packs):
        mixed_grad[pack] = value[:, pack * 128 : (pack + 1) * 128]
    for xb, far in ((1 - x, True), (x, False)):
        emit_narrow(0, xb, far, dot(side(mixed, xb), mixer_grad[...], 0, 0))
    agenda.spend(3.5)
    settle(0)
    for image in range(images):
        attend_back(1 - x, image)
    qkv_back(1 - x, True)
    settle(0)
    for image in range(images):
        attend_back(x, image)
    qkv_back(x, False)
    settle(0)

    for j in range(3):
        grad = jnp.concatenate([heads[j, pack] for pack in range(2 * packs)], axis=1)
        part = dot(grad, wqkv[j], 1, 0)
        work[...] = part if j == 0 else work[...] + part
        agenda.spend(1.4)

    def first_back(image, row, at):
        tokens_grad[at, :] += norm_back(tok[at, :].astype(F32), work[at, :], 0)

    over_rows(first_back)
    agenda.spend(2.2)

    small_devices = (
        [core_dev, x_dev, diag_dev],
        [y_dev],
        [quad_dev(k) for k in range(1, 4)],
        [group_dev(k) for k in range(1, groups)],
    )
    small_slots = ((0, 4, m), (0, 2, y), (2, 4, quad), (6, groups, group))
    last_small = 2 if groups == 1 else 3

    def small_buffer(stage):
        return small_got if stage == 0 else small_part

    def small_copies(stage):
        first, _, place = small_slots[stage]
        sems = sum(len(devices) for devices in small_devices[:stage])
        part = small_buffer(stage).at[first + place]
        return [
            remote(part, part, small_send.at[sems + i], small_recv.at[sems + i], device)
            for i, device in enumerate(small_devices[stage])
        ]

    def small_start(stage, value):
        first, _, place = small_slots[stage]
        small_buffer(stage)[first + place] = value
        for copy in small_copies(stage):
            copy.start()
        agenda.post(agenda.now + HOP + 3.0, functools.partial(small_stage, stage))

    def small_stage(stage):
        for copy in small_copies(stage):
            copy.wait_recv()
        first, count, _ = small_slots[stage]
        buffer = small_buffer(stage)
        total = buffer[first]
        for other in range(1, count):
            total = total + buffer[first + other]
        if stage == 0:
            small[...] = total
            lanes = pl.ds(pl.multiple_of(x * pair, 128), pair)
            ours = jnp.concatenate([small[4:5, lanes], small[5:6, lanes]], axis=1)
            own = small[pl.ds(8 + m, 1), :]
            total = jnp.concatenate([total[0:4], total[6:8], own, ours], axis=0)
        if stage < last_small:
            small_start(stage + 1, total)
        else:
            small[0:8, :] = total

    small_start(0, small[...])
    for i, (block, _, _) in enumerate(order):
        part = dot(act[block], wdn[block], 1, 0)
        work[...] = part if i == 0 else work[...] + part
        agenda.spend(1.4)

    def finish(image, row, at):
        value = middle[at, :] + live_rate(1, image, row) * (work[at, :] + pbias[1:2, :])
        block_out[at, :] = value.astype(BF)

    over_rows(finish)
    agenda.spend(1.2)
    agenda.until(lambda: not agenda.queue)
    small_out[0:8, :] = small[0:8, :]
    for i in range(2):
        low = i * pair
        qkv_row[i : i + 1, :] = small[7:8, low : low + pair]
    small_out[8:10, 0:cols] = jnp.where(c == 0, qkv_row[:, 0:cols], qkv_row[:, cols:pair])

    for sub in range(len(subs)):
        yag_copy(sub).wait_recv()
    for i in range(6):
        bias_copy(i).wait_send()
    for p in pieces:
        for route in range(10):
            ag_copy(route, p).wait_send()
    for copy in core_started[4:]:
        core_copy(*copy).wait_send()
    for sub in range(len(subs)):
        x_copy(sub).wait_send()
        y_copy(sub).wait_send()
        yag_copy(sub).wait_send()
        for step in range(1, 4):
            z_copy(sub, step).wait_send()
            zag_copy(sub, step).wait_send()
        for step in range(1, groups):
            group_copy(sub, step).wait_send()
    for stage in range(last_small + 1):
        for copy in small_copies(stage):
            copy.wait_send()


def finish_kernel(
    grads,
    tokens_part,
    block_part,
    small_part,
    block_out,
    tokens_grad,
    gain_grad,
    shift_grad,
    qkv_grad,
    qkv_bias_grad,
    proj_grad,
    proj_bias_grad,
    up_grad,
    up_bias_grad,
    down_grad,
    held,
    wide,
    tokens,
    block,
    small,
    in_sem,
    out_sem,
):
    parts = grads.shape[0]
    loads = [pltpu.make_async_copy(grads.at[i], held.at[i], in_sem.at[i]) for i in range(parts)]
    passed = [(tokens_part, tokens, tokens_grad), (block_part, block, block_out)]
    for i, (source, place, _) in enumerate(passed):
        loads.append(pltpu.make_async_copy(source, place, in_sem.at[parts + i]))
    loads.append(pltpu.make_async_copy(small_part, small, in_sem.at[parts + 2]))
    for load in loads:
        load.start()
    stores = []
    for i in range(parts):
        job, s = i // SUBS, i % SUBS
        if job < 2:
            dest = (down_grad, up_grad)[job].at[s]
        else:
            dest = proj_grad if s == 0 else qkv_grad.at[s - 1]
        loads[i].wait()
        wide[i] = held[i].astype(F32)
        stores.append(pltpu.make_async_copy(wide.at[i], dest, out_sem.at[i]))
        stores[-1].start()
    for i, (_, place, dest) in enumerate(passed):
        loads[parts + i].wait()
        stores.append(pltpu.make_async_copy(place, dest, out_sem.at[parts + i]))
        stores[-1].start()
    loads[parts + 2].wait()
    gain_grad[...] = small[0:2, :]
    shift_grad[...] = small[2:4, :]
    proj_bias_grad[...] = small[4:6, :]
    qkv_bias_grad[...] = small[8:10, 0 : qkv_bias_grad.shape[1]]
    up_bias_grad[...] = small[6:7, :].reshape(up_bias_grad.shape)
    for store in stores:
        store.wait()


def local(
    tokens,
    norm_gain,
    norm_shift,
    qkv_weight,
    qkv_bias,
    proj_weight,
    proj_bias,
    up_weight,
    up_bias,
    down_weight,
    patch_grids,
    keep_masks,
    out_cotangent,
):
    rows, width = tokens.shape
    mp = lax.axis_size("mp")
    nz = lax.axis_size("dp") // 2
    images = patch_grids.shape[0] // mp
    slot = rows // images
    cols = qkv_weight.shape[2]
    pair = 2 * cols
    packs = pair // 128
    subs = len(sub_list(width, cols))
    groups = nz // 4
    cross = max(1, subs * (groups - 1))
    qkv_rows = jnp.transpose(qkv_weight, (0, 2, 1))
    vmem = pl.BlockSpec(memory_space=pltpu.VMEM)
    smem = pl.BlockSpec(memory_space=pltpu.SMEM)
    hbm = pl.BlockSpec(memory_space=pl.ANY)
    dma = pltpu.SemaphoreType.DMA
    scratch = [
        pltpu.VMEM((3, width, width), BF),
        pltpu.VMEM((width, width), BF),
        pltpu.VMEM((4, width, width), BF),
        pltpu.VMEM((4, width, width), BF),
        pltpu.VMEM((rows, width), BF),
        pltpu.VMEM((rows, width), BF),
        pltpu.VMEM((4, 1, width), F32),
        pltpu.VMEM((4, 2, cols), F32),
        pltpu.VMEM((1, width), F32),
        pltpu.VMEM((2, pair), F32),
        pltpu.VMEM((2, cols, width), F32),
        pltpu.VMEM((rows, width), BF),
        pltpu.VMEM((rows, width), BF),
        pltpu.VMEM((rows, width), BF),
        pltpu.VMEM((3, 2 * packs, rows, 128), BF),
        pltpu.VMEM((2 * packs, rows, 128), BF),
        pltpu.VMEM((2 * packs, rows, 128), BF),
        pltpu.VMEM((4, rows, width), BF),
        pltpu.VMEM((4, rows, width), BF),
        pltpu.VMEM((rows, width), F32),
        pltpu.VMEM((rows, width), F32),
        pltpu.VMEM((2, 2, width, width), BF),
        pltpu.VMEM((JOBS, 2, width, width), BF),
        pltpu.VMEM((JOBS * width, width), BF),
        pltpu.VMEM((JOBS * width // 2, width), BF),
        pltpu.VMEM((4, JOBS * width // 4, width // 2), BF),
        pltpu.VMEM((groups, JOBS * width // 4 if groups > 1 else 16, width // 2), BF),
        pltpu.VMEM((16, width), F32),
        pltpu.VMEM((4, 16, width), F32),
        pltpu.VMEM((6 + groups, 8, width), F32),
        dma((12,)),
        dma((10, 6)),
        dma((10, 6)),
        dma((6,)),
        dma((6,)),
        dma((14,)),
        dma((14,)),
        dma((subs,)),
        dma((subs,)),
        dma((subs,)),
        dma((subs,)),
        dma((3 * subs,)),
        dma((3 * subs,)),
        dma((cross,)),
        dma((cross,)),
        dma((3 * subs,)),
        dma((3 * subs,)),
        dma((subs,)),
        dma((subs,)),
        dma((subs,)),
        dma((6 + groups,)),
        dma((6 + groups,)),
    ]
    grads, tokens_grad, block_out, small = pl.pallas_call(
        functools.partial(layer_kernel, (nz, images, slot, width, cols)),
        out_shape=(
            jax.ShapeDtypeStruct((JOBS * width, width), BF),
            jax.ShapeDtypeStruct((rows, width), F32),
            jax.ShapeDtypeStruct((rows, width), BF),
            jax.ShapeDtypeStruct((16, width), F32),
        ),
        in_specs=[hbm] * 2 + [vmem] * 3 + [smem] * 2 + [vmem] * 2 + [hbm] * 4,
        out_specs=(hbm, vmem, vmem, vmem),
        scratch_shapes=scratch,
        compiler_params=pltpu.CompilerParams(
            collective_id=0, has_side_effects=True, vmem_limit_bytes=64 * 2**20 - 2**17
        ),
    )(
        tokens,
        out_cotangent,
        norm_gain,
        norm_shift,
        proj_bias,
        patch_grids.T,
        keep_masks.T,
        up_bias,
        qkv_bias,
        qkv_rows,
        proj_weight,
        up_weight,
        down_weight,
    )
    out = pl.pallas_call(
        finish_kernel,
        out_shape=(
            jax.ShapeDtypeStruct((rows, width), BF),
            jax.ShapeDtypeStruct((rows, width), F32),
            jax.ShapeDtypeStruct((2, width), F32),
            jax.ShapeDtypeStruct((2, width), F32),
            jax.ShapeDtypeStruct((3, cols, width), F32),
            jax.ShapeDtypeStruct((2, cols), F32),
            jax.ShapeDtypeStruct((cols, width), F32),
            jax.ShapeDtypeStruct((2, width), F32),
            jax.ShapeDtypeStruct((SUBS, cols, width), F32),
            jax.ShapeDtypeStruct((width,), F32),
            jax.ShapeDtypeStruct((SUBS, cols, width), F32),
        ),
        in_specs=[hbm] * 4,
        out_specs=(hbm, hbm, vmem, vmem, hbm, vmem, hbm, vmem, hbm, vmem, hbm),
        scratch_shapes=[
            pltpu.VMEM((JOBS * SUBS, cols, width), BF),
            pltpu.VMEM((JOBS * SUBS, cols, width), F32),
            pltpu.VMEM((rows, width), F32),
            pltpu.VMEM((rows, width), BF),
            pltpu.VMEM((16, width), F32),
            dma((JOBS * SUBS + 3,)),
            dma((JOBS * SUBS + 2,)),
        ],
        compiler_params=pltpu.CompilerParams(vmem_limit_bytes=60 * 2**20),
    )(grads.reshape(JOBS * SUBS, cols, width), tokens_grad, block_out, small)
    out = list(out)
    out[4] = jnp.transpose(out[4], (0, 2, 1))
    out[8] = out[8].reshape(up_weight.shape)
    out[10] = out[10].reshape(down_weight.shape)
    return tuple(out)


def solution(mesh):
    return jax.shard_map(
        local,
        mesh=mesh,
        in_specs=(
            P(("dp", "mp"), None),
            P(),
            P(),
            P(None, None, "mp"),
            P(None, "mp"),
            P("mp", None),
            P(),
            P(None, "mp"),
            P("mp"),
            P("mp", None),
            P("dp", None),
            P("dp", None),
            P(("dp", "mp"), None),
        ),
        out_specs=(
            P(("dp", "mp"), None),
            P(("dp", "mp"), None),
            P(),
            P(),
            P(None, None, "mp"),
            P(None, "mp"),
            P("mp", None),
            P(),
            P(None, "mp"),
            P("mp"),
            P("mp", None),
        ),
        check_vma=False,
    )
```

```python
import functools
import heapq

import jax
import jax.numpy as jnp
from jax import lax
from jax.experimental import pallas as pl
from jax.experimental.pallas import tpu as pltpu
from jax.sharding import PartitionSpec as P

HEAD_DIM = 64
EPSILON = 1e-06
KEEP_RATE = 0.9
MESH = pl.DeviceIdType.MESH
BF = jnp.bfloat16
F32 = jnp.float32
TILE = 96
JOBS = 3
SUBS = 4
LINK_ROW = 0.033
HOP = 2.0
HANDLE = 0.3
LATE = 4
LATE_Z = 0


def dot(left, right, left_dim, right_dim):
    return lax.dot_general(
        left, right, (((left_dim,), (right_dim,)), ((), ())), preferred_element_type=F32
    )


def normalise(rows):
    centred = rows - jnp.mean(rows, axis=-1, keepdims=True)
    spread = jnp.mean(centred * centred, axis=-1, keepdims=True)
    scale = lax.rsqrt(spread + EPSILON)
    return centred * scale, scale


def sub_list(width, cols):
    parts = [(k * cols, cols) for k in range(JOBS * SUBS)]
    third = cols // 3
    first = [(k * third, third) for k in range(3)]
    last = [(parts[-1][0] + k * third, third) for k in range(3)]
    return first + parts[1:-1] + last


class Agenda:
    def __init__(self):
        self.now = 0.0
        self.free = {}
        self.queue = []
        self.number = 0

    def send(self, link, rows):
        begin = max(self.now, self.free.get(link, 0.0))
        self.free[link] = begin + rows * LINK_ROW
        return self.free[link] + HOP

    def post(self, ready, action):
        self.number += 1
        heapq.heappush(self.queue, (ready, self.number, action))

    def handle(self):
        ready, _, action = heapq.heappop(self.queue)
        self.now = max(self.now, ready) + HANDLE
        action()

    def spend(self, time):
        self.now += time
        while self.queue and self.queue[0][0] <= self.now:
            self.handle()

    def until(self, reached):
        while not reached():
            self.handle()


def column_sum(rows):
    return jnp.sum(rows, axis=0, keepdims=True)


def layer_kernel(
    sizes,
    tok_in,
    cot_in,
    gain,
    shift,
    pbias,
    grids,
    masks,
    up_bias,
    qkv_bias,
    wqkv_in,
    wproj_in,
    wup_in,
    wdn_in,
    grads_out,
    tokens_out,
    block_out,
    small_out,
    wqkv,
    wproj,
    wup,
    wdn,
    tok,
    cot,
    up_all,
    qkv_all,
    up_own,
    qkv_row,
    keep,
    entry,
    entry_two,
    ret_grad,
    heads,
    mixed,
    mixed_grad,
    act,
    slope,
    work,
    middle,
    tokens_grad,
    finished,
    give,
    sum_core,
    got_x,
    got_y,
    got_z,
    got_group,
    small,
    small_got,
    small_part,
    local_sem,
    ag_send,
    ag_recv,
    bias_send,
    bias_recv,
    core_send,
    core_recv,
    x_send,
    x_recv,
    y_send,
    y_recv,
    z_send,
    z_recv,
    group_send,
    group_recv,
    zag_send,
    zag_recv,
    yag_send,
    yag_recv,
    own_sem,
    small_send,
    small_recv,
):
    nz, images, slot, width, cols = sizes
    rows = images * slot
    pair = 2 * cols
    half = cols // 2
    packs = pair // 128
    groups = nz // 4
    subs = sub_list(width, cols)

    d = lax.axis_index("dp")
    m = lax.axis_index("mp")
    y = lax.rem(d, 2)
    z = d // 2
    x = m // 2
    c = lax.rem(m, 2)
    core_dev = (d, x * 2 + 1 - c)
    x_dev = (d, (1 - x) * 2 + c)
    diag_dev = (d, (1 - x) * 2 + 1 - c)
    y_dev = (z * 2 + 1 - y, m)
    group, quad = z // 4, lax.rem(z, 4)

    def z_dev(other):
        return (other * 2 + y, m)

    def quad_dev(step):
        return z_dev(group * 4 + lax.rem(quad + step, 4))

    def group_dev(step):
        return z_dev(lax.rem(group + step, groups) * 4 + quad)

    def remote(src, dst, send, recv, device):
        return pltpu.make_async_remote_copy(
            src_ref=src,
            dst_ref=dst,
            send_sem=send,
            recv_sem=recv,
            device_id=device,
            device_id_type=MESH,
        )

    tok_copy = pltpu.make_async_copy(tok_in, tok, local_sem.at[8])
    cot_copy = pltpu.make_async_copy(cot_in, cot, local_sem.at[9])
    tok_copy.start()
    cot_copy.start()
    barrier = pltpu.get_barrier_semaphore()
    greeted = [core_dev, x_dev, diag_dev, y_dev]
    greeted += [quad_dev(k) for k in range(1, 4)]
    greeted += [group_dev(k) for k in range(1, groups)]
    for device in greeted:
        pl.semaphore_signal(barrier, inc=1, device_id=device, device_id_type=MESH)
    pl.semaphore_wait(barrier, len(greeted))

    own_block = m
    peer_block = x * 2 + 1 - c
    far_block = (1 - x) * 2 + c
    far_peer = (1 - x) * 2 + 1 - c

    pieces = ("q", "k", "v", "p", "u0", "u1", "d")
    near_z = z + 1 - 2 * lax.rem(z, 2)
    side_z = lax.rem(z, 2)
    quarters = (y * 2 + side_z, (1 - y) * 2 + side_z, y * 2 + 1 - side_z, 3 - y * 2 - side_z)
    wide = width // 2

    def rows_of(piece, part):
        size = {"u0": width // 2, "u1": width // 2, "d": width}.get(piece, cols)
        if part is None:
            return 0, size
        return quarters[part] * (size // 4), size // 4

    def view(piece, block, part, lanes=None):
        start, size = rows_of(piece, part)
        lanes = pl.ds(0, width) if lanes is None else pl.ds(lanes * wide, wide)
        if piece in "qkvp":
            at = pl.ds(pl.multiple_of(block * cols + start, 16), size)
            if piece == "p":
                return wproj.at[at, lanes]
            return wqkv.at["qkv".index(piece), at, lanes]
        first = width // 2 if piece == "u1" else 0
        at = pl.ds(pl.multiple_of(first + start, 16), size)
        return (wdn if piece == "d" else wup).at[block, at, lanes]

    def view_in(piece, part):
        start, size = rows_of(piece, part)
        first = width // 2 if piece == "u1" else 0
        at = pl.ds(first + start if part is None else pl.multiple_of(first + start, 16), size)
        if piece in "qkv":
            return wqkv_in.at["qkv".index(piece), at, :]
        return {"p": wproj_in, "d": wdn_in}.get(piece, wup_in).at[at, :]

    def ag_local(p):
        i = pieces.index(p)
        return pltpu.make_async_copy(view_in(p, None), view(p, own_block, None), local_sem.at[i])

    def ag_copy(route, p):
        i = pieces.index(p)
        send, recv = ag_send.at[route, i], ag_recv.at[route, i]
        if route == 0:
            return remote(view_in(p, None), view(p, own_block, None), send, recv, core_dev)
        if route == 1:
            return remote(view_in(p, 0), view(p, own_block, 0), send, recv, x_dev)
        if route == 2:
            part, lanes, device = 0, None, y_dev
        elif route == 3:
            part, lanes, device = 0, None, z_dev(near_z)
        elif route == 4:
            part, lanes, device = 2, 0, y_dev
        elif route == 5:
            part, lanes, device = 1, 1, z_dev(near_z)
        else:
            part, lanes, device = route - 6, None, core_dev
        source = view(p, far_block, part, lanes)
        return remote(source, source, send, recv, device)

    def quarter_rows(p):
        return rows_of(p, None)[1] // 4

    def admit(*names):
        for p in names:
            agenda.post(max(agenda.now, x_ready[p]), functools.partial(from_x, p))

    def from_x(p):
        ag_copy(1, p).wait_recv()
        for route in (2, 3, 6):
            ag_copy(route, p).start()
        ready = max(agenda.send("y", quarter_rows(p)), agenda.send("z", quarter_rows(p)))
        agenda.post(ready, functools.partial(from_yz, p))

    def from_yz(p):
        ag_copy(2, p).wait_recv()
        ag_copy(5, p).start()
        ag_copy(7, p).start()
        ag_copy(3, p).wait_recv()
        ag_copy(4, p).start()
        ag_copy(8, p).start()
        rows_ = quarter_rows(p) // 2
        ready = max(agenda.send("y", rows_), agenda.send("z", rows_))
        agenda.post(ready, functools.partial(from_both, p))
        if p == "v":
            admit("p", "u0", "u1")
        elif p == "u1":
            admit("d")

    def from_both(p):
        ag_copy(4, p).wait_recv()
        ag_copy(5, p).wait_recv()
        ag_copy(9, p).start()
        gathered.add(p)

    def bias_copy(i):
        source, dest = (up_own, up_all) if i % 2 == 0 else (qkv_bias, qkv_all)
        device = (x_dev, diag_dev, core_dev)[i // 2]
        return remote(source, dest.at[m], bias_send.at[i], bias_recv.at[i], device)

    def bias_own(i):
        source, dest = (up_own, up_all) if i % 2 == 0 else (qkv_bias, qkv_all)
        return pltpu.make_async_copy(source, dest.at[m], local_sem.at[10 + i])

    up_own[...] = up_bias[...].reshape(1, width)
    for i in range(4):
        bias_copy(i).start()
    agenda = Agenda()
    gathered = set()
    x_ready = {}
    for p in pieces:
        ag_copy(1, p).start()
        x_ready[p] = agenda.send("x", quarter_rows(p))
    admit("q", "k", "v")
    for p in pieces[:3]:
        ag_copy(0, p).start()
        ag_local(p).start()
    for i in range(2):
        bias_copy(4 + i).start()
        bias_own(i).start()

    def near_ready(*names):
        for p in names:
            ag_local(p).wait()
            ag_copy(0, p).wait_recv()

    def far_ready(*names):
        for p in names:
            agenda.until(lambda: p in gathered)
            for route in (6, 7, 8, 9):
                ag_copy(route, p).wait_recv()

    core_started = []

    def core_copy(job, xb, slot_, first, size):
        at = pl.ds(first, size)
        return remote(
            give.at[job % 2, xb, at, :],
            sum_core.at[job, xb, at, :],
            core_send.at[slot_],
            core_recv.at[slot_],
            core_dev,
        )

    def core_start(*copy):
        core_started.append(copy)
        core_copy(*copy).start()

    def x_copy(sub):
        first, size = subs[sub]
        source = sum_core.at[first // width, 1 - x, pl.ds(first % width, size), :]
        return remote(
            source, got_x.at[pl.ds(first, size), :], x_send.at[sub], x_recv.at[sub], x_dev
        )

    def y_part(sub, which):
        first, size = subs[sub]
        start = pl.multiple_of(first % width + which * (size // 2), 16)
        return first // width, pl.ds(start, size // 2)

    def y_got(sub):
        first, size = subs[sub]
        return pl.ds(first // 2, size // 2)

    def y_copy(sub):
        job, at = y_part(sub, 1 - y)
        return remote(
            sum_core.at[job, x, at, :],
            got_y.at[y_got(sub), :],
            y_send.at[sub],
            y_recv.at[sub],
            y_dev,
        )

    def z_part(sub, owner):
        tall = subs[sub][1] // 4
        row = pl.multiple_of((owner // 2) * tall, 16)
        lanes = pl.ds(pl.multiple_of(lax.rem(owner, 2) * wide, 128), wide)
        return row, lanes, tall

    def z_got(sub, owner):
        row, lanes, tall = z_part(sub, owner)
        return got_y.at[pl.ds(pl.multiple_of(subs[sub][0] // 2 + row, 16), tall), lanes]

    def z_slot(sub, place):
        first, size = subs[sub]
        return got_z.at[place, pl.ds(first // 4, size // 4), :]

    def z_copy(sub, step):
        sem = sub * 3 + step - 1
        return remote(
            z_got(sub, lax.rem(quad + step, 4)),
            z_slot(sub, step - 1),
            z_send.at[sem],
            z_recv.at[sem],
            quad_dev(step),
        )

    def group_slot(sub, place):
        first, size = subs[sub]
        return got_group.at[place, pl.ds(first // 4, size // 4), :]

    def group_copy(sub, step):
        sem = sub * (groups - 1) + step - 1
        part = group_slot(sub, group)
        return remote(part, part, group_send.at[sem], group_recv.at[sem], group_dev(step))

    def final_part(sub):
        first, size = subs[sub]
        row, lanes, tall = z_part(sub, quad)
        row = pl.multiple_of(first + row + y * (size // 2), 16)
        return grads_out.at[pl.ds(row, tall), lanes]

    def zag_copy(sub, step):
        sem = sub * 3 + step - 1
        return remote(
            z_slot(sub, 3), final_part(sub), zag_send.at[sem], zag_recv.at[sem], quad_dev(step)
        )

    def own_copy(sub):
        return pltpu.make_async_copy(z_slot(sub, 3), final_part(sub), own_sem.at[sub])

    def yag_copy(sub):
        first, size = subs[sub]
        start = pl.multiple_of(first + y * (size // 2), 16)
        part = grads_out.at[pl.ds(start, size // 2), :]
        return remote(part, part, yag_send.at[sub], yag_recv.at[sub], y_dev)

    own_rows = []
    early = []
    summed_y = []
    held = []
    summed_z = []
    held_z = []

    def start_x(first, size):
        for sub, (row, length) in enumerate(subs):
            if first <= row < first + size:
                x_copy(sub).start()
                agenda.post(agenda.send("x", length), functools.partial(x_stage, sub))

    def own_ready(first, size):
        own_rows.append((first, first + size))
        for sub in list(early):
            if has_own(sub):
                early.remove(sub)
                agenda.post(agenda.now, functools.partial(x_stage, sub))

    def has_own(sub):
        first, size = subs[sub]
        return any(low <= first and first + size <= high for low, high in own_rows)

    def x_stage(sub):
        if not has_own(sub):
            early.append(sub)
            return
        x_copy(sub).wait_recv()
        first, size = subs[sub]
        job, at = first // width, pl.ds(first % width, size)
        sum_core[job, x, at, :] = sum_core[job, x, at, :] + got_x[pl.ds(first, size), :]
        y_copy(sub).start()
        agenda.post(agenda.send("y", size // 2), functools.partial(y_stage, sub))
        summed_y.append(sub)
        if len(summed_y) == len(subs):
            hand_out()

    def y_stage(sub):
        y_copy(sub).wait_recv()
        job, at = y_part(sub, y)
        got = y_got(sub)
        got_y[got, :] = sum_core[job, x, at, :] + got_y[got, :]
        for step in range(1, 4):
            z_copy(sub, step).start()
        agenda.post(agenda.send("z", subs[sub][1] // 2), functools.partial(z_stage, sub))
        summed_z.append(sub)
        if len(summed_z) == len(subs):
            share()

    def z_stage(sub):
        total = z_got(sub, quad)[...].astype(F32)
        for step in range(1, 4):
            z_copy(sub, step).wait_recv()
            total = total + z_slot(sub, step - 1)[...].astype(F32)
        if groups == 1:
            publish(sub, total)
            return
        group_slot(sub, group)[...] = total.astype(BF)
        for step in range(1, groups):
            group_copy(sub, step).start()
        agenda.post(agenda.send("z", subs[sub][1] // 2), functools.partial(group_stage, sub))

    def group_stage(sub):
        for step in range(1, groups):
            group_copy(sub, step).wait_recv()
        total = group_slot(sub, 0)[...].astype(F32)
        for other in range(1, groups):
            total = total + group_slot(sub, other)[...].astype(F32)
        publish(sub, total)

    def publish(sub, total):
        z_slot(sub, 3)[...] = total.astype(BF)
        own_copy(sub).start()
        held_z.append(sub)
        share()

    def share():
        if len(subs) - LATE_Z <= len(summed_z) < len(subs):
            return
        for sub in held_z:
            for step in range(1, 4):
                zag_copy(sub, step).start()
            agenda.post(agenda.send("z", subs[sub][1] // 2), functools.partial(zag_stage, sub))
        held_z.clear()

    def zag_stage(sub):
        own_copy(sub).wait()
        for step in range(1, 4):
            zag_copy(sub, step).wait_recv()
        held.append(sub)
        hand_out()

    def hand_out():
        if len(subs) - LATE <= len(summed_y) < len(subs):
            return
        for sub in held:
            yag_copy(sub).start()
            agenda.send("y", subs[sub][1] // 2)
        held.clear()

    def live_rate(which, image, row):
        index = m * images + image
        length = grids[0, index] * grids[1, index] + 2
        kept = masks[which, index].astype(F32) / KEEP_RATE
        position = lax.broadcasted_iota(jnp.int32, (TILE, 1), 0) + row
        return jnp.where(position < length, kept, 0.0)

    def over_rows(body):
        for image in range(images):

            def step(i, carry):
                row = i * TILE
                body(image, row, pl.ds(pl.multiple_of(image * slot + row, 16), TILE))
                return carry

            lax.fori_loop(0, slot // TILE, step, 0, unroll=True)

    small[...] = jnp.zeros_like(small)

    def first_norm(image, row, at):
        normed, _ = normalise(tok[at, :].astype(F32))
        entry[at, :] = (normed * gain[0:1, :] + shift[0:1, :]).astype(BF)

    def return_rows(image, row, at):
        grad = live_rate(1, image, row) * cot[at, :].astype(F32)
        ret_grad[at, :] = grad.astype(BF)
        small[7:8, :] += column_sum(grad)

    tok_copy.wait()
    over_rows(first_norm)

    lane = lax.broadcasted_iota(jnp.int32, (slot, 128), 1)
    low_lanes = lane < HEAD_DIM
    position = lax.broadcasted_iota(jnp.int32, (slot, slot), 1)
    padded = (slot + 127) // 128 * 128
    padded_position = lax.broadcasted_iota(jnp.int32, (slot, padded), 1)
    score_scale = HEAD_DIM ** (-0.5)

    def pick(head, values):
        mask = low_lanes if head == 0 else jnp.logical_not(low_lanes)
        return jnp.where(mask, values, jnp.zeros_like(values))

    def stacked(values):
        blank = jnp.zeros((padded - slot, 128), BF)
        return jnp.concatenate([pick(0, values), blank, pick(1, values), blank], axis=0)

    def key_length(image):
        index = m * images + image
        return grids[0, index] * grids[1, index] + 2

    def softmax(scores, length):
        places = position if scores.shape[1] == slot else padded_position
        scores = jnp.where(places < length, scores * score_scale, -1000000000.0)
        raised = jnp.exp(scores - jnp.max(scores, axis=-1, keepdims=True))
        return raised * (1.0 / jnp.sum(raised, axis=-1, keepdims=True))

    def project(xb):
        at = pl.ds(pl.multiple_of(xb * pair, 16), pair)
        qkv_row[:, 0:cols] = qkv_all[xb * 2]
        qkv_row[:, cols:pair] = qkv_all[xb * 2 + 1]
        for j in range(3):
            value = dot(entry[...], wqkv[j, at, :], 1, 1)
            if j != 1:
                row = j // 2
                value = value + qkv_row[row : row + 1, :]
            value = value.astype(BF)
            for pack in range(packs):
                heads[j, xb * packs + pack] = value[:, pack * 128 : (pack + 1) * 128]
            agenda.spend(0.8)

    def attend(xb, image):
        for i in range(packs):
            pack = xb * packs + i
            at = pl.ds(pl.multiple_of(image * slot, 16), slot)
            queries, keys, values = (heads[j, pack, at, :] for j in range(3))
            length = key_length(image)
            scores = dot(queries, stacked(keys), 1, 1)
            probs = [softmax(scores[:, k * padded : (k + 1) * padded], length) for k in range(2)]
            probs = jnp.concatenate([part.astype(BF) for part in probs], axis=1)
            total = dot(probs, stacked(values), 1, 0)
            mixed[pack, at, :] = total.astype(BF)
            agenda.spend(0.7)

    agenda.spend(1.5)
    for p in pieces[3:]:
        ag_copy(0, p).start()
        ag_local(p).start()
    bias_own(1).wait()
    bias_copy(5).wait_recv()
    near_ready("q", "k", "v")
    agenda.spend(1.0)
    project(x)
    for image in range(images):
        attend(x, image)
    cot_copy.wait()
    over_rows(return_rows)
    agenda.spend(1.0)
    near_ready("d")
    grad_peer = give.at[1, x, pl.ds(0, rows), :]
    grad_peer[...] = dot(ret_grad[...], wdn[peer_block], 1, 1).astype(BF)
    agenda.spend(1.2)
    value = dot(ret_grad[...], wdn[own_block], 1, 1).astype(BF)
    for pack in range(2 * packs):
        mixed_grad[pack] = value[:, pack * 128 : (pack + 1) * 128]
    agenda.spend(1.2)
    bias_own(0).wait()
    for i in range(5):
        bias_copy(i).wait_recv()
    far_ready("q", "k", "v")
    project(1 - x)
    for image in range(images):
        attend(1 - x, image)

    near_ready("p")
    far_ready("p")
    all_mixed = jnp.concatenate([mixed[pack] for pack in range(2 * packs)], axis=1)
    work[...] = dot(all_mixed, wproj[...], 1, 0)

    def second_norm(image, row, at):
        value = tok[at, :].astype(F32) + live_rate(0, image, row) * (work[at, :] + pbias[0:1, :])
        middle[at, :] = value
        normed, _ = normalise(value)
        entry_two[at, :] = (normed * gain[1:2, :] + shift[1:2, :]).astype(BF)

    over_rows(second_norm)
    agenda.spend(2.7)

    def emit(job, xb, slot_, mine, first, size, value):
        kept, far = mine
        at = pl.ds(first, size)
        if not kept:
            give[job % 2, xb, at, :] = value.astype(BF)
            core_start(job, xb, slot_, first, size)
            return
        core_copy(job, xb, slot_, first, size).wait_recv()
        total = value + sum_core[job, xb, at, :].astype(F32)
        sum_core[job, xb, at, :] = total.astype(BF)
        if far:
            start_x(job * width + first, size)
        else:
            own_ready(job * width + first, size)

    def feed_first(block, xb, mine, part):
        first, size = part * wide, wide
        lanes = slice(first, first + size)
        hidden = dot(entry_two[...], wup[block, :, lanes], 1, 0) + up_all[block, :, lanes]
        share = 0.5 * (1.0 + lax.erf(hidden * 0.7071067811865476))
        density = jnp.exp(-0.5 * hidden * hidden) * 0.3989422804014327
        active = (hidden * share).astype(BF)
        act[block, :, lanes] = active
        slope[block, :, lanes] = (share + hidden * density).astype(BF)
        slot_ = (0 if mine[1] else 2) + part
        emit(0, xb, slot_, mine, first, size, dot(active, ret_grad[...], 0, 0))
        agenda.spend(1.9)

    def feed_back(block, xb, mine, first):
        if mine == (False, False):
            grad = grad_peer[...].astype(F32)
        elif mine == (True, False):
            grad = jnp.concatenate([mixed_grad[pack] for pack in range(2 * packs)], axis=1)
            grad = grad.astype(F32)
        else:
            grad = dot(ret_grad[...], wdn[block], 1, 1)
            agenda.spend(1.2)
        grad = (grad * slope[block].astype(F32)).astype(BF)
        slope[block] = grad
        small[pl.ds(8 + block, 1), :] = column_sum(grad.astype(F32))
        agenda.spend(0.4)
        slot_ = 4 if mine[1] else 5
        emit(1, xb, slot_, mine, 0, width, dot(entry_two[...], slope[block], 0, 0))
        agenda.spend(1.4)
        value = dot(slope[block], wup[block], 1, 1)
        if first:
            tokens_grad[...] = value
        else:
            tokens_grad[...] += value
        agenda.spend(1.2)

    order = (
        (far_peer, 1 - x, (False, True)),
        (far_block, 1 - x, (True, True)),
        (peer_block, x, (False, False)),
        (own_block, x, (True, False)),
    )
    near_ready("u0", "u1")
    far_ready("u0", "u1")
    for part in range(2):
        for item in order:
            feed_first(*item, part)
    far_ready("d")
    for i, item in enumerate(order):
        feed_back(*item, i == 0)

    def norm_back(values, grad, r):
        normed, scale = normalise(values)
        small[r : r + 1, :] += column_sum(grad * normed)
        small[2 + r : 3 + r, :] += column_sum(grad)
        scaled = grad * gain[r : r + 1, :]
        mean_one = jnp.mean(scaled, axis=-1, keepdims=True)
        mean_two = jnp.mean(scaled * normed, axis=-1, keepdims=True)
        return scale * (scaled - mean_one - normed * mean_two)

    def second_back(image, row, at):
        grad = cot[at, :].astype(F32) + norm_back(middle[at, :], tokens_grad[at, :], 1)
        tokens_grad[at, :] = grad
        scaled = live_rate(0, image, row) * grad
        mixer_grad[at, :] = scaled.astype(BF)
        small[6:7, :] += column_sum(scaled)

    mixer_grad = entry_two
    over_rows(second_back)
    agenda.spend(2.2)

    for copy in core_started[:4]:
        core_copy(*copy).wait_send()
    waiting = []

    def emit_narrow(s, xb, far, value):
        part = pl.ds(s * cols, cols)
        place = len(waiting) % 2
        low, high = value[0:cols], value[cols:pair]
        give[0, xb, part, :] = jnp.where(c == 0, high, low).astype(BF)
        keep[place] = jnp.where(c == 0, low, high)
        core_start(2, xb, 6 + s * 2 + (0 if far else 1), s * cols, cols)
        waiting.append((s, xb, far, place))

    def settle(left):
        while len(waiting) - settled[0] > left:
            s, xb, far, place = waiting[settled[0]]
            settled[0] += 1
            part = pl.ds(s * cols, cols)
            core_copy(2, xb, 6 + s * 2 + (0 if far else 1), s * cols, cols).wait_recv()
            total = keep[place] + sum_core[2, xb, part, :].astype(F32)
            sum_core[2, xb, part, :] = total.astype(BF)
            if far:
                start_x(2 * width + s * cols, cols)
            else:
                own_ready(2 * width + s * cols, cols)

    settled = [0]

    def side(ref, xb):
        return jnp.concatenate([ref[xb * packs + pack] for pack in range(packs)], axis=1)

    def attend_back(xb, image):
        for i in range(packs):
            pack = xb * packs + i
            at = pl.ds(pl.multiple_of(image * slot, 16), slot)
            queries, keys, values = (heads[j, pack, at, :] for j in range(3))
            grads = mixed_grad[pack, at, :]
            length = key_length(image)
            query_grad = jnp.zeros((slot, 128), F32)
            key_grad = jnp.zeros((slot, 128), F32)
            value_grad = jnp.zeros((slot, 128), F32)
            for head in range(2):
                head_keys = pick(head, keys)
                probs = softmax(dot(queries, head_keys, 1, 1), length)
                probs_grad = dot(grads, pick(head, values), 1, 1)
                inner = jnp.sum(probs * probs_grad, axis=-1, keepdims=True)
                score_grad = (probs * (probs_grad - inner)).astype(BF)
                query_grad = query_grad + dot(score_grad, head_keys, 1, 0)
                key_grad = key_grad + dot(score_grad, pick(head, queries), 0, 0)
                value_grad = value_grad + dot(probs.astype(BF), pick(head, grads), 0, 0)
            heads[0, pack, at, :] = (query_grad * score_scale).astype(BF)
            heads[1, pack, at, :] = (key_grad * score_scale).astype(BF)
            heads[2, pack, at, :] = value_grad.astype(BF)
            agenda.spend(1.2)

    def qkv_back(xb, far):
        lanes = pl.ds(pl.multiple_of(xb * pair, 128), pair)
        for j in range(3):
            grad = side(heads.at[j], xb)
            emit_narrow(1 + j, xb, far, dot(grad, entry[...], 0, 0))
            settle(1)
            if j != 1:
                row = 4 if j == 0 else 5
                small[row : row + 1, lanes] = column_sum(grad.astype(F32))
            agenda.spend(1.2)

    value = dot(mixer_grad[...], wproj[...], 1, 1).astype(BF)
    for pack in range(2 * packs):
        mixed_grad[pack] = value[:, pack * 128 : (pack + 1) * 128]
    for xb, far in ((1 - x, True), (x, False)):
        emit_narrow(0, xb, far, dot(side(mixed, xb), mixer_grad[...], 0, 0))
    agenda.spend(3.5)
    settle(0)
    for image in range(images):
        attend_back(1 - x, image)
    qkv_back(1 - x, True)
    settle(0)
    for image in range(images):
        attend_back(x, image)
    qkv_back(x, False)
    settle(0)

    for j in range(3):
        grad = jnp.concatenate([heads[j, pack] for pack in range(2 * packs)], axis=1)
        part = dot(grad, wqkv[j], 1, 0)
        work[...] = part if j == 0 else work[...] + part
        agenda.spend(1.4)

    def first_back(image, row, at):
        tokens_grad[at, :] += norm_back(tok[at, :].astype(F32), work[at, :], 0)

    over_rows(first_back)
    tokens_copy = pltpu.make_async_copy(tokens_grad, tokens_out, local_sem.at[12])
    tokens_copy.start()
    agenda.spend(2.2)

    small_devices = (
        [core_dev, x_dev, diag_dev],
        [y_dev],
        [quad_dev(k) for k in range(1, 4)],
        [group_dev(k) for k in range(1, groups)],
    )
    small_slots = ((0, 4, m), (0, 2, y), (2, 4, quad), (6, groups, group))
    last_small = 2 if groups == 1 else 3

    def small_buffer(stage):
        return small_got if stage == 0 else small_part

    def small_copies(stage):
        first, _, place = small_slots[stage]
        sems = sum(len(devices) for devices in small_devices[:stage])
        part = small_buffer(stage).at[first + place]
        return [
            remote(part, part, small_send.at[sems + i], small_recv.at[sems + i], device)
            for i, device in enumerate(small_devices[stage])
        ]

    def small_start(stage, value):
        first, _, place = small_slots[stage]
        small_buffer(stage)[first + place] = value
        for copy in small_copies(stage):
            copy.start()
        agenda.post(agenda.now + HOP + 3.0, functools.partial(small_stage, stage))

    def small_stage(stage):
        for copy in small_copies(stage):
            copy.wait_recv()
        first, count, _ = small_slots[stage]
        buffer = small_buffer(stage)
        total = buffer[first]
        for other in range(1, count):
            total = total + buffer[first + other]
        if stage == 0:
            small[...] = total
            lanes = pl.ds(pl.multiple_of(x * pair, 128), pair)
            ours = jnp.concatenate([small[4:5, lanes], small[5:6, lanes]], axis=1)
            own = small[pl.ds(8 + m, 1), :]
            total = jnp.concatenate([total[0:4], total[6:8], own, ours], axis=0)
        if stage < last_small:
            small_start(stage + 1, total)
        else:
            small[0:8, :] = total

    small_start(0, small[...])
    for i, (block, _, _) in enumerate(order):
        part = dot(act[block], wdn[block], 1, 0)
        work[...] = part if i == 0 else work[...] + part
        agenda.spend(1.4)

    def finish(image, row, at):
        value = middle[at, :] + live_rate(1, image, row) * (work[at, :] + pbias[1:2, :])
        finished[at, :] = value.astype(BF)

    over_rows(finish)
    block_copy = pltpu.make_async_copy(finished, block_out, local_sem.at[13])
    block_copy.start()
    agenda.spend(1.2)
    agenda.until(lambda: not agenda.queue)
    small_out[0:8, :] = small[0:8, :]
    for i in range(2):
        low = i * pair
        qkv_row[i : i + 1, :] = small[7:8, low : low + pair]
    small_out[8:10, 0:cols] = jnp.where(c == 0, qkv_row[:, 0:cols], qkv_row[:, cols:pair])

    tokens_copy.wait()
    block_copy.wait()
    for sub in range(len(subs)):
        yag_copy(sub).wait_recv()
    for i in range(6):
        bias_copy(i).wait_send()
    for p in pieces:
        for route in range(10):
            ag_copy(route, p).wait_send()
    for copy in core_started[4:]:
        core_copy(*copy).wait_send()
    for sub in range(len(subs)):
        x_copy(sub).wait_send()
        y_copy(sub).wait_send()
        yag_copy(sub).wait_send()
        for step in range(1, 4):
            z_copy(sub, step).wait_send()
            zag_copy(sub, step).wait_send()
        for step in range(1, groups):
            group_copy(sub, step).wait_send()
    for stage in range(last_small + 1):
        for copy in small_copies(stage):
            copy.wait_send()


def finish_kernel(
    grads,
    tokens_part,
    block_part,
    small_part,
    block_out,
    tokens_grad,
    gain_grad,
    shift_grad,
    qkv_grad,
    qkv_bias_grad,
    proj_grad,
    proj_bias_grad,
    up_grad,
    up_bias_grad,
    down_grad,
    held,
    wide,
    tokens,
    block,
    small,
    in_sem,
    out_sem,
):
    parts = grads.shape[0]
    loads = [pltpu.make_async_copy(grads.at[i], held.at[i], in_sem.at[i]) for i in range(parts)]
    passed = [(tokens_part, tokens, tokens_grad), (block_part, block, block_out)]
    for i, (source, place, _) in enumerate(passed):
        loads.append(pltpu.make_async_copy(source, place, in_sem.at[parts + i]))
    loads.append(pltpu.make_async_copy(small_part, small, in_sem.at[parts + 2]))
    for load in loads:
        load.start()
    stores = []
    for i in range(parts):
        job, s = i // SUBS, i % SUBS
        if job < 2:
            dest = (down_grad, up_grad)[job].at[s]
        else:
            dest = proj_grad if s == 0 else qkv_grad.at[s - 1]
        loads[i].wait()
        wide[i] = held[i].astype(F32)
        stores.append(pltpu.make_async_copy(wide.at[i], dest, out_sem.at[i]))
        stores[-1].start()
    for i, (_, place, dest) in enumerate(passed):
        loads[parts + i].wait()
        stores.append(pltpu.make_async_copy(place, dest, out_sem.at[parts + i]))
        stores[-1].start()
    loads[parts + 2].wait()
    gain_grad[...] = small[0:2, :]
    shift_grad[...] = small[2:4, :]
    proj_bias_grad[...] = small[4:6, :]
    qkv_bias_grad[...] = small[8:10, 0 : qkv_bias_grad.shape[1]]
    up_bias_grad[...] = small[6:7, :].reshape(up_bias_grad.shape)
    for store in stores:
        store.wait()


def local(
    tokens,
    norm_gain,
    norm_shift,
    qkv_weight,
    qkv_bias,
    proj_weight,
    proj_bias,
    up_weight,
    up_bias,
    down_weight,
    patch_grids,
    keep_masks,
    out_cotangent,
):
    rows, width = tokens.shape
    mp = lax.axis_size("mp")
    nz = lax.axis_size("dp") // 2
    images = patch_grids.shape[0] // mp
    slot = rows // images
    cols = qkv_weight.shape[2]
    pair = 2 * cols
    packs = pair // 128
    subs = len(sub_list(width, cols))
    groups = nz // 4
    cross = max(1, subs * (groups - 1))
    qkv_rows = jnp.transpose(qkv_weight, (0, 2, 1))
    vmem = pl.BlockSpec(memory_space=pltpu.VMEM)
    smem = pl.BlockSpec(memory_space=pltpu.SMEM)
    hbm = pl.BlockSpec(memory_space=pl.ANY)
    dma = pltpu.SemaphoreType.DMA
    scratch = [
        pltpu.VMEM((3, width, width), BF),
        pltpu.VMEM((width, width), BF),
        pltpu.VMEM((4, width, width), BF),
        pltpu.VMEM((4, width, width), BF),
        pltpu.VMEM((rows, width), BF),
        pltpu.VMEM((rows, width), BF),
        pltpu.VMEM((4, 1, width), F32),
        pltpu.VMEM((4, 2, cols), F32),
        pltpu.VMEM((1, width), F32),
        pltpu.VMEM((2, pair), F32),
        pltpu.VMEM((2, cols, width), F32),
        pltpu.VMEM((rows, width), BF),
        pltpu.VMEM((rows, width), BF),
        pltpu.VMEM((rows, width), BF),
        pltpu.VMEM((3, 2 * packs, rows, 128), BF),
        pltpu.VMEM((2 * packs, rows, 128), BF),
        pltpu.VMEM((2 * packs, rows, 128), BF),
        pltpu.VMEM((4, rows, width), BF),
        pltpu.VMEM((4, rows, width), BF),
        pltpu.VMEM((rows, width), F32),
        pltpu.VMEM((rows, width), F32),
        pltpu.VMEM((rows, width), F32),
        pltpu.VMEM((rows, width), BF),
        pltpu.VMEM((2, 2, width, width), BF),
        pltpu.VMEM((JOBS, 2, width, width), BF),
        pltpu.VMEM((JOBS * width, width), BF),
        pltpu.VMEM((JOBS * width // 2, width), BF),
        pltpu.VMEM((4, JOBS * width // 4, width // 2), BF),
        pltpu.VMEM((groups, JOBS * width // 4 if groups > 1 else 16, width // 2), BF),
        pltpu.VMEM((16, width), F32),
        pltpu.VMEM((4, 16, width), F32),
        pltpu.VMEM((6 + groups, 8, width), F32),
        dma((14,)),
        dma((10, 7)),
        dma((10, 7)),
        dma((6,)),
        dma((6,)),
        dma((14,)),
        dma((14,)),
        dma((subs,)),
        dma((subs,)),
        dma((subs,)),
        dma((subs,)),
        dma((3 * subs,)),
        dma((3 * subs,)),
        dma((cross,)),
        dma((cross,)),
        dma((3 * subs,)),
        dma((3 * subs,)),
        dma((subs,)),
        dma((subs,)),
        dma((subs,)),
        dma((6 + groups,)),
        dma((6 + groups,)),
    ]
    grads, tokens_grad, block_out, small = pl.pallas_call(
        functools.partial(layer_kernel, (nz, images, slot, width, cols)),
        out_shape=(
            jax.ShapeDtypeStruct((JOBS * width, width), BF),
            jax.ShapeDtypeStruct((rows, width), F32),
            jax.ShapeDtypeStruct((rows, width), BF),
            jax.ShapeDtypeStruct((16, width), F32),
        ),
        in_specs=[hbm] * 2 + [vmem] * 3 + [smem] * 2 + [vmem] * 2 + [hbm] * 4,
        out_specs=(hbm, hbm, hbm, vmem),
        scratch_shapes=scratch,
        compiler_params=pltpu.CompilerParams(
            collective_id=0, has_side_effects=True, vmem_limit_bytes=64 * 2**20 - 2**17
        ),
    )(
        tokens,
        out_cotangent,
        norm_gain,
        norm_shift,
        proj_bias,
        patch_grids.T,
        keep_masks.T,
        up_bias,
        qkv_bias,
        qkv_rows,
        proj_weight,
        up_weight,
        down_weight,
    )
    out = pl.pallas_call(
        finish_kernel,
        out_shape=(
            jax.ShapeDtypeStruct((rows, width), BF),
            jax.ShapeDtypeStruct((rows, width), F32),
            jax.ShapeDtypeStruct((2, width), F32),
            jax.ShapeDtypeStruct((2, width), F32),
            jax.ShapeDtypeStruct((3, cols, width), F32),
            jax.ShapeDtypeStruct((2, cols), F32),
            jax.ShapeDtypeStruct((cols, width), F32),
            jax.ShapeDtypeStruct((2, width), F32),
            jax.ShapeDtypeStruct((SUBS, cols, width), F32),
            jax.ShapeDtypeStruct((width,), F32),
            jax.ShapeDtypeStruct((SUBS, cols, width), F32),
        ),
        in_specs=[hbm] * 4,
        out_specs=(hbm, hbm, vmem, vmem, hbm, vmem, hbm, vmem, hbm, vmem, hbm),
        scratch_shapes=[
            pltpu.VMEM((JOBS * SUBS, cols, width), BF),
            pltpu.VMEM((JOBS * SUBS, cols, width), F32),
            pltpu.VMEM((rows, width), F32),
            pltpu.VMEM((rows, width), BF),
            pltpu.VMEM((16, width), F32),
            dma((JOBS * SUBS + 3,)),
            dma((JOBS * SUBS + 2,)),
        ],
        compiler_params=pltpu.CompilerParams(vmem_limit_bytes=60 * 2**20),
    )(grads.reshape(JOBS * SUBS, cols, width), tokens_grad, block_out, small)
    out = list(out)
    out[4] = jnp.transpose(out[4], (0, 2, 1))
    out[8] = out[8].reshape(up_weight.shape)
    out[10] = out[10].reshape(down_weight.shape)
    return tuple(out)


def solution(mesh):
    return jax.shard_map(
        local,
        mesh=mesh,
        in_specs=(
            P(("dp", "mp"), None),
            P(),
            P(),
            P(None, None, "mp"),
            P(None, "mp"),
            P("mp", None),
            P(),
            P(None, "mp"),
            P("mp"),
            P("mp", None),
            P("dp", None),
            P("dp", None),
            P(("dp", "mp"), None),
        ),
        out_specs=(
            P(("dp", "mp"), None),
            P(("dp", "mp"), None),
            P(),
            P(),
            P(None, None, "mp"),
            P(None, "mp"),
            P("mp", None),
            P(),
            P(None, "mp"),
            P("mp"),
            P("mp", None),
        ),
        check_vma=False,
    )
```

```python
import functools
import heapq

import jax
import jax.numpy as jnp
from jax import lax
from jax.experimental import pallas as pl
from jax.experimental.pallas import tpu as pltpu
from jax.sharding import PartitionSpec as P

HEAD_DIM = 64
EPSILON = 1e-06
KEEP_RATE = 0.9
MESH = pl.DeviceIdType.MESH
BF = jnp.bfloat16
F32 = jnp.float32
TILE = 96
JOBS = 3
SUBS = 4
LINK_ROW = 0.0325
HOP = 2.0
HANDLE = 0.3
LATE = 4
LATE_Z = 0


def dot(left, right, left_dim, right_dim):
    return lax.dot_general(
        left, right, (((left_dim,), (right_dim,)), ((), ())), preferred_element_type=F32
    )


def normalise(rows):
    centred = rows - jnp.mean(rows, axis=-1, keepdims=True)
    spread = jnp.mean(centred * centred, axis=-1, keepdims=True)
    scale = lax.rsqrt(spread + EPSILON)
    return centred * scale, scale


def sub_list(width, cols):
    parts = [(k * cols, cols) for k in range(JOBS * SUBS)]
    third = cols // 3
    first = [(k * third, third) for k in range(3)]
    last = [(parts[-1][0] + k * third, third) for k in range(3)]
    return first + parts[1:-1] + last


class Agenda:
    def __init__(self):
        self.now = 0.0
        self.free = {}
        self.queue = []
        self.number = 0

    def send(self, link, rows):
        begin = max(self.now, self.free.get(link, 0.0))
        self.free[link] = begin + rows * LINK_ROW
        return self.free[link] + HOP

    def post(self, ready, action):
        self.number += 1
        heapq.heappush(self.queue, (ready, self.number, action))

    def handle(self):
        ready, _, action = heapq.heappop(self.queue)
        self.now = max(self.now, ready) + HANDLE
        action()

    def spend(self, time):
        self.now += time
        while self.queue and self.queue[0][0] <= self.now:
            self.handle()

    def until(self, reached):
        while not reached():
            self.handle()


def column_sum(rows):
    return jnp.sum(rows, axis=0, keepdims=True)


def layer_kernel(
    sizes,
    tok_in,
    cot_in,
    gain,
    shift,
    pbias,
    grids,
    masks,
    up_bias,
    qkv_bias,
    wqkv_in,
    wproj_in,
    wup_in,
    wdn_in,
    grads_out,
    tokens_out,
    block_out,
    small_out,
    wqkv,
    wproj,
    wup,
    wdn,
    tok,
    cot,
    up_all,
    qkv_all,
    up_own,
    qkv_row,
    keep,
    entry,
    entry_two,
    ret_grad,
    heads,
    mixed,
    mixed_grad,
    act,
    slope,
    work,
    middle,
    tokens_grad,
    finished,
    give,
    sum_core,
    got_x,
    got_y,
    got_z,
    got_group,
    small,
    small_got,
    small_part,
    local_sem,
    ag_send,
    ag_recv,
    bias_send,
    bias_recv,
    core_send,
    core_recv,
    x_send,
    x_recv,
    y_send,
    y_recv,
    z_send,
    z_recv,
    group_send,
    group_recv,
    zag_send,
    zag_recv,
    yag_send,
    yag_recv,
    own_sem,
    small_send,
    small_recv,
):
    nz, images, slot, width, cols = sizes
    rows = images * slot
    pair = 2 * cols
    half = cols // 2
    packs = pair // 128
    groups = nz // 4
    subs = sub_list(width, cols)

    d = lax.axis_index("dp")
    m = lax.axis_index("mp")
    y = lax.rem(d, 2)
    z = d // 2
    x = m // 2
    c = lax.rem(m, 2)
    core_dev = (d, x * 2 + 1 - c)
    x_dev = (d, (1 - x) * 2 + c)
    diag_dev = (d, (1 - x) * 2 + 1 - c)
    y_dev = (z * 2 + 1 - y, m)
    group, quad = z // 4, lax.rem(z, 4)

    def z_dev(other):
        return (other * 2 + y, m)

    def quad_dev(step):
        return z_dev(group * 4 + lax.rem(quad + step, 4))

    def group_dev(step):
        return z_dev(lax.rem(group + step, groups) * 4 + quad)

    def remote(src, dst, send, recv, device):
        return pltpu.make_async_remote_copy(
            src_ref=src,
            dst_ref=dst,
            send_sem=send,
            recv_sem=recv,
            device_id=device,
            device_id_type=MESH,
        )

    tok_copy = pltpu.make_async_copy(tok_in, tok, local_sem.at[8])
    cot_copy = pltpu.make_async_copy(cot_in, cot, local_sem.at[9])
    tok_copy.start()
    cot_copy.start()
    barrier = pltpu.get_barrier_semaphore()
    greeted = [core_dev, x_dev, diag_dev, y_dev]
    greeted += [quad_dev(k) for k in range(1, 4)]
    greeted += [group_dev(k) for k in range(1, groups)]
    for device in greeted:
        pl.semaphore_signal(barrier, inc=1, device_id=device, device_id_type=MESH)
    pl.semaphore_wait(barrier, len(greeted))

    own_block = m
    peer_block = x * 2 + 1 - c
    far_block = (1 - x) * 2 + c
    far_peer = (1 - x) * 2 + 1 - c

    pieces = ("q", "k", "v", "p", "u0", "u1", "d")
    near_z = z + 1 - 2 * lax.rem(z, 2)
    side_z = lax.rem(z, 2)
    quarters = (y * 2 + side_z, (1 - y) * 2 + side_z, y * 2 + 1 - side_z, 3 - y * 2 - side_z)
    wide = width // 2

    def rows_of(piece, part):
        size = {"u0": width // 2, "u1": width // 2, "d": width}.get(piece, cols)
        if part is None:
            return 0, size
        return quarters[part] * (size // 4), size // 4

    def view(piece, block, part, lanes=None):
        start, size = rows_of(piece, part)
        lanes = pl.ds(0, width) if lanes is None else pl.ds(lanes * wide, wide)
        if piece in "qkvp":
            at = pl.ds(pl.multiple_of(block * cols + start, 16), size)
            if piece == "p":
                return wproj.at[at, lanes]
            return wqkv.at["qkv".index(piece), at, lanes]
        first = width // 2 if piece == "u1" else 0
        at = pl.ds(pl.multiple_of(first + start, 16), size)
        return (wdn if piece == "d" else wup).at[block, at, lanes]

    def view_in(piece, part):
        start, size = rows_of(piece, part)
        first = width // 2 if piece == "u1" else 0
        at = pl.ds(first + start if part is None else pl.multiple_of(first + start, 16), size)
        if piece in "qkv":
            return wqkv_in.at["qkv".index(piece), at, :]
        return {"p": wproj_in, "d": wdn_in}.get(piece, wup_in).at[at, :]

    def ag_local(p):
        i = pieces.index(p)
        return pltpu.make_async_copy(view_in(p, None), view(p, own_block, None), local_sem.at[i])

    def ag_copy(route, p):
        i = pieces.index(p)
        send, recv = ag_send.at[route, i], ag_recv.at[route, i]
        if route == 0:
            return remote(view_in(p, None), view(p, own_block, None), send, recv, core_dev)
        if route == 1:
            return remote(view_in(p, 0), view(p, own_block, 0), send, recv, x_dev)
        if route == 2:
            part, lanes, device = 0, None, y_dev
        elif route == 3:
            part, lanes, device = 0, None, z_dev(near_z)
        elif route == 4:
            part, lanes, device = 2, 0, y_dev
        elif route == 5:
            part, lanes, device = 1, 1, z_dev(near_z)
        else:
            part, lanes, device = route - 6, None, core_dev
        source = view(p, far_block, part, lanes)
        return remote(source, source, send, recv, device)

    def quarter_rows(p):
        return rows_of(p, None)[1] // 4

    def admit(*names):
        for p in names:
            agenda.post(max(agenda.now, x_ready[p]), functools.partial(from_x, p))

    def from_x(p):
        ag_copy(1, p).wait_recv()
        for route in (2, 3, 6):
            ag_copy(route, p).start()
        ready = max(agenda.send("y", quarter_rows(p)), agenda.send("z", quarter_rows(p)))
        agenda.post(ready, functools.partial(from_yz, p))

    def from_yz(p):
        ag_copy(2, p).wait_recv()
        ag_copy(5, p).start()
        ag_copy(7, p).start()
        ag_copy(3, p).wait_recv()
        ag_copy(4, p).start()
        ag_copy(8, p).start()
        rows_ = quarter_rows(p) // 2
        ready = max(agenda.send("y", rows_), agenda.send("z", rows_))
        agenda.post(ready, functools.partial(from_both, p))
        if p == "v":
            admit("p", "u0", "u1")
        elif p == "u1":
            admit("d")

    def from_both(p):
        ag_copy(4, p).wait_recv()
        ag_copy(5, p).wait_recv()
        ag_copy(9, p).start()
        gathered.add(p)

    def bias_copy(i):
        source, dest = (up_own, up_all) if i % 2 == 0 else (qkv_bias, qkv_all)
        device = (x_dev, diag_dev, core_dev)[i // 2]
        return remote(source, dest.at[m], bias_send.at[i], bias_recv.at[i], device)

    def bias_own(i):
        source, dest = (up_own, up_all) if i % 2 == 0 else (qkv_bias, qkv_all)
        return pltpu.make_async_copy(source, dest.at[m], local_sem.at[10 + i])

    up_own[...] = up_bias[...].reshape(1, width)
    for i in range(4):
        bias_copy(i).start()
    agenda = Agenda()
    gathered = set()
    x_ready = {}
    for p in pieces:
        ag_copy(1, p).start()
        x_ready[p] = agenda.send("x", quarter_rows(p))
    admit("q", "k", "v")
    for p in pieces[:3]:
        ag_copy(0, p).start()
        ag_local(p).start()
    for i in range(2):
        bias_copy(4 + i).start()
        bias_own(i).start()

    def near_ready(*names):
        for p in names:
            ag_local(p).wait()
            ag_copy(0, p).wait_recv()

    def far_ready(*names):
        for p in names:
            agenda.until(lambda: p in gathered)
            for route in (6, 7, 8, 9):
                ag_copy(route, p).wait_recv()

    core_started = []

    def core_copy(job, xb, slot_, first, size):
        at = pl.ds(first, size)
        return remote(
            give.at[job % 2, xb, at, :],
            sum_core.at[job, xb, at, :],
            core_send.at[slot_],
            core_recv.at[slot_],
            core_dev,
        )

    def core_start(*copy):
        core_started.append(copy)
        core_copy(*copy).start()

    def x_copy(sub):
        first, size = subs[sub]
        source = sum_core.at[first // width, 1 - x, pl.ds(first % width, size), :]
        return remote(
            source, got_x.at[pl.ds(first, size), :], x_send.at[sub], x_recv.at[sub], x_dev
        )

    def y_part(sub, which):
        first, size = subs[sub]
        start = pl.multiple_of(first % width + which * (size // 2), 16)
        return first // width, pl.ds(start, size // 2)

    def y_got(sub):
        first, size = subs[sub]
        return pl.ds(first // 2, size // 2)

    def y_copy(sub):
        job, at = y_part(sub, 1 - y)
        return remote(
            sum_core.at[job, x, at, :],
            got_y.at[y_got(sub), :],
            y_send.at[sub],
            y_recv.at[sub],
            y_dev,
        )

    def z_part(sub, owner):
        tall = subs[sub][1] // 4
        row = pl.multiple_of((owner // 2) * tall, 16)
        lanes = pl.ds(pl.multiple_of(lax.rem(owner, 2) * wide, 128), wide)
        return row, lanes, tall

    def z_got(sub, owner):
        row, lanes, tall = z_part(sub, owner)
        return got_y.at[pl.ds(pl.multiple_of(subs[sub][0] // 2 + row, 16), tall), lanes]

    def z_slot(sub, place):
        first, size = subs[sub]
        return got_z.at[place, pl.ds(first // 4, size // 4), :]

    def z_copy(sub, step):
        sem = sub * 3 + step - 1
        return remote(
            z_got(sub, lax.rem(quad + step, 4)),
            z_slot(sub, step - 1),
            z_send.at[sem],
            z_recv.at[sem],
            quad_dev(step),
        )

    def group_slot(sub, place):
        first, size = subs[sub]
        return got_group.at[place, pl.ds(first // 4, size // 4), :]

    def group_copy(sub, step):
        sem = sub * (groups - 1) + step - 1
        part = group_slot(sub, group)
        return remote(part, part, group_send.at[sem], group_recv.at[sem], group_dev(step))

    def final_part(sub):
        first, size = subs[sub]
        row, lanes, tall = z_part(sub, quad)
        row = pl.multiple_of(first + row + y * (size // 2), 16)
        return grads_out.at[pl.ds(row, tall), lanes]

    def zag_copy(sub, step):
        sem = sub * 3 + step - 1
        return remote(
            z_slot(sub, 3), final_part(sub), zag_send.at[sem], zag_recv.at[sem], quad_dev(step)
        )

    def own_copy(sub):
        return pltpu.make_async_copy(z_slot(sub, 3), final_part(sub), own_sem.at[sub])

    def yag_copy(sub):
        first, size = subs[sub]
        start = pl.multiple_of(first + y * (size // 2), 16)
        part = grads_out.at[pl.ds(start, size // 2), :]
        return remote(part, part, yag_send.at[sub], yag_recv.at[sub], y_dev)

    own_rows = []
    early = []
    summed_y = []
    held = []
    summed_z = []
    held_z = []

    def start_x(first, size):
        for sub, (row, length) in enumerate(subs):
            if first <= row < first + size:
                x_copy(sub).start()
                agenda.post(agenda.send("x", length), functools.partial(x_stage, sub))

    def own_ready(first, size):
        own_rows.append((first, first + size))
        for sub in list(early):
            if has_own(sub):
                early.remove(sub)
                agenda.post(agenda.now, functools.partial(x_stage, sub))

    def has_own(sub):
        first, size = subs[sub]
        return any(low <= first and first + size <= high for low, high in own_rows)

    def x_stage(sub):
        if not has_own(sub):
            early.append(sub)
            return
        x_copy(sub).wait_recv()
        first, size = subs[sub]
        job, at = first // width, pl.ds(first % width, size)
        sum_core[job, x, at, :] = sum_core[job, x, at, :] + got_x[pl.ds(first, size), :]
        y_copy(sub).start()
        agenda.post(agenda.send("y", size // 2), functools.partial(y_stage, sub))
        summed_y.append(sub)
        if len(summed_y) == len(subs):
            hand_out()

    def y_stage(sub):
        y_copy(sub).wait_recv()
        job, at = y_part(sub, y)
        got = y_got(sub)
        got_y[got, :] = sum_core[job, x, at, :] + got_y[got, :]
        for step in range(1, 4):
            z_copy(sub, step).start()
        agenda.post(agenda.send("z", subs[sub][1] // 2), functools.partial(z_stage, sub))
        summed_z.append(sub)
        if len(summed_z) == len(subs):
            share()

    def z_stage(sub):
        total = z_got(sub, quad)[...].astype(F32)
        for step in range(1, 4):
            z_copy(sub, step).wait_recv()
            total = total + z_slot(sub, step - 1)[...].astype(F32)
        if groups == 1:
            publish(sub, total)
            return
        group_slot(sub, group)[...] = total.astype(BF)
        for step in range(1, groups):
            group_copy(sub, step).start()
        agenda.post(agenda.send("z", subs[sub][1] // 2), functools.partial(group_stage, sub))

    def group_stage(sub):
        for step in range(1, groups):
            group_copy(sub, step).wait_recv()
        total = group_slot(sub, 0)[...].astype(F32)
        for other in range(1, groups):
            total = total + group_slot(sub, other)[...].astype(F32)
        publish(sub, total)

    def publish(sub, total):
        z_slot(sub, 3)[...] = total.astype(BF)
        own_copy(sub).start()
        held_z.append(sub)
        share()

    def share():
        if len(subs) - LATE_Z <= len(summed_z) < len(subs):
            return
        for sub in held_z:
            for step in range(1, 4):
                zag_copy(sub, step).start()
            agenda.post(agenda.send("z", subs[sub][1] // 2), functools.partial(zag_stage, sub))
        held_z.clear()

    def zag_stage(sub):
        own_copy(sub).wait()
        for step in range(1, 4):
            zag_copy(sub, step).wait_recv()
        held.append(sub)
        hand_out()

    def hand_out():
        if len(subs) - LATE <= len(summed_y) < len(subs):
            return
        for sub in held:
            yag_copy(sub).start()
            agenda.send("y", subs[sub][1] // 2)
        held.clear()

    def live_rate(which, image, row):
        index = m * images + image
        length = grids[0, index] * grids[1, index] + 2
        kept = masks[which, index].astype(F32) / KEEP_RATE
        position = lax.broadcasted_iota(jnp.int32, (TILE, 1), 0) + row
        return jnp.where(position < length, kept, 0.0)

    def over_rows(body, time=0.0):
        for image in range(images):

            def step(i, carry):
                row = i * TILE
                body(image, row, pl.ds(pl.multiple_of(image * slot + row, 16), TILE))
                return carry

            lax.fori_loop(0, slot // TILE, step, 0, unroll=True)
            agenda.spend(time / images)

    small[...] = jnp.zeros_like(small)

    def first_norm(image, row, at):
        normed, _ = normalise(tok[at, :].astype(F32))
        entry[at, :] = (normed * gain[0:1, :] + shift[0:1, :]).astype(BF)

    def return_rows(image, row, at):
        grad = live_rate(1, image, row) * cot[at, :].astype(F32)
        ret_grad[at, :] = grad.astype(BF)
        small[7:8, :] += column_sum(grad)

    tok_copy.wait()
    over_rows(first_norm)

    lane = lax.broadcasted_iota(jnp.int32, (slot, 128), 1)
    low_lanes = lane < HEAD_DIM
    position = lax.broadcasted_iota(jnp.int32, (slot, slot), 1)
    padded = (slot + 127) // 128 * 128
    padded_position = lax.broadcasted_iota(jnp.int32, (slot, padded), 1)
    score_scale = HEAD_DIM ** (-0.5)

    def pick(head, values):
        mask = low_lanes if head == 0 else jnp.logical_not(low_lanes)
        return jnp.where(mask, values, jnp.zeros_like(values))

    def stacked(values):
        blank = jnp.zeros((padded - slot, 128), BF)
        return jnp.concatenate([pick(0, values), blank, pick(1, values), blank], axis=0)

    def key_length(image):
        index = m * images + image
        return grids[0, index] * grids[1, index] + 2

    def softmax(scores, length):
        places = position if scores.shape[1] == slot else padded_position
        scores = jnp.where(places < length, scores * score_scale, -1000000000.0)
        raised = jnp.exp(scores - jnp.max(scores, axis=-1, keepdims=True))
        return raised * (1.0 / jnp.sum(raised, axis=-1, keepdims=True))

    def project(xb, ready):
        at = pl.ds(pl.multiple_of(xb * pair, 16), pair)
        qkv_row[:, 0:cols] = qkv_all[xb * 2]
        qkv_row[:, cols:pair] = qkv_all[xb * 2 + 1]
        for j in range(3):
            ready("qkv"[j])
            value = dot(entry[...], wqkv[j, at, :], 1, 1)
            if j != 1:
                row = j // 2
                value = value + qkv_row[row : row + 1, :]
            value = value.astype(BF)
            for pack in range(packs):
                heads[j, xb * packs + pack] = value[:, pack * 128 : (pack + 1) * 128]
            agenda.spend(0.8)

    def attend(xb, image):
        for i in range(packs):
            pack = xb * packs + i
            at = pl.ds(pl.multiple_of(image * slot, 16), slot)
            queries, keys, values = (heads[j, pack, at, :] for j in range(3))
            length = key_length(image)
            scores = dot(queries, stacked(keys), 1, 1)
            probs = [softmax(scores[:, k * padded : (k + 1) * padded], length) for k in range(2)]
            probs = jnp.concatenate([part.astype(BF) for part in probs], axis=1)
            total = dot(probs, stacked(values), 1, 0)
            mixed[pack, at, :] = total.astype(BF)
            agenda.spend(0.7)

    agenda.spend(1.5)
    for p in pieces[3:]:
        ag_copy(0, p).start()
        ag_local(p).start()
    bias_own(1).wait()
    bias_copy(5).wait_recv()
    agenda.spend(1.0)
    project(x, near_ready)
    for image in range(images):
        attend(x, image)
    cot_copy.wait()
    over_rows(return_rows)
    agenda.spend(1.0)
    near_ready("d")
    grad_peer = give.at[1, x, pl.ds(0, rows), :]
    grad_peer[...] = dot(ret_grad[...], wdn[peer_block], 1, 1).astype(BF)
    agenda.spend(1.2)
    value = dot(ret_grad[...], wdn[own_block], 1, 1).astype(BF)
    for pack in range(2 * packs):
        mixed_grad[pack] = value[:, pack * 128 : (pack + 1) * 128]
    agenda.spend(1.2)
    bias_own(0).wait()
    for i in range(5):
        bias_copy(i).wait_recv()
    project(1 - x, far_ready)
    for image in range(images):
        attend(1 - x, image)

    near_ready("p")
    far_ready("p")
    all_mixed = jnp.concatenate([mixed[pack] for pack in range(2 * packs)], axis=1)
    work[...] = dot(all_mixed, wproj[...], 1, 0)

    def second_norm(image, row, at):
        value = tok[at, :].astype(F32) + live_rate(0, image, row) * (work[at, :] + pbias[0:1, :])
        middle[at, :] = value
        normed, _ = normalise(value)
        entry_two[at, :] = (normed * gain[1:2, :] + shift[1:2, :]).astype(BF)

    over_rows(second_norm)
    agenda.spend(2.7)

    def emit(job, xb, slot_, mine, first, size, value):
        kept, far = mine
        at = pl.ds(first, size)
        if not kept:
            give[job % 2, xb, at, :] = value.astype(BF)
            core_start(job, xb, slot_, first, size)
            return
        core_copy(job, xb, slot_, first, size).wait_recv()
        total = value + sum_core[job, xb, at, :].astype(F32)
        sum_core[job, xb, at, :] = total.astype(BF)
        if far:
            start_x(job * width + first, size)
        else:
            own_ready(job * width + first, size)

    def feed_first(block, xb, mine, part):
        first, size = part * wide, wide
        lanes = slice(first, first + size)
        hidden = dot(entry_two[...], wup[block, :, lanes], 1, 0) + up_all[block, :, lanes]
        share = 0.5 * (1.0 + lax.erf(hidden * 0.7071067811865476))
        density = jnp.exp(-0.5 * hidden * hidden) * 0.3989422804014327
        active = (hidden * share).astype(BF)
        act[block, :, lanes] = active
        slope[block, :, lanes] = (share + hidden * density).astype(BF)
        slot_ = (0 if mine[1] else 2) + part
        emit(0, xb, slot_, mine, first, size, dot(active, ret_grad[...], 0, 0))
        agenda.spend(1.9)

    def feed_back(block, xb, mine, first):
        if mine == (False, False):
            grad = grad_peer[...].astype(F32)
        elif mine == (True, False):
            grad = jnp.concatenate([mixed_grad[pack] for pack in range(2 * packs)], axis=1)
            grad = grad.astype(F32)
        else:
            grad = dot(ret_grad[...], wdn[block], 1, 1)
            agenda.spend(1.2)
        grad = (grad * slope[block].astype(F32)).astype(BF)
        slope[block] = grad
        small[pl.ds(8 + block, 1), :] = column_sum(grad.astype(F32))
        agenda.spend(0.4)
        slot_ = 4 if mine[1] else 5
        emit(1, xb, slot_, mine, 0, width, dot(entry_two[...], slope[block], 0, 0))
        agenda.spend(1.4)
        value = dot(slope[block], wup[block], 1, 1)
        if first:
            tokens_grad[...] = value
        else:
            tokens_grad[...] += value
        agenda.spend(1.2)

    order = (
        (far_peer, 1 - x, (False, True)),
        (far_block, 1 - x, (True, True)),
        (peer_block, x, (False, False)),
        (own_block, x, (True, False)),
    )
    near_ready("u0", "u1")
    far_ready("u0", "u1")
    for part in range(2):
        for item in order:
            feed_first(*item, part)
    far_ready("d")
    for i, item in enumerate(order):
        feed_back(*item, i == 0)

    def norm_back(values, grad, r):
        normed, scale = normalise(values)
        small[r : r + 1, :] += column_sum(grad * normed)
        small[2 + r : 3 + r, :] += column_sum(grad)
        scaled = grad * gain[r : r + 1, :]
        mean_one = jnp.mean(scaled, axis=-1, keepdims=True)
        mean_two = jnp.mean(scaled * normed, axis=-1, keepdims=True)
        return scale * (scaled - mean_one - normed * mean_two)

    def second_back(image, row, at):
        grad = cot[at, :].astype(F32) + norm_back(middle[at, :], tokens_grad[at, :], 1)
        tokens_grad[at, :] = grad
        scaled = live_rate(0, image, row) * grad
        mixer_grad[at, :] = scaled.astype(BF)
        small[6:7, :] += column_sum(scaled)

    mixer_grad = entry_two
    over_rows(second_back, 2.2)

    for copy in core_started[:4]:
        core_copy(*copy).wait_send()
    waiting = []

    def emit_narrow(s, xb, far, value):
        part = pl.ds(s * cols, cols)
        place = len(waiting) % 2
        low, high = value[0:cols], value[cols:pair]
        give[0, xb, part, :] = jnp.where(c == 0, high, low).astype(BF)
        keep[place] = jnp.where(c == 0, low, high)
        core_start(2, xb, 6 + s * 2 + (0 if far else 1), s * cols, cols)
        waiting.append((s, xb, far, place))

    def settle(left):
        while len(waiting) - settled[0] > left:
            s, xb, far, place = waiting[settled[0]]
            settled[0] += 1
            part = pl.ds(s * cols, cols)
            core_copy(2, xb, 6 + s * 2 + (0 if far else 1), s * cols, cols).wait_recv()
            total = keep[place] + sum_core[2, xb, part, :].astype(F32)
            sum_core[2, xb, part, :] = total.astype(BF)
            if far:
                start_x(2 * width + s * cols, cols)
            else:
                own_ready(2 * width + s * cols, cols)

    settled = [0]

    def side(ref, xb):
        return jnp.concatenate([ref[xb * packs + pack] for pack in range(packs)], axis=1)

    def attend_back(xb, image):
        for i in range(packs):
            pack = xb * packs + i
            at = pl.ds(pl.multiple_of(image * slot, 16), slot)
            queries, keys, values = (heads[j, pack, at, :] for j in range(3))
            grads = mixed_grad[pack, at, :]
            length = key_length(image)
            query_grad = jnp.zeros((slot, 128), F32)
            key_grad = jnp.zeros((slot, 128), F32)
            value_grad = jnp.zeros((slot, 128), F32)
            for head in range(2):
                head_keys = pick(head, keys)
                probs = softmax(dot(queries, head_keys, 1, 1), length)
                probs_grad = dot(grads, pick(head, values), 1, 1)
                inner = jnp.sum(probs * probs_grad, axis=-1, keepdims=True)
                score_grad = (probs * (probs_grad - inner)).astype(BF)
                query_grad = query_grad + dot(score_grad, head_keys, 1, 0)
                key_grad = key_grad + dot(score_grad, pick(head, queries), 0, 0)
                value_grad = value_grad + dot(probs.astype(BF), pick(head, grads), 0, 0)
            heads[0, pack, at, :] = (query_grad * score_scale).astype(BF)
            heads[1, pack, at, :] = (key_grad * score_scale).astype(BF)
            heads[2, pack, at, :] = value_grad.astype(BF)
            agenda.spend(1.2)

    def qkv_back(xb, far):
        lanes = pl.ds(pl.multiple_of(xb * pair, 128), pair)
        for j in range(3):
            grad = side(heads.at[j], xb)
            emit_narrow(1 + j, xb, far, dot(grad, entry[...], 0, 0))
            settle(1)
            if j != 1:
                row = 4 if j == 0 else 5
                small[row : row + 1, lanes] = column_sum(grad.astype(F32))
            agenda.spend(1.2)

    value = dot(mixer_grad[...], wproj[...], 1, 1).astype(BF)
    for pack in range(2 * packs):
        mixed_grad[pack] = value[:, pack * 128 : (pack + 1) * 128]
    for xb, far in ((1 - x, True), (x, False)):
        emit_narrow(0, xb, far, dot(side(mixed, xb), mixer_grad[...], 0, 0))
    agenda.spend(3.5)
    settle(0)
    for image in range(images):
        attend_back(1 - x, image)
    qkv_back(1 - x, True)
    settle(0)
    for image in range(images):
        attend_back(x, image)
    qkv_back(x, False)
    settle(0)

    for j in range(3):
        grad = jnp.concatenate([heads[j, pack] for pack in range(2 * packs)], axis=1)
        part = dot(grad, wqkv[j], 1, 0)
        work[...] = part if j == 0 else work[...] + part
        agenda.spend(1.4)

    def first_back(image, row, at):
        tokens_grad[at, :] += norm_back(tok[at, :].astype(F32), work[at, :], 0)

    over_rows(first_back, 2.2)
    tokens_copy = pltpu.make_async_copy(tokens_grad, tokens_out, local_sem.at[12])
    tokens_copy.start()

    small_devices = (
        [core_dev, x_dev, diag_dev],
        [y_dev],
        [quad_dev(k) for k in range(1, 4)],
        [group_dev(k) for k in range(1, groups)],
    )
    small_slots = ((0, 4, m), (0, 2, y), (2, 4, quad), (6, groups, group))
    last_small = 2 if groups == 1 else 3

    def small_buffer(stage):
        return small_got if stage == 0 else small_part

    def small_copies(stage):
        first, _, place = small_slots[stage]
        sems = sum(len(devices) for devices in small_devices[:stage])
        part = small_buffer(stage).at[first + place]
        return [
            remote(part, part, small_send.at[sems + i], small_recv.at[sems + i], device)
            for i, device in enumerate(small_devices[stage])
        ]

    def small_start(stage, value):
        first, _, place = small_slots[stage]
        small_buffer(stage)[first + place] = value
        for copy in small_copies(stage):
            copy.start()
        agenda.post(agenda.now + HOP + 3.0, functools.partial(small_stage, stage))

    def small_stage(stage):
        for copy in small_copies(stage):
            copy.wait_recv()
        first, count, _ = small_slots[stage]
        buffer = small_buffer(stage)
        total = buffer[first]
        for other in range(1, count):
            total = total + buffer[first + other]
        if stage == 0:
            small[...] = total
            lanes = pl.ds(pl.multiple_of(x * pair, 128), pair)
            ours = jnp.concatenate([small[4:5, lanes], small[5:6, lanes]], axis=1)
            own = small[pl.ds(8 + m, 1), :]
            total = jnp.concatenate([total[0:4], total[6:8], own, ours], axis=0)
        if stage < last_small:
            small_start(stage + 1, total)
        else:
            small[0:8, :] = total

    small_start(0, small[...])
    for i, (block, _, _) in enumerate(order):
        part = dot(act[block], wdn[block], 1, 0)
        work[...] = part if i == 0 else work[...] + part
        agenda.spend(1.4)

    def finish(image, row, at):
        value = middle[at, :] + live_rate(1, image, row) * (work[at, :] + pbias[1:2, :])
        finished[at, :] = value.astype(BF)

    over_rows(finish, 1.2)
    block_copy = pltpu.make_async_copy(finished, block_out, local_sem.at[13])
    block_copy.start()
    agenda.until(lambda: not agenda.queue)
    small_out[0:8, :] = small[0:8, :]
    for i in range(2):
        low = i * pair
        qkv_row[i : i + 1, :] = small[7:8, low : low + pair]
    small_out[8:10, 0:cols] = jnp.where(c == 0, qkv_row[:, 0:cols], qkv_row[:, cols:pair])

    tokens_copy.wait()
    block_copy.wait()
    for sub in range(len(subs)):
        yag_copy(sub).wait_recv()
    for i in range(6):
        bias_copy(i).wait_send()
    for p in pieces:
        for route in range(10):
            ag_copy(route, p).wait_send()
    for copy in core_started[4:]:
        core_copy(*copy).wait_send()
    for sub in range(len(subs)):
        x_copy(sub).wait_send()
        y_copy(sub).wait_send()
        yag_copy(sub).wait_send()
        for step in range(1, 4):
            z_copy(sub, step).wait_send()
            zag_copy(sub, step).wait_send()
        for step in range(1, groups):
            group_copy(sub, step).wait_send()
    for stage in range(last_small + 1):
        for copy in small_copies(stage):
            copy.wait_send()


def finish_kernel(
    grads,
    tokens_part,
    block_part,
    small_part,
    block_out,
    tokens_grad,
    gain_grad,
    shift_grad,
    qkv_grad,
    qkv_bias_grad,
    proj_grad,
    proj_bias_grad,
    up_grad,
    up_bias_grad,
    down_grad,
    held,
    wide,
    tokens,
    block,
    small,
    in_sem,
    out_sem,
):
    parts = grads.shape[0]
    loads = [pltpu.make_async_copy(grads.at[i], held.at[i], in_sem.at[i]) for i in range(parts)]
    passed = [(tokens_part, tokens, tokens_grad), (block_part, block, block_out)]
    for i, (source, place, _) in enumerate(passed):
        loads.append(pltpu.make_async_copy(source, place, in_sem.at[parts + i]))
    loads.append(pltpu.make_async_copy(small_part, small, in_sem.at[parts + 2]))
    for load in loads:
        load.start()
    stores = []
    for i in range(parts):
        job, s = i // SUBS, i % SUBS
        if job < 2:
            dest = (down_grad, up_grad)[job].at[s]
        else:
            dest = proj_grad if s == 0 else qkv_grad.at[s - 1]
        loads[i].wait()
        wide[i] = held[i].astype(F32)
        stores.append(pltpu.make_async_copy(wide.at[i], dest, out_sem.at[i]))
        stores[-1].start()
    for i, (_, place, dest) in enumerate(passed):
        loads[parts + i].wait()
        stores.append(pltpu.make_async_copy(place, dest, out_sem.at[parts + i]))
        stores[-1].start()
    loads[parts + 2].wait()
    gain_grad[...] = small[0:2, :]
    shift_grad[...] = small[2:4, :]
    proj_bias_grad[...] = small[4:6, :]
    qkv_bias_grad[...] = small[8:10, 0 : qkv_bias_grad.shape[1]]
    up_bias_grad[...] = small[6:7, :].reshape(up_bias_grad.shape)
    for store in stores:
        store.wait()


def local(
    tokens,
    norm_gain,
    norm_shift,
    qkv_weight,
    qkv_bias,
    proj_weight,
    proj_bias,
    up_weight,
    up_bias,
    down_weight,
    patch_grids,
    keep_masks,
    out_cotangent,
):
    rows, width = tokens.shape
    mp = lax.axis_size("mp")
    nz = lax.axis_size("dp") // 2
    images = patch_grids.shape[0] // mp
    slot = rows // images
    cols = qkv_weight.shape[2]
    pair = 2 * cols
    packs = pair // 128
    subs = len(sub_list(width, cols))
    groups = nz // 4
    cross = max(1, subs * (groups - 1))
    qkv_rows = jnp.transpose(qkv_weight, (0, 2, 1))
    vmem = pl.BlockSpec(memory_space=pltpu.VMEM)
    smem = pl.BlockSpec(memory_space=pltpu.SMEM)
    hbm = pl.BlockSpec(memory_space=pl.ANY)
    dma = pltpu.SemaphoreType.DMA
    scratch = [
        pltpu.VMEM((3, width, width), BF),
        pltpu.VMEM((width, width), BF),
        pltpu.VMEM((4, width, width), BF),
        pltpu.VMEM((4, width, width), BF),
        pltpu.VMEM((rows, width), BF),
        pltpu.VMEM((rows, width), BF),
        pltpu.VMEM((4, 1, width), F32),
        pltpu.VMEM((4, 2, cols), F32),
        pltpu.VMEM((1, width), F32),
        pltpu.VMEM((2, pair), F32),
        pltpu.VMEM((2, cols, width), F32),
        pltpu.VMEM((rows, width), BF),
        pltpu.VMEM((rows, width), BF),
        pltpu.VMEM((rows, width), BF),
        pltpu.VMEM((3, 2 * packs, rows, 128), BF),
        pltpu.VMEM((2 * packs, rows, 128), BF),
        pltpu.VMEM((2 * packs, rows, 128), BF),
        pltpu.VMEM((4, rows, width), BF),
        pltpu.VMEM((4, rows, width), BF),
        pltpu.VMEM((rows, width), F32),
        pltpu.VMEM((rows, width), F32),
        pltpu.VMEM((rows, width), F32),
        pltpu.VMEM((rows, width), BF),
        pltpu.VMEM((2, 2, width, width), BF),
        pltpu.VMEM((JOBS, 2, width, width), BF),
        pltpu.VMEM((JOBS * width, width), BF),
        pltpu.VMEM((JOBS * width // 2, width), BF),
        pltpu.VMEM((4, JOBS * width // 4, width // 2), BF),
        pltpu.VMEM((groups, JOBS * width // 4 if groups > 1 else 16, width // 2), BF),
        pltpu.VMEM((16, width), F32),
        pltpu.VMEM((4, 16, width), F32),
        pltpu.VMEM((6 + groups, 8, width), F32),
        dma((14,)),
        dma((10, 7)),
        dma((10, 7)),
        dma((6,)),
        dma((6,)),
        dma((14,)),
        dma((14,)),
        dma((subs,)),
        dma((subs,)),
        dma((subs,)),
        dma((subs,)),
        dma((3 * subs,)),
        dma((3 * subs,)),
        dma((cross,)),
        dma((cross,)),
        dma((3 * subs,)),
        dma((3 * subs,)),
        dma((subs,)),
        dma((subs,)),
        dma((subs,)),
        dma((6 + groups,)),
        dma((6 + groups,)),
    ]
    grads, tokens_grad, block_out, small = pl.pallas_call(
        functools.partial(layer_kernel, (nz, images, slot, width, cols)),
        out_shape=(
            jax.ShapeDtypeStruct((JOBS * width, width), BF),
            jax.ShapeDtypeStruct((rows, width), F32),
            jax.ShapeDtypeStruct((rows, width), BF),
            jax.ShapeDtypeStruct((16, width), F32),
        ),
        in_specs=[hbm] * 2 + [vmem] * 3 + [smem] * 2 + [vmem] * 2 + [hbm] * 4,
        out_specs=(hbm, hbm, hbm, vmem),
        scratch_shapes=scratch,
        compiler_params=pltpu.CompilerParams(
            collective_id=0, has_side_effects=True, vmem_limit_bytes=64 * 2**20 - 2**17
        ),
    )(
        tokens,
        out_cotangent,
        norm_gain,
        norm_shift,
        proj_bias,
        patch_grids.T,
        keep_masks.T,
        up_bias,
        qkv_bias,
        qkv_rows,
        proj_weight,
        up_weight,
        down_weight,
    )
    out = pl.pallas_call(
        finish_kernel,
        out_shape=(
            jax.ShapeDtypeStruct((rows, width), BF),
            jax.ShapeDtypeStruct((rows, width), F32),
            jax.ShapeDtypeStruct((2, width), F32),
            jax.ShapeDtypeStruct((2, width), F32),
            jax.ShapeDtypeStruct((3, cols, width), F32),
            jax.ShapeDtypeStruct((2, cols), F32),
            jax.ShapeDtypeStruct((cols, width), F32),
            jax.ShapeDtypeStruct((2, width), F32),
            jax.ShapeDtypeStruct((SUBS, cols, width), F32),
            jax.ShapeDtypeStruct((width,), F32),
            jax.ShapeDtypeStruct((SUBS, cols, width), F32),
        ),
        in_specs=[hbm] * 4,
        out_specs=(hbm, hbm, vmem, vmem, hbm, vmem, hbm, vmem, hbm, vmem, hbm),
        scratch_shapes=[
            pltpu.VMEM((JOBS * SUBS, cols, width), BF),
            pltpu.VMEM((JOBS * SUBS, cols, width), F32),
            pltpu.VMEM((rows, width), F32),
            pltpu.VMEM((rows, width), BF),
            pltpu.VMEM((16, width), F32),
            dma((JOBS * SUBS + 3,)),
            dma((JOBS * SUBS + 2,)),
        ],
        compiler_params=pltpu.CompilerParams(vmem_limit_bytes=60 * 2**20),
    )(grads.reshape(JOBS * SUBS, cols, width), tokens_grad, block_out, small)
    out = list(out)
    out[4] = jnp.transpose(out[4], (0, 2, 1))
    out[8] = out[8].reshape(up_weight.shape)
    out[10] = out[10].reshape(down_weight.shape)
    return tuple(out)


def solution(mesh):
    return jax.shard_map(
        local,
        mesh=mesh,
        in_specs=(
            P(("dp", "mp"), None),
            P(),
            P(),
            P(None, None, "mp"),
            P(None, "mp"),
            P("mp", None),
            P(),
            P(None, "mp"),
            P("mp"),
            P("mp", None),
            P("dp", None),
            P("dp", None),
            P(("dp", "mp"), None),
        ),
        out_specs=(
            P(("dp", "mp"), None),
            P(("dp", "mp"), None),
            P(),
            P(),
            P(None, None, "mp"),
            P(None, "mp"),
            P("mp", None),
            P(),
            P(None, "mp"),
            P("mp"),
            P("mp", None),
        ),
        check_vma=False,
    )
```
